256 devices in a mesh: lon: 16 (over x, y_lo, core), lat: 16 (over y_hi, z).
Axes of the slice: x: 4, y: 4 (y_hi: 2, y_lo: 2; y = y_hi * 2 + y_lo), z: 8, core: 2. Of those that a mesh axis runs over, the one named last changes fastest.
Arguments:
- tokens: bfloat16 [128, 512, 512], P('lat', 'lon')
- w_qkv: bfloat16 [512, 1536], replicated
- w_proj: bfloat16 [512, 512], replicated, may hold values from -0.25 to 0.25
- w_merge: bfloat16 [2048, 1024], replicated, may hold values from -0.125 to 0.125
- skip_grad: bfloat16 [128, 512, 512], P('lat', 'lon'), may hold values from -6 to 6
- merged_grad: bfloat16 [64, 256, 1024], P('lat', 'lon'), may hold values from -6 to 6
- window_shift: int32 [2], replicated, may hold values from 1 to 7, as said below
Outputs:
- skip_out: bfloat16 [128, 512, 512], P('lat', 'lon')
- merged_out: bfloat16 [64, 256, 1024], P('lat', 'lon')
- input_grad: bfloat16 [128, 512, 512], P('lat', 'lon')
- dw_qkv: float32 [512, 1536], P('lon', 'lat')
- dw_proj: float32 [512, 512], P('lon', 'lat')
- dw_merge: float32 [2048, 1024], P('lon', 'lat')
The draws below stay inside these ranges and needn't reach their ends.
Inputs may be any that keep to these rules, and one draw needn't show every extreme that they name: window_shift[0] is the latitude offset and window_shift[1] the longitude offset of the windows; one of the two equals 7 and the two differ.
All inputs are finite; a program needn't handle non-finite values.
Results may differ from the reference program's by a relative error of at most 0.029.
The reference program's roundings to bfloat16 on the way count: a program that leaves them out, or rounds other values in their place, can miss the bound.
Values may be sent and summed in bfloat16 or wider, within the bound.
A program may use at most 128 MiB of HBM per device.

```python
import jax
import jax.numpy as jnp
from jax import lax

D = 512
D2 = 1024
HEADS = 16
WIN = 8
LAT = 128
LON = 512


def draw_tokens(key, part):
    key = jax.random.fold_in(key, 17)
    normal_cells = jax.random.normal(key, (LAT, LON, D), jnp.float32)
    return jnp.clip(normal_cells, -6.0, 6.0).astype(jnp.bfloat16)


def draw_w_qkv(key, part):
    key = jax.random.fold_in(key, 29)
    normal_part = jax.random.normal(key, (D, 3 * D), jnp.float32) * D ** (-0.5)
    return jnp.clip(normal_part, -6.0 * D ** (-0.5), 6.0 * D ** (-0.5)).astype(jnp.bfloat16)


def draw_window_shift(key, part):
    key = jax.random.fold_in(key, 41)
    widest = jax.random.randint(key, (), 0, 2)
    offsets = jax.random.randint(jax.random.fold_in(key, 1), (2,), 1, WIN - 1)
    return jnp.where(jnp.arange(2) == widest, WIN - 1, offsets).astype(jnp.int32)


def block_scale(stream_key, shape, split, low, largest):
    gain = 1.0
    for position, shards_of in split:
        steps = jax.random.uniform(jax.random.fold_in(jax.random.fold_in(stream_key, 6), position), (shards_of,), jnp.float32, low / len(split), largest / len(split))
        gain = gain * jnp.repeat(jnp.exp(steps), shape[position] // shards_of).reshape((-1,) + (1,) * (len(shape) - 1 - position))
    return gain


def scatter_about(key, shape, scale, most, shards=(), kind=jnp.bfloat16):
    entries = jax.random.normal(key, shape, jnp.float32) * scale
    if len(shards) > 0:
        entries = block_scale(key, shape, shards, -0.22, 0.18) * entries
    return jnp.clip(entries, min=-most, max=most).astype(kind)


def setup_inputs(seed: int = 0) -> dict:
    streams_of = jax.random.split(jax.random.key(seed), 8)
    return {
        "tokens": draw_tokens(jax.random.fold_in(streams_of[7], 71), 0),
        "w_qkv": draw_w_qkv(jax.random.fold_in(streams_of[7], 71), 0),
        "w_proj": scatter_about(streams_of[2], (D, D), D ** -0.5, 0.25),
        "w_merge": scatter_about(streams_of[3], (4 * D, D2), (4 * D) ** -0.5, 0.125),
        "skip_grad": scatter_about(streams_of[4], (LAT, LON, D), 1.0, 6.0, ((0, 16), (1, 16))),
        "merged_grad": scatter_about(streams_of[5], (LAT // 2, LON // 2, D2), 1.0, 6.0, ((0, 16), (1, 16))),
        "window_shift": draw_window_shift(jax.random.fold_in(streams_of[7], 71), 0),
    }


EPSILON = 1e-05
NEGATIVE = -1e+30

def normalize(values):
    values = values.astype(jnp.float32)
    center = values - lax.optimization_barrier(jnp.mean(values, axis=-1, keepdims=True))
    inverse = lax.rsqrt(lax.optimization_barrier(jnp.mean(center * center, axis=-1, keepdims=True)) + EPSILON)
    return (center * inverse, inverse)

def norm_back(grad_in, normed, inverse):
    return inverse * (grad_in - lax.optimization_barrier(jnp.mean(grad_in, axis=-1, keepdims=True)) - normed * lax.optimization_barrier(jnp.mean(grad_in * normed, axis=-1, keepdims=True)))

def merge_cells(grid_in):
    height, across, channels = grid_in.shape
    return grid_in.reshape(height // 2, 2, across // 2, 2, channels).transpose(0, 2, 3, 1, 4).reshape(height // 2, across // 2, 4 * channels)

def split_cells(grid_in):
    height, across, channels = grid_in.shape
    quarter = channels // 4
    return grid_in.reshape(height, across, 2, 2, quarter).transpose(0, 3, 1, 2, 4).reshape(2 * height, 2 * across, quarter)

def to_windows(block_in, extent):
    height, across, channels = block_in.shape
    return block_in.reshape(height // extent, extent, across // extent, extent, channels).transpose(0, 2, 1, 3, 4).reshape(height // extent * (across // extent), extent * extent, channels)

def from_windows(window_in, extent, height, across):
    channels = window_in.shape[-1]
    return window_in.reshape(height // extent, across // extent, extent, extent, channels).transpose(0, 2, 1, 3, 4).reshape(height, across, channels)

def window_mask(row_flags, across):
    grid_flags = jnp.broadcast_to(row_flags[:, None, None], (row_flags.shape[0], across, 1))
    return to_windows(grid_flags, WIN)[:, :, 0]

def split_heads(packed, heads):
    windows, per_window, channels = packed.shape
    model_width = channels // 3
    pieces = packed.astype(jnp.float32).reshape(windows, per_window, 3, heads, model_width // heads)
    return (pieces[:, :, 0], pieces[:, :, 1], pieces[:, :, 2])

def weights_of(queries, key_rows, usable):
    factor = queries.shape[-1] ** (-0.5)
    scores = jnp.einsum('nqhd,nkhd->nhqk', queries, key_rows) * factor
    scores = jnp.where(usable[:, None, None, :], scores, NEGATIVE)
    highest = lax.optimization_barrier(jnp.max(scores, axis=-1, keepdims=True))
    raised = jnp.exp(scores - highest)
    return raised / lax.optimization_barrier(jnp.sum(raised, axis=-1, keepdims=True))

def attend(packed, usable, heads):
    queries, key_rows, value_rows = split_heads(packed, heads)
    probs = weights_of(queries, key_rows, usable)
    rounded = lax.optimization_barrier(probs.astype(jnp.bfloat16)).astype(jnp.float32)
    output = jnp.einsum('nhqk,nkhd->nqhd', rounded, value_rows)
    return output.reshape(output.shape[0], output.shape[1], -1).astype(jnp.bfloat16)

def attend_back(packed, usable, upstream, heads):
    queries, key_rows, value_rows = split_heads(packed, heads)
    windows, per_window = (queries.shape[0], queries.shape[1])
    factor = queries.shape[-1] ** (-0.5)
    probs = weights_of(queries, key_rows, usable)
    rounded = lax.optimization_barrier(probs.astype(jnp.bfloat16)).astype(jnp.float32)
    grad_out = upstream.astype(jnp.float32).reshape(queries.shape)
    prob_grad = jnp.einsum('nqhd,nkhd->nhqk', grad_out, value_rows)
    row_total = lax.optimization_barrier(jnp.sum(probs * prob_grad, axis=-1, keepdims=True))
    score_grad = lax.optimization_barrier((probs * (prob_grad - row_total) * factor).astype(jnp.bfloat16)).astype(jnp.float32)
    query_grad = jnp.einsum('nhqk,nkhd->nqhd', score_grad, key_rows)
    key_grad = jnp.einsum('nhqk,nqhd->nkhd', score_grad, queries)
    value_grad = jnp.einsum('nhqk,nqhd->nkhd', rounded, grad_out)
    return jnp.concatenate([query_grad.reshape(windows, per_window, -1), key_grad.reshape(windows, per_window, -1), value_grad.reshape(windows, per_window, -1)], axis=-1)

def band_layout(grid_in, offset_lat, offset_lon):
    lat_rows, lon_cols, channels = grid_in.shape
    padding = jnp.zeros((WIN, lon_cols, channels), grid_in.dtype)
    padded = jnp.concatenate([padding, grid_in, padding], axis=0)
    banded = lax.dynamic_slice_in_dim(padded, offset_lat, lat_rows + WIN, 0)
    return jnp.roll(banded, -offset_lon, axis=1)

def grid_layout(banded, offset_lat, offset_lon):
    unrolled = jnp.roll(banded, offset_lon, axis=1)
    return lax.dynamic_slice_in_dim(unrolled, WIN - offset_lat, banded.shape[0] - WIN, 0)

def reference(tokens, w_qkv, w_proj, w_merge, skip_grad, merged_grad, window_shift):
    offset_lat = window_shift[0].astype(jnp.int32)
    offset_lon = window_shift[1].astype(jnp.int32)
    band_count = (LAT + WIN) // WIN
    padded_rows = offset_lat + jnp.arange(LAT + WIN, dtype=jnp.int32)
    band_flags = ((padded_rows >= WIN) & (padded_rows < WIN + LAT)).reshape(band_count, WIN)
    normed, inverse = normalize(tokens)
    hidden = normed.astype(jnp.bfloat16)
    flat_hidden = hidden.reshape(-1, D)
    packed = jnp.dot(flat_hidden, w_qkv, preferred_element_type=jnp.float32).astype(jnp.bfloat16).reshape(LAT, LON, 3 * D)
    packed_bands = band_layout(packed, offset_lat, offset_lon).reshape(band_count, WIN, LON, 3 * D)

    def forward_band(inputs):
        block_in, block_flags = inputs
        usable = window_mask(block_flags, LON)
        return from_windows(attend(to_windows(block_in, WIN), usable, HEADS), WIN, WIN, LON)
    stacked = lax.map(forward_band, (packed_bands, band_flags))
    attended = grid_layout(stacked.reshape(LAT + WIN, LON, D), offset_lat, offset_lon)
    flat_attended = attended.reshape(-1, D)
    summed = tokens.astype(jnp.float32) + jnp.dot(flat_attended, w_proj, preferred_element_type=jnp.float32).reshape(LAT, LON, D)
    skip_out = summed.astype(jnp.bfloat16)
    merged_in = merge_cells(skip_out)
    merged_normed, merged_inverse = normalize(merged_in)
    merged_hidden = merged_normed.astype(jnp.bfloat16)
    flat_merged = merged_hidden.reshape(-1, 4 * D)
    merged_out = jnp.dot(flat_merged, w_merge, preferred_element_type=jnp.float32).astype(jnp.bfloat16).reshape(LAT // 2, LON // 2, D2)
    flat_mgrad = merged_grad.reshape(-1, D2)
    merged_back = jnp.dot(flat_mgrad, w_merge.T, preferred_element_type=jnp.float32).reshape(merged_in.shape)
    merged_delta = norm_back(merged_back, merged_normed, merged_inverse)
    total_grad = (skip_grad.astype(jnp.float32) + split_cells(merged_delta)).astype(jnp.bfloat16)
    flat_total = total_grad.reshape(-1, D)
    dw_merge = jnp.dot(flat_merged.T, flat_mgrad, preferred_element_type=jnp.float32)
    attended_grad = jnp.dot(flat_total, w_proj.T, preferred_element_type=jnp.float32).astype(jnp.bfloat16).reshape(LAT, LON, D)
    dw_proj = jnp.dot(flat_attended.T, flat_total, preferred_element_type=jnp.float32)
    grad_bands = band_layout(attended_grad, offset_lat, offset_lon).reshape(band_count, WIN, LON, D)

    def backward_band(inputs):
        block_in, block_grad, block_flags = inputs
        usable = window_mask(block_flags, LON)
        result = attend_back(to_windows(block_in, WIN), usable, to_windows(block_grad, WIN), HEADS)
        return from_windows(result, WIN, WIN, LON)
    stacked_grad = lax.map(backward_band, (packed_bands, grad_bands, band_flags))
    packed_grad = grid_layout(stacked_grad.reshape(LAT + WIN, LON, 3 * D), offset_lat, offset_lon).astype(jnp.bfloat16)
    flat_pgrad = packed_grad.reshape(-1, 3 * D)
    dw_qkv = jnp.dot(flat_hidden.T, flat_pgrad, preferred_element_type=jnp.float32)
    hidden_grad = jnp.dot(flat_pgrad, w_qkv.T, preferred_element_type=jnp.float32).reshape(LAT, LON, D)
    input_grad = (total_grad.astype(jnp.float32) + norm_back(hidden_grad, normed, inverse)).astype(jnp.bfloat16)
    return (skip_out, merged_out, input_grad, dw_qkv, dw_proj, dw_merge)
```

```python
import jax
import jax.numpy as jnp
from jax import lax
from jax.experimental import pallas as pl
from jax.experimental.pallas import tpu as pltpu
from jax.sharding import PartitionSpec as P

HEADS = 16
WIN = 8


XS, YLO, CORES, YHI, ZS = 4, 2, 2, 2, 8
YS = YLO * YHI
MESH = pl.DeviceIdType.MESH


class Place:
    def __init__(self):
        lon = lax.axis_index("lon")
        lat = lax.axis_index("lat")
        self.lon, self.lat = lon, lat
        self.core = lon % CORES
        self.ylo = (lon // CORES) % YLO
        self.x = lon // (CORES * YLO)
        self.z = lat % ZS
        self.yhi = lat // ZS

    def at(self, x=None, ylo=None, core=None, yhi=None, z=None):
        x = self.x if x is None else x
        ylo = self.ylo if ylo is None else ylo
        core = self.core if core is None else core
        yhi = self.yhi if yhi is None else yhi
        z = self.z if z is None else z
        return ((x * YLO + ylo) * CORES + core, yhi * ZS + z)

    def sibling(self):
        return self.at(core=1 - self.core)

    def x_step(self, k):
        return (self.x + k) % XS

    def y_step(self, k):
        y = (self.yhi * YLO + self.ylo + k) % YS
        return (y // YLO, y % YLO)

    def z_step(self, k):
        return (self.z + k) % ZS

    def sum_partners(self):
        out = [self.sibling()]
        out += [self.at(x=self.x_step(k)) for k in range(1, XS)]
        for k in range(1, YS):
            yhi, ylo = self.y_step(k)
            out.append(self.at(yhi=yhi, ylo=ylo))
        out += [self.at(z=self.z_step(k)) for k in range(1, ZS)]
        return out


def device_of(pair):
    return {"lon": pair[0], "lat": pair[1]}


def greet(partners):
    barrier = pltpu.get_barrier_semaphore()
    for pair in partners:
        pl.semaphore_signal(barrier, inc=1, device_id=device_of(pair), device_id_type=MESH)
    pl.semaphore_wait(barrier, len(partners))


HALF = ZS // 2


def sum_scratch(rows):
    b16 = jnp.bfloat16
    copies = 2 + 2 * ((XS - 1) + (YS - 1)) + (ZS - 1)
    return [
        pltpu.VMEM((XS, YLO, YHI, ZS, rows, 128), b16),
        pltpu.VMEM((XS - 1, YLO, YHI, HALF, rows, 128), b16),
        pltpu.VMEM((YS - 1, XS, HALF, rows, 128), b16),
        pltpu.VMEM((YLO, YHI, HALF, rows, 128), b16),
        pltpu.VMEM((XS, HALF, rows, 128), b16),
        pltpu.VMEM((YS - 1, HALF, rows, 128), b16),
        pltpu.VMEM((XS - 1, HALF, rows, 128), b16),
        pltpu.VMEM((ZS, rows, 128), b16),
        pltpu.VMEM((ZS - 1, rows, 128), b16),
        pltpu.SemaphoreType.DMA((copies,)),
        pltpu.SemaphoreType.DMA((copies,)),
    ]


class Summing:
    def __init__(self, place, parts, scratch):
        (self.kept, self.from_x, self.from_y, self.sum_x, self.sum_y) = scratch[:5]
        (self.late_y, self.late_x, self.column, self.from_z) = scratch[5:9]
        self.send, self.recv = scratch[9:]
        self.parts, self.place = parts, place
        self.used = 0
        self.flying = {}

    def copy(self, src, dst, pair):
        slot = self.used
        self.used += 1
        made = pltpu.make_async_remote_copy(
            src_ref=src,
            dst_ref=dst,
            send_sem=self.send.at[slot],
            recv_sem=self.recv.at[slot],
            device_id=device_of(pair),
            device_id_type=MESH,
        )
        made.start()
        return made

    def start_core(self):
        other = 1 - self.place.core
        self.flying["core"] = [
            self.copy(
                self.parts.at[:, :, other, :, pl.ds(h * HALF, HALF)],
                self.kept.at[:, :, :, pl.ds(h * HALF, HALF)],
                self.place.sibling(),
            )
            for h in range(2)
        ]

    def add_core(self, h):
        core = self.place.core
        self.flying["core"][h].wait()

        def body(i, carry):
            x, rest = i // (YLO * YHI), i % (YLO * YHI)
            ylo, yhi = rest // YHI, rest % YHI
            zs = pl.ds(h * HALF, HALF)
            own = self.parts[x, ylo, core, yhi, zs].astype(jnp.float32)
            got = self.kept[x, ylo, yhi, zs].astype(jnp.float32)
            self.kept[x, ylo, yhi, zs] = (own + got).astype(jnp.bfloat16)
            return carry

        lax.fori_loop(0, XS * YLO * YHI, body, 0)

    def start_first(self, h):
        place = self.place
        zs = pl.ds(h * HALF, HALF)
        if h == 0:
            self.flying["x"] = [
                self.copy(
                    self.kept.at[place.x_step(k), :, :, zs],
                    self.from_x.at[k - 1],
                    place.at(x=place.x_step(k)),
                )
                for k in range(1, XS)
            ]
        else:
            self.flying["y"] = []
            for k in range(1, YS):
                yhi, ylo = place.y_step(k)
                self.flying["y"].append(
                    self.copy(
                        self.kept.at[:, ylo, yhi, zs],
                        self.from_y.at[k - 1],
                        place.at(yhi=yhi, ylo=ylo),
                    )
                )

    def add_first(self, h):
        place = self.place
        zs = pl.ds(h * HALF, HALF)
        for made in self.flying["x" if h == 0 else "y"]:
            made.wait()
        if h == 0:

            def body(i, carry):
                ylo, yhi = i // YHI, i % YHI
                total = self.kept[place.x, ylo, yhi, zs].astype(jnp.float32)
                for k in range(XS - 1):
                    total += self.from_x[k, ylo, yhi].astype(jnp.float32)
                self.sum_x[ylo, yhi] = total.astype(jnp.bfloat16)
                return carry

            lax.fori_loop(0, YLO * YHI, body, 0)
        else:

            def body(x, carry):
                total = self.kept[x, place.ylo, place.yhi, zs].astype(jnp.float32)
                for k in range(YS - 1):
                    total += self.from_y[k, x].astype(jnp.float32)
                self.sum_y[x] = total.astype(jnp.bfloat16)
                return carry

            lax.fori_loop(0, XS, body, 0)

    def start_second(self, h):
        place = self.place
        if h == 0:
            self.flying["late_y"] = []
            for k in range(1, YS):
                yhi, ylo = place.y_step(k)
                self.flying["late_y"].append(
                    self.copy(
                        self.sum_x.at[ylo, yhi],
                        self.late_y.at[k - 1],
                        place.at(yhi=yhi, ylo=ylo),
                    )
                )
        else:
            self.flying["late_x"] = [
                self.copy(
                    self.sum_y.at[place.x_step(k)],
                    self.late_x.at[k - 1],
                    place.at(x=place.x_step(k)),
                )
                for k in range(1, XS)
            ]

    def add_second(self, h):
        place = self.place
        for made in self.flying["late_y" if h == 0 else "late_x"]:
            made.wait()
        if h == 0:
            total = self.sum_x[place.ylo, place.yhi].astype(jnp.float32)
            for k in range(YS - 1):
                total += self.late_y[k].astype(jnp.float32)
        else:
            total = self.sum_y[place.x].astype(jnp.float32)
            for k in range(XS - 1):
                total += self.late_x[k].astype(jnp.float32)
        self.column[pl.ds(h * HALF, HALF)] = total.astype(jnp.bfloat16)

    def start_last(self):
        place = self.place
        self.flying["z"] = [
            self.copy(
                self.column.at[place.z_step(k)],
                self.from_z.at[k - 1],
                place.at(z=place.z_step(k)),
            )
            for k in range(1, ZS)
        ]

    def add_last(self, out):
        for made in self.flying["z"]:
            made.wait()
        total = self.column[self.place.z].astype(jnp.float32)
        for k in range(ZS - 1):
            total += self.from_z[k].astype(jnp.float32)
        out[...] = total


def sum_kernel(parts, out, *scratch):
    place = Place()
    greet(place.sum_partners())
    work = Summing(place, parts, scratch)
    work.start_core()
    for h in range(2):
        work.add_core(h)
        work.start_first(h)
    for h in range(2):
        work.add_first(h)
        work.start_second(h)
    for h in range(2):
        work.add_second(h)
    work.start_last()
    work.add_last(out)


def weight_sums(parts):
    rows = parts.shape[5]
    return pl.pallas_call(
        sum_kernel,
        out_shape=jax.ShapeDtypeStruct((rows, 128), jnp.float32),
        in_specs=[pl.BlockSpec(memory_space=pltpu.VMEM)],
        out_specs=pl.BlockSpec(memory_space=pltpu.VMEM),
        scratch_shapes=sum_scratch(rows),
        compiler_params=pltpu.CompilerParams(
            collective_id=0, has_side_effects=True, vmem_limit_bytes=48 * 2**20
        ),
    )(parts)


EPSILON = 1e-05
NEGATIVE = -1e30


def with_halo(shard, sides, width):
    for axis, dim in sides:
        count, length = (lax.axis_size(axis), shard.shape[dim])
        up = [(i, (i + 1) % count) for i in range(count)]
        down = [(j, i) for i, j in up]
        last = lax.slice_in_dim(shard, length - width, length, axis=dim)
        leading = lax.slice_in_dim(shard, 0, width, axis=dim)
        before = lax.ppermute(last, axis, up)
        after = lax.ppermute(leading, axis, down)
        shard = jnp.concatenate([before, shard, after], axis=dim)
    return shard


def normalize(values):
    values = values.astype(jnp.float32)
    center = values - jnp.mean(values, axis=-1, keepdims=True)
    inverse = lax.rsqrt(jnp.mean(center * center, axis=-1, keepdims=True) + EPSILON)
    return (center * inverse, inverse)


def norm_back(grad_in, normed, inverse):
    return inverse * (
        grad_in
        - jnp.mean(grad_in, axis=-1, keepdims=True)
        - normed * jnp.mean(grad_in * normed, axis=-1, keepdims=True)
    )


def merge_cells(grid_in):
    height, across, channels = grid_in.shape
    return (
        grid_in.reshape(height // 2, 2, across // 2, 2, channels)
        .transpose(0, 2, 3, 1, 4)
        .reshape(height // 2, across // 2, 4 * channels)
    )


def split_cells(grid_in):
    height, across, channels = grid_in.shape
    quarter = channels // 4
    return (
        grid_in.reshape(height, across, 2, 2, quarter)
        .transpose(0, 3, 1, 2, 4)
        .reshape(2 * height, 2 * across, quarter)
    )


def to_windows(block_in, extent):
    height, across, channels = block_in.shape
    return (
        block_in.reshape(height // extent, extent, across // extent, extent, channels)
        .transpose(0, 2, 1, 3, 4)
        .reshape(height // extent * (across // extent), extent * extent, channels)
    )


def from_windows(window_in, extent, height, across):
    channels = window_in.shape[-1]
    return (
        window_in.reshape(height // extent, across // extent, extent, extent, channels)
        .transpose(0, 2, 1, 3, 4)
        .reshape(height, across, channels)
    )


def window_mask(row_flags, across):
    grid_flags = jnp.broadcast_to(row_flags[:, None, None], (row_flags.shape[0], across, 1))
    return to_windows(grid_flags, WIN)[:, :, 0]


def split_heads(packed, heads):
    windows, per_window, channels = packed.shape
    model_width = channels // 3
    pieces = packed.reshape(windows, per_window, 3, heads, model_width // heads)
    return (pieces[:, :, 0], pieces[:, :, 1], pieces[:, :, 2])


def weights_of(queries, key_rows, usable):
    factor = queries.shape[-1] ** (-0.5)
    scores = (
        jnp.einsum("nqhd,nkhd->nhqk", queries, key_rows, preferred_element_type=jnp.float32)
        * factor
    )
    scores = jnp.where(usable[:, None, None, :], scores, NEGATIVE)
    highest = jnp.max(scores, axis=-1, keepdims=True)
    raised = jnp.exp(scores - highest)
    return raised / jnp.sum(raised, axis=-1, keepdims=True)


def attend(packed, usable, heads):
    queries, key_rows, value_rows = split_heads(packed, heads)
    probs = weights_of(queries, key_rows, usable)
    rounded = probs.astype(jnp.bfloat16)
    output = jnp.einsum("nhqk,nkhd->nqhd", rounded, value_rows, preferred_element_type=jnp.float32)
    return output.reshape(output.shape[0], output.shape[1], -1).astype(jnp.bfloat16)


def attend_back(packed, usable, upstream, heads):
    queries, key_rows, value_rows = split_heads(packed, heads)
    windows, per_window = (queries.shape[0], queries.shape[1])
    factor = queries.shape[-1] ** (-0.5)
    probs = weights_of(queries, key_rows, usable)
    rounded = probs.astype(jnp.bfloat16)
    grad_out = upstream.reshape(queries.shape)
    prob_grad = jnp.einsum(
        "nqhd,nkhd->nhqk", grad_out, value_rows, preferred_element_type=jnp.float32
    )
    row_total = jnp.sum(probs * prob_grad, axis=-1, keepdims=True)
    score_grad = (probs * (prob_grad - row_total) * factor).astype(jnp.bfloat16)
    query_grad = jnp.einsum(
        "nhqk,nkhd->nqhd", score_grad, key_rows, preferred_element_type=jnp.float32
    )
    key_grad = jnp.einsum(
        "nhqk,nqhd->nkhd", score_grad, queries, preferred_element_type=jnp.float32
    )
    value_grad = jnp.einsum(
        "nhqk,nqhd->nkhd", rounded, grad_out, preferred_element_type=jnp.float32
    )
    return jnp.concatenate(
        [
            query_grad.reshape(windows, per_window, -1),
            key_grad.reshape(windows, per_window, -1),
            value_grad.reshape(windows, per_window, -1),
        ],
        axis=-1,
    )


def on_device(tokens, w_qkv, w_proj, w_merge, skip_grad, merged_grad, window_shift):
    height, across, model_width = tokens.shape
    offset_lat = window_shift[0]
    offset_lon = window_shift[1]
    band_index = lax.axis_index("lat")
    total_rows = height * lax.axis_size("lat")
    global_rows = band_index * height - WIN + jnp.arange(height + 2 * WIN, dtype=jnp.int32)
    row_flags = (global_rows >= 0) & (global_rows < total_rows)
    normed, inverse = normalize(tokens)
    hidden = normed.astype(jnp.bfloat16)
    flat_hidden = hidden.reshape(-1, model_width)
    packed = (
        jnp.dot(flat_hidden, w_qkv, preferred_element_type=jnp.float32)
        .astype(jnp.bfloat16)
        .reshape(height, across, 3 * model_width)
    )
    packed_ext = with_halo(packed, (("lon", 1), ("lat", 0)), WIN)
    packed_ext = jnp.where(row_flags[:, None, None], packed_ext, jnp.zeros_like(packed_ext))
    cut_height = (height // WIN + 1) * WIN
    cut_across = (across // WIN + 1) * WIN
    packed_cut = lax.dynamic_slice(
        packed_ext, (offset_lat, offset_lon, 0), (cut_height, cut_across, 3 * model_width)
    )
    flags_cut = lax.dynamic_slice_in_dim(row_flags, offset_lat, cut_height, 0)
    usable = window_mask(flags_cut, cut_across)
    packed_win = to_windows(packed_cut, WIN)
    output_cut = from_windows(attend(packed_win, usable, HEADS), WIN, cut_height, cut_across)
    attended = lax.dynamic_slice(
        output_cut, (WIN - offset_lat, WIN - offset_lon, 0), (height, across, model_width)
    )
    flat_attended = attended.reshape(-1, model_width)
    summed = tokens.astype(jnp.float32) + jnp.dot(
        flat_attended, w_proj, preferred_element_type=jnp.float32
    ).reshape(height, across, model_width)
    skip_out = summed.astype(jnp.bfloat16)
    merged_in = merge_cells(skip_out)
    merged_normed, merged_inverse = normalize(merged_in)
    merged_hidden = merged_normed.astype(jnp.bfloat16)
    flat_merged = merged_hidden.reshape(-1, 4 * model_width)
    merged_out = (
        jnp.dot(flat_merged, w_merge, preferred_element_type=jnp.float32)
        .astype(jnp.bfloat16)
        .reshape(height // 2, across // 2, -1)
    )
    flat_mgrad = merged_grad.reshape(-1, merged_grad.shape[-1])
    merged_back = jnp.einsum(
        "te,de->td", flat_mgrad, w_merge, preferred_element_type=jnp.float32
    ).reshape(merged_in.shape)
    merged_delta = norm_back(merged_back, merged_normed, merged_inverse)
    total_grad = (skip_grad.astype(jnp.float32) + split_cells(merged_delta)).astype(jnp.bfloat16)
    flat_total = total_grad.reshape(-1, model_width)
    merge_part = jnp.einsum(
        "tc,te->ce", flat_merged, flat_mgrad, preferred_element_type=jnp.float32
    )
    attended_grad = (
        jnp.einsum("te,de->td", flat_total, w_proj, preferred_element_type=jnp.float32)
        .astype(jnp.bfloat16)
        .reshape(height, across, model_width)
    )
    proj_part = jnp.einsum(
        "td,te->de", flat_attended, flat_total, preferred_element_type=jnp.float32
    )
    grad_ext = with_halo(attended_grad, (("lon", 1), ("lat", 0)), WIN)
    grad_ext = jnp.where(row_flags[:, None, None], grad_ext, jnp.zeros_like(grad_ext))
    grad_cut = lax.dynamic_slice(
        grad_ext, (offset_lat, offset_lon, 0), (cut_height, cut_across, model_width)
    )
    packed_back = attend_back(packed_win, usable, to_windows(grad_cut, WIN), HEADS)
    packed_grid = from_windows(packed_back, WIN, cut_height, cut_across)
    packed_grad = lax.dynamic_slice(
        packed_grid, (WIN - offset_lat, WIN - offset_lon, 0), (height, across, 3 * model_width)
    ).astype(jnp.bfloat16)
    flat_pgrad = packed_grad.reshape(-1, 3 * model_width)
    qkv_part = jnp.einsum("td,te->de", flat_hidden, flat_pgrad, preferred_element_type=jnp.float32)
    hidden_grad = jnp.einsum(
        "te,de->td", flat_pgrad, w_qkv, preferred_element_type=jnp.float32
    ).reshape(height, across, model_width)
    input_grad = (total_grad.astype(jnp.float32) + norm_back(hidden_grad, normed, inverse)).astype(
        jnp.bfloat16
    )
    merge_block = (
        merge_part.astype(jnp.bfloat16)
        .reshape(XS, YLO, CORES, 128, YHI, ZS, 64)
        .transpose(0, 1, 2, 4, 5, 6, 3)
    )
    qkv_block = qkv_part.astype(jnp.bfloat16).reshape(XS, YLO, CORES, 32, YHI, ZS, 96)
    proj_block = proj_part.astype(jnp.bfloat16).reshape(XS, YLO, CORES, 32, YHI, ZS, 32)
    fine_block = jnp.concatenate([qkv_block, proj_block], axis=-1).transpose(0, 1, 2, 4, 5, 3, 6)
    mine = weight_sums(jnp.concatenate([merge_block, fine_block], axis=5))
    return (
        skip_out,
        merged_out,
        input_grad,
        mine[64:, :96],
        mine[64:, 96:],
        mine[:64].T,
    )


def solution(mesh):
    in_specs = (
        P("lat", "lon", None),
        P(),
        P(),
        P(),
        P("lat", "lon", None),
        P("lat", "lon", None),
        P(),
    )
    out_specs = (
        P("lat", "lon", None),
        P("lat", "lon", None),
        P("lat", "lon", None),
        P("lon", "lat"),
        P("lon", "lat"),
        P("lon", "lat"),
    )
    return jax.shard_map(
        on_device, mesh=mesh, in_specs=in_specs, out_specs=out_specs, check_vma=False
    )
```

```python
import jax
import jax.numpy as jnp
from jax import lax
from jax.experimental import pallas as pl
from jax.experimental.pallas import tpu as pltpu
from jax.sharding import PartitionSpec as P

HEADS = 16
WIN = 8
EPSILON = 1e-05
NEGATIVE = -1e30
D = 512
D2 = 1024
ROWS, COLS = 8, 32
CELLS = ROWS * COLS
ACROSS = COLS // WIN + 1
BAND = ACROSS * WIN * WIN
LAT = 128
FACTOR = 32 ** (-0.5)
MERGED = CELLS // 4
EDGE = ROWS * WIN
LEFT = 3 * CELLS
RIGHT = LEFT + 3 * EDGE
SOURCES = RIGHT + 3 * EDGE
F32, B16 = jnp.float32, jnp.bfloat16

XS, YLO, CORES, YHI, ZS = 4, 2, 2, 2, 8
YS = YLO * YHI
MESH = pl.DeviceIdType.MESH


class Place:
    def __init__(self):
        lon = lax.axis_index("lon")
        lat = lax.axis_index("lat")
        self.lon, self.lat = lon, lat
        self.core = lon % CORES
        self.ylo = (lon // CORES) % YLO
        self.x = lon // (CORES * YLO)
        self.z = lat % ZS
        self.yhi = lat // ZS

    def at(self, x=None, ylo=None, core=None, yhi=None, z=None):
        x = self.x if x is None else x
        ylo = self.ylo if ylo is None else ylo
        core = self.core if core is None else core
        yhi = self.yhi if yhi is None else yhi
        z = self.z if z is None else z
        return ((x * YLO + ylo) * CORES + core, yhi * ZS + z)

    def beside(self, dlat, dlon):
        lons, lats = XS * YLO * CORES, YHI * ZS
        return ((self.lon + dlon) % lons, (self.lat + dlat) % lats)

    def sibling(self):
        return self.at(core=1 - self.core)

    def x_step(self, k):
        return (self.x + k) % XS

    def y_step(self, k):
        y = (self.yhi * YLO + self.ylo + k) % YS
        return (y // YLO, y % YLO)

    def z_step(self, k):
        return (self.z + k) % ZS

    def sum_partners(self):
        out = [self.sibling()]
        out += [self.at(x=self.x_step(k)) for k in range(1, XS)]
        for k in range(1, YS):
            yhi, ylo = self.y_step(k)
            out.append(self.at(yhi=yhi, ylo=ylo))
        out += [self.at(z=self.z_step(k)) for k in range(1, ZS)]
        return out


def device_of(pair):
    return {"lon": pair[0], "lat": pair[1]}


def greet(partners):
    barrier = pltpu.get_barrier_semaphore()
    for pair in partners:
        pl.semaphore_signal(barrier, inc=1, device_id=device_of(pair), device_id_type=MESH)
    pl.semaphore_wait(barrier, len(partners))


HALF = ZS // 2


def sum_scratch(rows):
    b16 = jnp.bfloat16
    copies = 2 + 2 * ((XS - 1) + (YS - 1)) + (ZS - 1)
    return [
        pltpu.VMEM((XS, YLO, YHI, ZS, rows, 128), b16),
        pltpu.VMEM((XS - 1, YLO, YHI, HALF, rows, 128), b16),
        pltpu.VMEM((YS - 1, XS, HALF, rows, 128), b16),
        pltpu.VMEM((YLO, YHI, HALF, rows, 128), b16),
        pltpu.VMEM((XS, HALF, rows, 128), b16),
        pltpu.VMEM((YS - 1, HALF, rows, 128), b16),
        pltpu.VMEM((XS - 1, HALF, rows, 128), b16),
        pltpu.VMEM((ZS, rows, 128), b16),
        pltpu.VMEM((ZS - 1, rows, 128), b16),
        pltpu.SemaphoreType.DMA((copies,)),
        pltpu.SemaphoreType.DMA((copies,)),
    ]


class Summing:
    def __init__(self, place, parts, scratch):
        (self.kept, self.from_x, self.from_y, self.sum_x, self.sum_y) = scratch[:5]
        (self.late_y, self.late_x, self.column, self.from_z) = scratch[5:9]
        self.send, self.recv = scratch[9:]
        self.parts, self.place = parts, place
        self.used = 0
        self.flying = {}

    def copy(self, src, dst, pair):
        slot = self.used
        self.used += 1
        made = pltpu.make_async_remote_copy(
            src_ref=src,
            dst_ref=dst,
            send_sem=self.send.at[slot],
            recv_sem=self.recv.at[slot],
            device_id=device_of(pair),
            device_id_type=MESH,
        )
        made.start()
        return made

    def start_core(self):
        other = 1 - self.place.core
        self.flying["core"] = [
            self.copy(
                self.parts.at[:, :, other, :, pl.ds(h * HALF, HALF)],
                self.kept.at[:, :, :, pl.ds(h * HALF, HALF)],
                self.place.sibling(),
            )
            for h in range(2)
        ]

    def add_core(self, h):
        core = self.place.core
        self.flying["core"][h].wait()

        def body(i, carry):
            x, rest = i // (YLO * YHI), i % (YLO * YHI)
            ylo, yhi = rest // YHI, rest % YHI
            zs = pl.ds(h * HALF, HALF)
            own = self.parts[x, ylo, core, yhi, zs].astype(jnp.float32)
            got = self.kept[x, ylo, yhi, zs].astype(jnp.float32)
            self.kept[x, ylo, yhi, zs] = (own + got).astype(jnp.bfloat16)
            return carry

        lax.fori_loop(0, XS * YLO * YHI, body, 0)

    def start_first(self, h):
        place = self.place
        zs = pl.ds(h * HALF, HALF)
        if h == 0:
            self.flying["x"] = [
                self.copy(
                    self.kept.at[place.x_step(k), :, :, zs],
                    self.from_x.at[k - 1],
                    place.at(x=place.x_step(k)),
                )
                for k in range(1, XS)
            ]
        else:
            self.flying["y"] = []
            for k in range(1, YS):
                yhi, ylo = place.y_step(k)
                self.flying["y"].append(
                    self.copy(
                        self.kept.at[:, ylo, yhi, zs],
                        self.from_y.at[k - 1],
                        place.at(yhi=yhi, ylo=ylo),
                    )
                )

    def add_first(self, h):
        place = self.place
        zs = pl.ds(h * HALF, HALF)
        for made in self.flying["x" if h == 0 else "y"]:
            made.wait()
        if h == 0:

            def body(i, carry):
                ylo, yhi = i // YHI, i % YHI
                total = self.kept[place.x, ylo, yhi, zs].astype(jnp.float32)
                for k in range(XS - 1):
                    total += self.from_x[k, ylo, yhi].astype(jnp.float32)
                self.sum_x[ylo, yhi] = total.astype(jnp.bfloat16)
                return carry

            lax.fori_loop(0, YLO * YHI, body, 0)
        else:

            def body(x, carry):
                total = self.kept[x, place.ylo, place.yhi, zs].astype(jnp.float32)
                for k in range(YS - 1):
                    total += self.from_y[k, x].astype(jnp.float32)
                self.sum_y[x] = total.astype(jnp.bfloat16)
                return carry

            lax.fori_loop(0, XS, body, 0)

    def start_second(self, h):
        place = self.place
        if h == 0:
            self.flying["late_y"] = []
            for k in range(1, YS):
                yhi, ylo = place.y_step(k)
                self.flying["late_y"].append(
                    self.copy(
                        self.sum_x.at[ylo, yhi],
                        self.late_y.at[k - 1],
                        place.at(yhi=yhi, ylo=ylo),
                    )
                )
        else:
            self.flying["late_x"] = [
                self.copy(
                    self.sum_y.at[place.x_step(k)],
                    self.late_x.at[k - 1],
                    place.at(x=place.x_step(k)),
                )
                for k in range(1, XS)
            ]

    def add_second(self, h):
        place = self.place
        for made in self.flying["late_y" if h == 0 else "late_x"]:
            made.wait()
        if h == 0:
            total = self.sum_x[place.ylo, place.yhi].astype(jnp.float32)
            for k in range(YS - 1):
                total += self.late_y[k].astype(jnp.float32)
        else:
            total = self.sum_y[place.x].astype(jnp.float32)
            for k in range(XS - 1):
                total += self.late_x[k].astype(jnp.float32)
        self.column[pl.ds(h * HALF, HALF)] = total.astype(jnp.bfloat16)

    def start_last(self):
        place = self.place
        self.flying["z"] = [
            self.copy(
                self.column.at[place.z_step(k)],
                self.from_z.at[k - 1],
                place.at(z=place.z_step(k)),
            )
            for k in range(1, ZS)
        ]

    def add_last(self, out):
        for made in self.flying["z"]:
            made.wait()
        total = self.column[self.place.z].astype(jnp.float32)
        for k in range(ZS - 1):
            total += self.from_z[k].astype(jnp.float32)
        out[...] = total


def iota(shape, dim):
    return lax.broadcasted_iota(jnp.int32, shape, dim)


def one_hot(rows, cols, index):
    place = index(iota((rows, 1), 0))
    return jnp.where(iota((rows, cols), 1) == place, 1.0, 0.0).astype(B16)


def dot(a, b):
    return jnp.dot(a, b, preferred_element_type=F32)


def dot_nt(a, b):
    return lax.dot_general(a, b, (((1,), (1,)), ((), ())), preferred_element_type=F32)


def dot_tn(a, b):
    return lax.dot_general(a, b, (((0,), (0,)), ((), ())), preferred_element_type=F32)


def merge_order(n):
    part, r, c = n >> 6, (n >> 4) & 3, n & 15
    return 2 * r + (part & 1), 2 * c + (part >> 1)


def merge_index(n):
    i, j = n >> 5, n & 31
    return (((j & 1) * 2 + (i & 1)) << 6) + ((i >> 1) << 4) + (j >> 1)


def to_merged_index(n):
    i, j = merge_order(n)
    return i * COLS + j


def edge_index(n):
    return ((n >> 3) & 7) * COLS + (n & 7) + (n >> 6) * (COLS - WIN)


def normalize(values):
    center = values - jnp.mean(values, axis=-1, keepdims=True)
    inverse = lax.rsqrt(jnp.mean(center * center, axis=-1, keepdims=True) + EPSILON)
    return center * inverse, inverse


class Halo:
    def __init__(self, place, ext, edges, send, recv):
        self.place, self.ext, self.edges = place, ext, edges
        self.send, self.recv = send, recv

    def start(self, own):
        self.flying = []
        jobs = [(own, 0, 1, 0), (own, 2 * CELLS, -1, 0)]
        first, last = self.edges.at[pl.ds(0, EDGE)], self.edges.at[pl.ds(EDGE, EDGE)]
        for step in range(3):
            dlat = 1 - step
            jobs.append((last, LEFT + step * EDGE, dlat, 1))
            jobs.append((first, RIGHT + step * EDGE, dlat, -1))
        for slot, (src, offset, dlat, dlon) in enumerate(jobs):
            made = pltpu.make_async_remote_copy(
                src_ref=src,
                dst_ref=self.ext.at[pl.ds(offset, src.shape[0])],
                send_sem=self.send.at[slot],
                recv_sem=self.recv.at[slot],
                device_id=device_of(self.place.beside(dlat, dlon)),
                device_id_type=MESH,
            )
            made.start()
            self.flying.append(made)

    def wait(self):
        for made in self.flying:
            made.wait()


def halo_partners(place):
    return [
        place.beside(dlat, dlon)
        for dlat in (-1, 0, 1)
        for dlon in (-1, 0, 1)
        if (dlat, dlon) != (0, 0)
    ]


def band_of(ext, k, gather):
    source = jnp.concatenate(
        [
            ext[pl.ds(CELLS * k, 2 * CELLS)],
            ext[pl.ds(LEFT + EDGE * k, 2 * EDGE)],
            ext[pl.ds(RIGHT + EDGE * k, 2 * EDGE)],
        ],
        axis=0,
    )
    return dot(gather[...], source)


def row_valid(place, shift_lat, k, n):
    row = ROWS * place.lat - WIN + shift_lat + WIN * k + ((n >> 3) & 7)
    return (row >= 0) & (row < LAT)


def section_kernel(
    shift,
    tokens,
    skip_grad,
    merged_grad,
    w_qkv_hbm,
    w_proj_hbm,
    w_merge_hbm,
    skip_out,
    merged_out,
    input_grad,
    sum_merge,
    sum_fine,
    w_qkv,
    w_proj,
    w_merge,
    load,
    ext,
    ext_back,
    edges,
    edges_back,
    grad_own,
    halo_send,
    halo_recv,
    halo_back_send,
    halo_back_recv,
    gather,
    scatter,
    hidden,
    packed,
    probs,
    attended,
    back_in,
    packed_grad,
    own_both,
    spread,
    merged_hidden,
    total_grad,
    parts_merge,
    parts_fine,
    *scratch,
):
    place = Place()
    a, b = shift[0], shift[1]
    loads = [
        pltpu.make_async_copy(src, dst, load.at[n])
        for n, (src, dst) in enumerate(
            ((w_qkv_hbm, w_qkv), (w_proj_hbm, w_proj), (w_merge_hbm, w_merge))
        )
    ]
    for made in loads:
        made.start()
    count = len(scratch) // 2
    merge_sum = Summing(place, parts_merge, scratch[:count])
    fine_sum = Summing(place, parts_fine, scratch[count:])

    pick_edges = one_hot(2 * EDGE, CELLS, edge_index)
    edges[...] = dot(pick_edges, tokens[...]).astype(B16)
    greet(place.sum_partners() + halo_partners(place))
    halo = Halo(place, ext, edges, halo_send, halo_recv)
    halo.start(tokens)
    ext[pl.ds(CELLS, CELLS)] = tokens[...]

    def gather_index(n):
        w, i, j = n >> 6, (n >> 3) & 7, n & 7
        row, col = a + i, b + WIN * w + j - WIN
        inside = row * COLS + col
        left = 2 * CELLS + row * WIN + col + WIN
        right = 2 * CELLS + 2 * EDGE + row * WIN + col - COLS
        return jnp.where(col < 0, left, jnp.where(col >= COLS, right, inside))

    gather[...] = one_hot(BAND, 2 * CELLS + 4 * EDGE, gather_index)

    def scatter_index(n):
        i, j = merge_order(n)
        row, col = ROWS + i - a, WIN + j - b
        return (row >> 3) * BAND + ((col >> 3) << 6) + ((row & 7) << 3) + (col & 7)

    scatter[...] = one_hot(CELLS, 2 * BAND, scatter_index)
    to_merged = one_hot(CELLS, CELLS, to_merged_index)
    to_rows = one_hot(CELLS, CELLS, merge_index)
    own_tokens = dot(to_merged, tokens[...])
    own_normed, own_inverse = normalize(own_tokens)
    own_both[pl.ds(0, CELLS)] = own_normed.astype(B16)
    own_skip = dot(to_merged, skip_grad[...])
    grads = merged_grad[...]
    loads[2].wait()
    merged_back = [
        dot_nt(grads, w_merge[pl.ds(D * part, D)]) for part in range(4)
    ]
    loads[0].wait()
    loads[1].wait()

    halo.wait()
    for k in range(2):
        rows = pl.ds(BAND * k, BAND)
        normed, _ = normalize(band_of(ext, k, gather))
        hidden[...] = normed.astype(B16)
        for n in range(3):
            packed[rows, pl.ds(D * n, D)] = dot(hidden[...], w_qkv[:, pl.ds(D * n, D)]).astype(B16)

    head_mask = (iota((4 * 64, 128), 0) >> 6) == (iota((4 * 64, 128), 1) >> 5)
    head_one = jnp.where(head_mask, 1.0, 0.0)
    head_b16 = head_one.astype(B16)

    def expand(values):
        return jnp.concatenate([values] * 4, axis=0) * head_b16

    def fold(values):
        kept = values * head_one
        return (kept[0:64] + kept[64:128]) + (kept[128:192] + kept[192:256])

    def lanes(n, g):
        return pl.ds(D * n + 128 * g, 128)

    def forward(w, carry):
        rows = pl.ds(pl.multiple_of(w * 64, 64), 64)
        valid = row_valid(place, a, (w >= ACROSS).astype(jnp.int32), iota((64, 1), 0))
        bias = jnp.where(valid, 0.0, NEGATIVE)
        for g in range(4):
            queries = expand(packed[rows, lanes(0, g)])
            scores = dot_nt(packed[rows, lanes(1, g)], queries) * FACTOR + bias
            raised = jnp.exp(scores - jnp.max(scores, axis=0, keepdims=True))
            prob = raised * (1.0 / jnp.sum(raised, axis=0, keepdims=True))
            probs[w, g] = prob
            output = dot_tn(prob.astype(B16), packed[rows, lanes(2, g)])
            attended[rows, pl.ds(128 * g, 128)] = fold(output).astype(B16)
        return carry

    lax.fori_loop(0, 2 * ACROSS, forward, 0)

    own_attended = dot(scatter[...], attended[...]).astype(B16)
    own_both[pl.ds(CELLS, CELLS)] = own_attended
    own_out = (own_tokens + dot(own_attended, w_proj[...])).astype(B16)
    skip_out[...] = dot(to_rows, own_out).astype(B16)
    merged_in = own_out.astype(F32)
    quarters = [merged_in[MERGED * n : MERGED * (n + 1)] for n in range(4)]
    wide = 1.0 / (4 * D)

    def mean(values):
        return sum(jnp.sum(v, axis=-1, keepdims=True) for v in values) * wide

    center_at = mean(quarters)
    centers = [q - center_at for q in quarters]
    merged_inverse = lax.rsqrt(mean([c * c for c in centers]) + EPSILON)
    merged_normed = [c * merged_inverse for c in centers]
    back_mean = mean(merged_back)
    back_dot = mean([g * n for g, n in zip(merged_back, merged_normed)])
    for n in range(4):
        rows = pl.ds(MERGED * n, MERGED)
        merged_hidden[:, pl.ds(D * n, D)] = merged_normed[n].astype(B16)
        delta = merged_inverse * (merged_back[n] - back_mean - merged_normed[n] * back_dot)
        total_grad[rows] = (own_skip[MERGED * n : MERGED * (n + 1)] + delta).astype(B16)

    own_grad = dot_nt(total_grad[...], w_proj[...]).astype(B16)
    grad_own[...] = dot(to_rows, own_grad).astype(B16)
    edges_back[...] = dot(pick_edges, grad_own[...]).astype(B16)
    back_halo = Halo(place, ext_back, edges_back, halo_back_send, halo_back_recv)
    back_halo.start(grad_own)
    ext_back[pl.ds(CELLS, CELLS)] = grad_own[...]

    def merge_parts(i, carry):
        yhi, half = i // 2, i % 2
        columns = pl.ds(pl.multiple_of(i * 256, 256), 256)
        left = merged_grad[:, columns]
        for n in range(4):
            block = dot_tn(left, merged_hidden[:, pl.ds(D * n, D)]).astype(B16)
            for m in range(4):
                parts_merge[n, m // 2, m % 2, yhi, pl.ds(half * 4, 4)] = block[
                    :, 128 * m : 128 * (m + 1)
                ].reshape(4, 64, 128)
        return carry

    lax.fori_loop(0, 4, merge_parts, 0)
    merge_sum.start_core()
    merged_out[...] = dot(merged_hidden[...], w_merge[...]).astype(B16)
    transposed = own_both[...].T

    back_halo.wait()
    for k in range(2):
        values = band_of(ext_back, k, gather)
        valid = row_valid(place, a, k, iota((BAND, 1), 0))
        back_in[pl.ds(BAND * k, BAND)] = jnp.where(valid, values, 0.0).astype(B16)

    def backward(w, carry):
        rows = pl.ds(pl.multiple_of(w * 64, 64), 64)
        for g in range(4):
            queries = expand(packed[rows, lanes(0, g)])
            upstream = expand(back_in[rows, pl.ds(128 * g, 128)])
            key_rows, value_rows = packed[rows, lanes(1, g)], packed[rows, lanes(2, g)]
            prob = probs[w, g]
            prob_grad = dot_nt(value_rows, upstream)
            total = jnp.sum(prob * prob_grad, axis=0, keepdims=True)
            score_grad = (prob * (prob_grad - total) * FACTOR).astype(B16)
            packed_grad[rows, lanes(0, g)] = fold(dot_tn(score_grad, key_rows)).astype(B16)
            packed_grad[rows, lanes(1, g)] = dot(score_grad, queries).astype(B16)
            packed_grad[rows, lanes(2, g)] = dot(prob.astype(B16), upstream).astype(B16)
        return carry

    lax.fori_loop(0, 3, backward, 0)
    for h in range(2):
        merge_sum.add_core(h)
        merge_sum.start_first(h)
    lax.fori_loop(3, 2 * ACROSS, backward, 0)

    def widen(n):
        return (n // 96) * 128 + n % 96

    widen_fine = one_hot(384, 512, widen)
    widen_proj = one_hot(128, 512, lambda n: (n >> 5) * 128 + 96 + (n & 31))
    for n in range(3):
        columns = pl.ds(D * n, D)
        packed[pl.ds(0, CELLS), columns] = dot(scatter[...], packed_grad[:, columns]).astype(B16)
    own_packed = packed[pl.ds(0, CELLS)]
    for n in range(4):
        columns = pl.ds(512 * n, 512)
        spread[pl.ds(0, CELLS), columns] = dot(
            own_packed[:, 384 * n : 384 * (n + 1)], widen_fine
        ).astype(B16)
        spread[pl.ds(CELLS, CELLS), columns] = dot(
            total_grad[:, pl.ds(128 * n, 128)], widen_proj
        ).astype(B16)
    for r in range(YHI * ZS // 4):
        block = dot(transposed, spread[:, pl.ds(512 * r, 512)]).astype(B16)
        for m in range(4):
            lat = 4 * r + m
            parts_fine[:, :, :, lat // ZS, lat % ZS] = block[:, 128 * m : 128 * (m + 1)].reshape(
                XS, YLO, CORES, 32, 128
            )
    fine_sum.start_core()
    hidden_grad = dot_nt(own_packed, w_qkv[...])
    own_input = total_grad[...].astype(F32) + own_inverse * (
        hidden_grad
        - jnp.mean(hidden_grad, axis=-1, keepdims=True)
        - own_normed * jnp.mean(hidden_grad * own_normed, axis=-1, keepdims=True)
    )
    input_grad[...] = dot(to_rows, own_input.astype(B16)).astype(B16)

    for h in range(2):
        merge_sum.add_first(h)
        merge_sum.start_second(h)
    for h in range(2):
        fine_sum.add_core(h)
        fine_sum.start_first(h)
    for h in range(2):
        merge_sum.add_second(h)
    merge_sum.start_last()
    for h in range(2):
        fine_sum.add_first(h)
        fine_sum.start_second(h)
    merge_sum.add_last(sum_merge)
    for h in range(2):
        fine_sum.add_second(h)
    fine_sum.start_last()
    fine_sum.add_last(sum_fine)


def on_device(tokens, w_qkv, w_proj, w_merge, skip_grad, merged_grad, window_shift):
    vmem, smem = pltpu.VMEM, pltpu.SMEM
    inside = pl.BlockSpec(memory_space=vmem)
    outside = pl.BlockSpec(memory_space=pl.ANY)
    windows = 2 * ACROSS
    skip_out, merged_out, input_grad, sum_merge, sum_fine = pl.pallas_call(
        section_kernel,
        out_shape=[
            jax.ShapeDtypeStruct((CELLS, D), B16),
            jax.ShapeDtypeStruct((MERGED, D2), B16),
            jax.ShapeDtypeStruct((CELLS, D), B16),
            jax.ShapeDtypeStruct((64, 128), F32),
            jax.ShapeDtypeStruct((32, 128), F32),
        ],
        in_specs=[pl.BlockSpec(memory_space=smem)] + [inside] * 3 + [outside] * 3,
        out_specs=[inside] * 5,
        scratch_shapes=[
            vmem((D, 3 * D), B16),
            vmem((D, D), B16),
            vmem((4 * D, D2), B16),
            pltpu.SemaphoreType.DMA((3,)),
            vmem((SOURCES, D), B16),
            vmem((SOURCES, D), B16),
            vmem((2 * EDGE, D), B16),
            vmem((2 * EDGE, D), B16),
            vmem((CELLS, D), B16),
            pltpu.SemaphoreType.DMA((8,)),
            pltpu.SemaphoreType.DMA((8,)),
            pltpu.SemaphoreType.DMA((8,)),
            pltpu.SemaphoreType.DMA((8,)),
            vmem((BAND, 2 * CELLS + 4 * EDGE), B16),
            vmem((CELLS, 2 * BAND), B16),
            vmem((BAND, D), B16),
            vmem((2 * BAND, 3 * D), B16),
            vmem((windows, 4, 64, 256), F32),
            vmem((2 * BAND, D), B16),
            vmem((2 * BAND, D), B16),
            vmem((2 * BAND, 3 * D), B16),
            vmem((2 * CELLS, D), B16),
            vmem((2 * CELLS, YHI * ZS * 128), B16),
            vmem((MERGED, 4 * D), B16),
            vmem((CELLS, D), B16),
            vmem((XS, YLO, CORES, YHI, ZS, 64, 128), B16),
            vmem((XS, YLO, CORES, YHI, ZS, 32, 128), B16),
        ]
        + sum_scratch(64)
        + sum_scratch(32),
        compiler_params=pltpu.CompilerParams(
            collective_id=0, has_side_effects=True, vmem_limit_bytes=56 * 2**20
        ),
    )(
        window_shift,
        tokens.reshape(CELLS, D),
        skip_grad.reshape(CELLS, D),
        merged_grad.reshape(MERGED, D2),
        w_qkv,
        w_proj,
        w_merge,
    )
    return (
        skip_out.reshape(ROWS, COLS, D),
        merged_out.reshape(ROWS // 2, COLS // 2, D2),
        input_grad.reshape(ROWS, COLS, D),
        sum_fine[:, :96],
        sum_fine[:, 96:],
        sum_merge.T,
    )


def solution(mesh):
    in_specs = (
        P("lat", "lon", None),
        P(),
        P(),
        P(),
        P("lat", "lon", None),
        P("lat", "lon", None),
        P(),
    )
    out_specs = (
        P("lat", "lon", None),
        P("lat", "lon", None),
        P("lat", "lon", None),
        P("lon", "lat"),
        P("lon", "lat"),
        P("lon", "lat"),
    )
    return jax.shard_map(
        on_device, mesh=mesh, in_specs=in_specs, out_specs=out_specs, check_vma=False
    )
```

```python
import jax
import jax.numpy as jnp
from jax import lax
from jax.experimental import pallas as pl
from jax.experimental.pallas import tpu as pltpu
from jax.sharding import PartitionSpec as P

HEADS = 16
WIN = 8
EPSILON = 1e-05
NEGATIVE = -1e30
D = 512
D2 = 1024
ROWS, COLS = 8, 32
CELLS = ROWS * COLS
WINDOWS = COLS // WIN
FACTOR = 32 ** (-0.5)
MERGED = CELLS // 4
FRINGE = 384
F32, B16 = jnp.float32, jnp.bfloat16

XS, YLO, CORES, YHI, ZS = 4, 2, 2, 2, 8
YS = YLO * YHI
MESH = pl.DeviceIdType.MESH


class Place:
    def __init__(self):
        lon = lax.axis_index("lon")
        lat = lax.axis_index("lat")
        self.lon, self.lat = lon, lat
        self.core = lon % CORES
        self.ylo = (lon // CORES) % YLO
        self.x = lon // (CORES * YLO)
        self.z = lat % ZS
        self.yhi = lat // ZS

    def at(self, x=None, ylo=None, core=None, yhi=None, z=None):
        x = self.x if x is None else x
        ylo = self.ylo if ylo is None else ylo
        core = self.core if core is None else core
        yhi = self.yhi if yhi is None else yhi
        z = self.z if z is None else z
        return ((x * YLO + ylo) * CORES + core, yhi * ZS + z)

    def beside(self, dlat, dlon):
        lons, lats = XS * YLO * CORES, YHI * ZS
        return ((self.lon + dlon) % lons, (self.lat + dlat) % lats)

    def sibling(self):
        return self.at(core=1 - self.core)

    def x_step(self, k):
        return (self.x + k) % XS

    def y_step(self, k):
        y = (self.yhi * YLO + self.ylo + k) % YS
        return (y // YLO, y % YLO)

    def z_step(self, k):
        return (self.z + k) % ZS

    def core_step(self, f):
        return 1 - self.core if f else self.core

    def partners(self):
        out = [self.sibling()]
        for k in range(1, XS):
            out += [self.at(x=self.x_step(k), core=self.core_step(f)) for f in range(2)]
        for k in range(1, YS):
            yhi, ylo = self.y_step(k)
            out += [self.at(yhi=yhi, ylo=ylo, core=self.core_step(f)) for f in range(2)]
        out += [self.at(z=self.z_step(k)) for k in range(1, ZS)]
        for dlat in (-1, 0, 1):
            for dlon in (-1, 0, 1):
                if (dlat, dlon) != (0, 0):
                    out.append(self.beside(dlat, dlon))
        return out


def device_of(pair):
    return {"lon": pair[0], "lat": pair[1]}


def greet(partners):
    barrier = pltpu.get_barrier_semaphore()
    for pair in partners:
        pl.semaphore_signal(barrier, inc=1, device_id=device_of(pair), device_id_type=MESH)


def await_greetings(partners):
    pl.semaphore_wait(pltpu.get_barrier_semaphore(), len(partners))


HALF = ZS // 2


class Copies:
    def __init__(self, place, send, recv):
        self.place, self.send, self.recv = place, send, recv
        self.used = 0
        self.flying = {}

    def copy(self, src, dst, pair):
        slot = self.used
        self.used += 1
        made = pltpu.make_async_remote_copy(
            src_ref=src,
            dst_ref=dst,
            send_sem=self.send.at[slot],
            recv_sem=self.recv.at[slot],
            device_id=device_of(pair),
            device_id_type=MESH,
        )
        made.start()
        return made

    def wait(self, name):
        for made in self.flying[name]:
            made.wait()


def late_scratch(rows):
    copies = (XS - 1) + (YS - 1) + (ZS - 1)
    return [
        pltpu.VMEM((YLO, YHI, HALF, rows, 128), B16),
        pltpu.VMEM((XS, HALF, rows, 128), B16),
        pltpu.VMEM((YS - 1, HALF, rows, 128), B16),
        pltpu.VMEM((XS - 1, HALF, rows, 128), B16),
        pltpu.VMEM((ZS, rows, 128), B16),
        pltpu.VMEM((ZS - 1, rows, 128), B16),
        pltpu.SemaphoreType.DMA((copies,)),
        pltpu.SemaphoreType.DMA((copies,)),
    ]


def early_scratch(rows):
    copies = 2 + (XS - 1) + (YS - 1)
    return [
        pltpu.VMEM((XS, YLO, YHI, ZS, rows, 128), B16),
        pltpu.VMEM((XS - 1, YLO, YHI, HALF, rows, 128), B16),
        pltpu.VMEM((YS - 1, XS, HALF, rows, 128), B16),
        pltpu.SemaphoreType.DMA((copies,)),
        pltpu.SemaphoreType.DMA((copies,)),
    ]


class Late(Copies):
    def __init__(self, place, scratch):
        (self.sum_x, self.sum_y, self.late_y, self.late_x, self.column, self.from_z) = scratch[:6]
        super().__init__(place, *scratch[6:])

    def start_second(self, h):
        place = self.place
        if h == 0:
            self.flying["late_y"] = []
            for k in range(1, YS):
                yhi, ylo = place.y_step(k)
                self.flying["late_y"].append(
                    self.copy(
                        self.sum_x.at[ylo, yhi],
                        self.late_y.at[k - 1],
                        place.at(yhi=yhi, ylo=ylo),
                    )
                )
        else:
            self.flying["late_x"] = [
                self.copy(
                    self.sum_y.at[place.x_step(k)],
                    self.late_x.at[k - 1],
                    place.at(x=place.x_step(k)),
                )
                for k in range(1, XS)
            ]

    def add_second(self, h):
        place = self.place
        self.wait("late_y" if h == 0 else "late_x")
        if h == 0:
            total = self.sum_x[place.ylo, place.yhi].astype(F32)
            for k in range(YS - 1):
                total += self.late_y[k].astype(F32)
        else:
            total = self.sum_y[place.x].astype(F32)
            for k in range(XS - 1):
                total += self.late_x[k].astype(F32)
        self.column[pl.ds(h * HALF, HALF)] = total.astype(B16)

    def start_last(self):
        place = self.place
        self.flying["z"] = [
            self.copy(
                self.column.at[place.z_step(k)],
                self.from_z.at[k - 1],
                place.at(z=place.z_step(k)),
            )
            for k in range(1, ZS)
        ]

    def add_last(self, out):
        self.wait("z")
        total = self.column[self.place.z].astype(F32)
        for k in range(ZS - 1):
            total += self.from_z[k].astype(F32)
        out[...] = total


class Early(Copies):
    def __init__(self, place, parts, late, scratch):
        self.kept, self.from_x, self.from_y = scratch[:3]
        self.parts, self.late = parts, late
        super().__init__(place, *scratch[3:])

    def start_core(self):
        other = 1 - self.place.core
        self.flying["core"] = [
            self.copy(
                self.parts.at[:, :, other, :, pl.ds(h * HALF, HALF)],
                self.kept.at[:, :, :, pl.ds(h * HALF, HALF)],
                self.place.sibling(),
            )
            for h in range(2)
        ]

    def add_core(self, h):
        core = self.place.core
        self.flying["core"][h].wait()

        def body(i, carry):
            x, rest = i // (YLO * YHI), i % (YLO * YHI)
            ylo, yhi = rest // YHI, rest % YHI
            zs = pl.ds(h * HALF, HALF)
            own = self.parts[x, ylo, core, yhi, zs].astype(F32)
            got = self.kept[x, ylo, yhi, zs].astype(F32)
            self.kept[x, ylo, yhi, zs] = (own + got).astype(B16)
            return carry

        lax.fori_loop(0, XS * YLO * YHI, body, 0)

    def start_first(self, h):
        place = self.place
        zs = pl.ds(h * HALF, HALF)
        if h == 0:
            self.flying["x"] = [
                self.copy(
                    self.kept.at[place.x_step(k), :, :, zs],
                    self.from_x.at[k - 1],
                    place.at(x=place.x_step(k)),
                )
                for k in range(1, XS)
            ]
        else:
            self.flying["y"] = []
            for k in range(1, YS):
                yhi, ylo = place.y_step(k)
                self.flying["y"].append(
                    self.copy(
                        self.kept.at[:, ylo, yhi, zs],
                        self.from_y.at[k - 1],
                        place.at(yhi=yhi, ylo=ylo),
                    )
                )

    def add_first(self, h):
        place, late = self.place, self.late
        zs = pl.ds(h * HALF, HALF)
        self.wait("x" if h == 0 else "y")
        if h == 0:

            def body(i, carry):
                ylo, yhi = i // YHI, i % YHI
                total = self.kept[place.x, ylo, yhi, zs].astype(F32)
                for k in range(XS - 1):
                    total += self.from_x[k, ylo, yhi].astype(F32)
                late.sum_x[ylo, yhi] = total.astype(B16)
                return carry

            lax.fori_loop(0, YLO * YHI, body, 0)
        else:

            def body(x, carry):
                total = self.kept[x, place.ylo, place.yhi, zs].astype(F32)
                for k in range(YS - 1):
                    total += self.from_y[k, x].astype(F32)
                late.sum_y[x] = total.astype(B16)
                return carry

            lax.fori_loop(0, XS, body, 0)


def gather_scratch():
    copies = 4 * (2 * XS - 1)
    return [
        pltpu.VMEM((2 * XS, MERGED, D), B16),
        pltpu.VMEM((2 * YS, MERGED, D // 2), B16),
        pltpu.VMEM((2 * XS, MERGED, D // 2), B16),
        pltpu.VMEM((2 * YS, MERGED, D), B16),
        pltpu.VMEM((YHI, MERGED, D // 2), B16),
        pltpu.VMEM((XS, CORES, MERGED, D // 2), B16),
        pltpu.VMEM((YLO, CORES, MERGED, D), B16),
        pltpu.SemaphoreType.DMA((copies,)),
        pltpu.SemaphoreType.DMA((copies,)),
    ]


class Gather(Copies):
    def __init__(self, place, scratch):
        (self.grad_x, self.grad_y, self.hidden_x, self.hidden_y) = scratch[:4]
        (self.grad_parts, self.hidden_parts_x, self.hidden_parts_y) = scratch[4:7]
        super().__init__(place, *scratch[7:])

    def around(self):
        return [(k, f) for k in range(XS) for f in range(2) if (k, f) != (0, 0)]

    def start_grads(self, grads):
        place = self.place
        quarter = D // 2
        self.grad_x[0, :, 0:quarter] = grads[:, 0:quarter]
        self.grad_x[0, :, quarter:D] = grads[:, D : D + quarter]
        for yhi in range(YHI):
            start = yhi * D + quarter
            self.grad_parts[yhi] = grads[:, start : start + quarter]
        self.grad_y[0] = self.grad_parts[place.yhi]
        self.flying["grads"] = []
        for k, f in self.around():
            pair = place.at(x=place.x_step(k), core=place.core_step(f))
            self.flying["grads"].append(
                self.copy(self.grad_x.at[0], self.grad_x.at[2 * k + f], pair)
            )
            yhi, ylo = place.y_step(k)
            pair = place.at(yhi=yhi, ylo=ylo, core=place.core_step(f))
            self.flying["grads"].append(
                self.copy(self.grad_parts.at[yhi], self.grad_y.at[2 * k + f], pair)
            )

    def start_hidden(self, hidden):
        place = self.place
        for x in range(XS):
            for ylo in range(YLO):
                for core in range(CORES):
                    start = ((x * YLO + ylo) * CORES + core) * 128
                    block = hidden[:, start : start + 128]
                    self.hidden_parts_x[x, core, :, 128 * ylo : 128 * (ylo + 1)] = block
                    self.hidden_parts_y[ylo, core, :, 128 * x : 128 * (x + 1)] = block
        self.flying["hidden_x"], self.flying["hidden_y"] = [], []
        for k, f in self.around():
            core = place.core_step(f)
            yhi, ylo = place.y_step(k)
            self.flying["hidden_y"].append(
                self.copy(
                    self.hidden_parts_y.at[ylo, core],
                    self.hidden_y.at[2 * k + f],
                    place.at(yhi=yhi, ylo=ylo, core=core),
                )
            )
            x = place.x_step(k)
            self.flying["hidden_x"].append(
                self.copy(
                    self.hidden_parts_x.at[x, core],
                    self.hidden_x.at[2 * k + f],
                    place.at(x=x, core=core),
                )
            )
        self.hidden_x[0] = self.hidden_parts_x[place.x, place.core]
        self.hidden_y[0] = self.hidden_parts_y[place.ylo, place.core]

    def sum_x(self, grads_t, late):
        self.wait("hidden_x")
        hidden = self.hidden_x[...].reshape(2 * XS * MERGED, D // 2)
        block = dot(grads_t[...], hidden).astype(B16)
        for ylo in range(YLO):
            late.sum_x[ylo] = block[:, 128 * ylo : 128 * (ylo + 1)].reshape(YHI, HALF, 64, 128)

    def sum_y(self, grads_t, late):
        self.wait("hidden_y")
        hidden = self.hidden_y[...].reshape(2 * YS * MERGED, D)
        block = dot(grads_t[...], hidden).astype(B16)
        for x in range(XS):
            late.sum_y[x] = block[:, 128 * x : 128 * (x + 1)].reshape(HALF, 64, 128)


def iota(shape, dim):
    return lax.broadcasted_iota(jnp.int32, shape, dim)


def one_hot(rows, cols, index):
    place = index(iota((rows, 1), 0))
    return jnp.where(iota((rows, cols), 1) == place, 1.0, 0.0).astype(B16)


def dot(a, b):
    return jnp.dot(a, b, preferred_element_type=F32)


def dot_nt(a, b):
    return lax.dot_general(a, b, (((1,), (1,)), ((), ())), preferred_element_type=F32)


def dot_tn(a, b):
    return lax.dot_general(a, b, (((0,), (0,)), ((), ())), preferred_element_type=F32)


def rows_at(n):
    return n >> 5, n & 31


def rows_index(i, j):
    return i * COLS + j


def merge_at(n):
    part, r, c = n >> 6, (n >> 4) & 3, n & 15
    return 2 * r + (part & 1), 2 * c + (part >> 1)


def merge_index(i, j):
    return (((j & 1) * 2 + (i & 1)) << 6) + ((i >> 1) << 4) + (j >> 1)


def window_at(n):
    return (n >> 3) & 7, ((n >> 6) << 3) + (n & 7)


def window_index(i, j):
    return ((j >> 3) << 6) + (i << 3) + (j & 7)


def fringe_at(n):
    side = n < 256
    m = n & 31
    strip = n < 320
    corner = n & 15
    second = jnp.where(n < 352, 0, 1)
    i_side = ((n >> 5) & 3) + jnp.where(n < 128, 0, 4)
    i = jnp.where(side, i_side, jnp.where(strip, m >> 2, (corner >> 2) + 4 * second))
    last = jnp.where(strip, jnp.where(n >= 288, 1, 0), (n >> 4) & 1)
    j = jnp.where(side, m, (n & 3) + last * (COLS - 4))
    return i, j


def around_index(index, i, j):
    up, down, left, right = i < 0, i >= ROWS, j < 0, j >= COLS
    row4 = jnp.where(up, i + 4, jnp.where(down, i - ROWS, i))
    col4 = jnp.where(left, j + 4, j - COLS)
    north = up | down
    side = north & ~(left | right)
    strip = (left | right) & ~north
    corner = north & (left | right)
    at = index(i, j)
    at = jnp.where(side, CELLS + jnp.where(up, 128, 0) + row4 * COLS + j, at)
    at = jnp.where(strip, CELLS + 256 + jnp.where(left, 32, 0) + row4 * 4 + col4, at)
    base = CELLS + 320 + jnp.where(up, 32, 0) + jnp.where(left, 16, 0)
    return jnp.where(corner, base + row4 * 4 + col4, at)


def normalize(values):
    center = values - jnp.mean(values, axis=-1, keepdims=True)
    inverse = lax.rsqrt(jnp.mean(center * center, axis=-1, keepdims=True) + EPSILON)
    return center * inverse, inverse


FRINGES = (
    (0, 128, -1, 0),
    (128, 128, 1, 0),
    (256, 32, 0, -1),
    (288, 32, 0, 1),
    (320, 16, -1, -1),
    (336, 16, -1, 1),
    (352, 16, 1, -1),
    (368, 16, 1, 1),
)


def around_scratch():
    return [
        pltpu.VMEM((CELLS + FRINGE, D), B16),
        pltpu.VMEM((FRINGE, D), B16),
        pltpu.SemaphoreType.DMA((len(FRINGES),)),
        pltpu.SemaphoreType.DMA((len(FRINGES),)),
    ]


class Around(Copies):
    def __init__(self, place, scratch):
        self.block, self.fringe = scratch[:2]
        super().__init__(place, *scratch[2:])

    def pick(self, values, picks):
        self.fringe[...] = dot(picks, values).astype(B16)

    def start(self, values):
        self.flying["fringe"] = [
            self.copy(
                self.fringe.at[pl.ds(offset, size)],
                self.block.at[pl.ds(CELLS + offset, size)],
                self.place.beside(dlat, dlon),
            )
            for offset, size, dlat, dlon in FRINGES
        ]
        self.block[pl.ds(0, CELLS)] = values

    def get(self, picks):
        self.wait("fringe")
        return dot(picks, self.block[...])


def section_kernel(
    shift,
    tokens,
    skip_grad,
    merged_grad,
    w_qkv_hbm,
    w_proj_hbm,
    w_merge_hbm,
    skip_out,
    merged_out,
    input_grad,
    sum_merge,
    sum_fine,
    w_qkv,
    w_proj,
    w_merge,
    load,
    to_back,
    to_windows,
    to_output,
    pick_window,
    pick_merge,
    normed,
    packed,
    probs,
    attended,
    window_total,
    packed_grad,
    both_t,
    spread,
    merged_hidden,
    total_grad,
    grads_x_t,
    grads_y_t,
    parts_fine,
    *scratch,
):
    place = Place()
    partners = place.partners()
    greet(partners)
    loads = [
        pltpu.make_async_copy(src, dst, load.at[n])
        for n, (src, dst) in enumerate(
            ((w_qkv_hbm, w_qkv), (w_proj_hbm, w_proj), (w_merge_hbm, w_merge))
        )
    ]
    for made in loads:
        made.start()
    rounds = [Around(place, scratch[4 * n : 4 * n + 4]) for n in range(4)]
    scratch = scratch[16:]
    factors = Gather(place, scratch[:9])
    merge_sum = Late(place, scratch[9:17])
    fine_late = Late(place, scratch[17:25])
    fine_sum = Early(place, parts_fine, fine_late, scratch[25:])

    a, b = shift[0], shift[1]
    down = jnp.where(a >= WIN // 2, a - WIN, a)
    right = jnp.where(b >= WIN // 2, b - WIN, b)

    def picker(index):
        return one_hot(FRINGE, CELLS, lambda n: index(*fringe_at(n)))

    def shifted(at, index, sign):
        def source(n):
            i, j = at(n)
            return around_index(index, i + sign * down, j + sign * right)

        return one_hot(CELLS, CELLS + FRINGE, source)

    rounds[0].pick(tokens[...], picker(rows_index))
    from_tokens = shifted(window_at, rows_index, 1)
    await_greetings(partners)
    rounds[0].start(tokens[...])
    factors.start_grads(merged_grad)

    to_back[...] = shifted(merge_at, window_index, -1)
    to_windows[...] = shifted(window_at, merge_index, 1)
    to_output[...] = shifted(rows_at, window_index, -1)
    pick_window[...] = picker(window_index)
    pick_merge[...] = picker(merge_index)
    to_merged = one_hot(CELLS, CELLS, lambda n: rows_index(*merge_at(n)))
    to_rows = one_hot(CELLS, CELLS, lambda n: merge_index(*rows_at(n)))
    own_tokens = dot(to_merged, tokens[...])
    own_skip = dot(to_merged, skip_grad[...])
    loads[0].wait()

    values, inverse = normalize(rounds[0].get(from_tokens))
    normed[...] = values
    hidden = values.astype(B16)
    for n in range(3):
        columns = pl.ds(D * n, D)
        packed[:, columns] = dot(hidden, w_qkv[:, columns]).astype(B16)

    head_mask = (iota((4 * 64, 128), 0) >> 6) == (iota((4 * 64, 128), 1) >> 5)
    head_one = jnp.where(head_mask, 1.0, 0.0)
    head_b16 = head_one.astype(B16)

    def expand(values):
        return jnp.concatenate([values] * 4, axis=0) * head_b16

    def fold(values):
        kept = values * head_one
        return (kept[0:64] + kept[64:128]) + (kept[128:192] + kept[192:256])

    def lanes(n, g):
        return pl.ds(D * n + 128 * g, 128)

    key_row = down + ((iota((64, 1), 0) >> 3) & 7)
    query_row = down + ((iota((1, 256), 1) >> 3) & 7)
    key_away = (key_row < 0) | (key_row >= ROWS)
    query_away = (query_row < 0) | (query_row >= ROWS)
    pole = place.lat == jnp.where(a >= WIN // 2, 0, YHI * ZS - 1)
    apart = jnp.where(key_away, 1, 0) != jnp.where(query_away, 1, 0)
    bias = jnp.where(apart, jnp.where(pole, NEGATIVE, 0.0), 0.0)

    def forward(w, carry):
        rows = pl.ds(pl.multiple_of(w * 64, 64), 64)
        for g in range(4):
            queries = expand(packed[rows, lanes(0, g)])
            scores = dot_nt(packed[rows, lanes(1, g)], queries) * FACTOR + bias
            raised = jnp.exp(scores - jnp.max(scores, axis=0, keepdims=True))
            prob = raised * (1.0 / jnp.sum(raised, axis=0, keepdims=True))
            probs[w, g] = prob
            output = dot_tn(prob.astype(B16), packed[rows, lanes(2, g)])
            attended[rows, pl.ds(128 * g, 128)] = fold(output).astype(B16)
        return carry

    lax.fori_loop(0, WINDOWS, forward, 0)
    rounds[1].pick(attended[...], pick_window[...])
    rounds[1].start(attended[...])

    loads[1].wait()
    loads[2].wait()
    merged_back = [
        dot_nt(merged_grad[...], w_merge[pl.ds(D * part, D)]) for part in range(4)
    ]
    both_t[:, pl.ds(0, CELLS)] = hidden.T
    both_t[:, pl.ds(CELLS, CELLS)] = attended[...].T
    factors.wait("grads")
    grads_x_t[...] = factors.grad_x[...].reshape(2 * XS * MERGED, D).T
    grads_y_t[...] = factors.grad_y[...].reshape(2 * YS * MERGED, D // 2).T

    own_attended = rounds[1].get(to_back[...]).astype(B16)
    own_out = (own_tokens + dot(own_attended, w_proj[...])).astype(B16)
    merged_in = own_out.astype(F32)
    quarters = [merged_in[MERGED * n : MERGED * (n + 1)] for n in range(4)]
    wide = 1.0 / (4 * D)

    def mean(values):
        return sum(jnp.sum(v, axis=-1, keepdims=True) for v in values) * wide

    center_at = mean(quarters)
    centers = [q - center_at for q in quarters]
    merged_inverse = lax.rsqrt(mean([c * c for c in centers]) + EPSILON)
    merged_normed = [c * merged_inverse for c in centers]
    back_mean = mean(merged_back)
    back_dot = mean([g * n for g, n in zip(merged_back, merged_normed)])
    for n in range(4):
        rows = pl.ds(MERGED * n, MERGED)
        merged_hidden[:, pl.ds(D * n, D)] = merged_normed[n].astype(B16)
        delta = merged_inverse * (merged_back[n] - back_mean - merged_normed[n] * back_dot)
        total_grad[rows] = (own_skip[MERGED * n : MERGED * (n + 1)] + delta).astype(B16)
    rounds[2].pick(total_grad[...], pick_merge[...])
    rounds[2].start(total_grad[...])
    factors.start_hidden(merged_hidden)

    skip_out[...] = dot(to_rows, own_out).astype(B16)
    merged_out[...] = dot(merged_hidden[...], w_merge[...]).astype(B16)

    window_total[...] = rounds[2].get(to_windows[...]).astype(B16)
    attended[...] = dot_nt(window_total[...], w_proj[...]).astype(B16)

    def backward(w, carry):
        rows = pl.ds(pl.multiple_of(w * 64, 64), 64)
        for g in range(4):
            queries = expand(packed[rows, lanes(0, g)])
            upstream = expand(attended[rows, pl.ds(128 * g, 128)])
            key_rows, value_rows = packed[rows, lanes(1, g)], packed[rows, lanes(2, g)]
            prob = probs[w, g]
            prob_grad = dot_nt(value_rows, upstream)
            total = jnp.sum(prob * prob_grad, axis=0, keepdims=True)
            score_grad = (prob * (prob_grad - total) * FACTOR).astype(B16)
            packed_grad[rows, lanes(0, g)] = fold(dot_tn(score_grad, key_rows)).astype(B16)
            packed_grad[rows, lanes(1, g)] = dot(score_grad, queries).astype(B16)
            packed_grad[rows, lanes(2, g)] = dot(prob.astype(B16), upstream).astype(B16)
        return carry

    lax.fori_loop(0, WINDOWS // 2, backward, 0)
    factors.sum_x(grads_x_t, merge_sum)
    merge_sum.start_second(0)
    factors.sum_y(grads_y_t, merge_sum)
    merge_sum.start_second(1)
    lax.fori_loop(WINDOWS // 2, WINDOWS, backward, 0)

    widen_fine = one_hot(384, 512, lambda n: (n // 96) * 128 + n % 96)
    widen_proj = one_hot(128, 512, lambda n: (n >> 5) * 128 + 96 + (n & 31))
    for n in range(4):
        columns = pl.ds(512 * n, 512)
        spread[pl.ds(0, CELLS), columns] = dot(
            packed_grad[:, pl.ds(384 * n, 384)], widen_fine
        ).astype(B16)
        spread[pl.ds(CELLS, CELLS), columns] = dot(
            window_total[:, pl.ds(128 * n, 128)], widen_proj
        ).astype(B16)
    for r in range(YHI * ZS // 4):
        block = dot(both_t[...], spread[:, pl.ds(512 * r, 512)]).astype(B16)
        for m in range(4):
            lat = 4 * r + m
            parts_fine[:, :, :, lat // ZS, lat % ZS] = block[:, 128 * m : 128 * (m + 1)].reshape(
                XS, YLO, CORES, 32, 128
            )
    fine_sum.start_core()
    merge_sum.add_second(0)
    merge_sum.add_second(1)
    merge_sum.start_last()
    for h in range(2):
        fine_sum.add_core(h)
        fine_sum.start_first(h)

    hidden_grad = dot_nt(packed_grad[...], w_qkv[...])
    window_input = window_total[...].astype(F32) + inverse * (
        hidden_grad
        - jnp.mean(hidden_grad, axis=-1, keepdims=True)
        - normed[...] * jnp.mean(hidden_grad * normed[...], axis=-1, keepdims=True)
    )
    window_input = window_input.astype(B16)
    rounds[3].pick(window_input, pick_window[...])
    rounds[3].start(window_input)

    for h in range(2):
        fine_sum.add_first(h)
        fine_late.start_second(h)
    merge_sum.add_last(sum_merge)
    for h in range(2):
        fine_late.add_second(h)
    fine_late.start_last()
    input_grad[...] = rounds[3].get(to_output[...]).astype(B16)
    fine_late.add_last(sum_fine)


def finish_kernel(sum_merge, sum_fine, *refs):
    for src, dst in zip(refs[:3], refs[3:6]):
        dst[...] = src[...]
    dw_qkv, dw_proj, dw_merge = refs[6:]
    dw_qkv[...] = sum_fine[:, 0:96]
    dw_proj[...] = sum_fine[:, 96:128]
    dw_merge[...] = sum_merge[...]


def on_device(tokens, w_qkv, w_proj, w_merge, skip_grad, merged_grad, window_shift):
    vmem, smem = pltpu.VMEM, pltpu.SMEM
    inside = pl.BlockSpec(memory_space=vmem)
    outside = pl.BlockSpec(memory_space=pl.ANY)
    shape = jax.ShapeDtypeStruct
    big = [shape((CELLS, D), B16), shape((MERGED, D2), B16), shape((CELLS, D), B16)]
    skip_out, merged_out, input_grad, sum_merge, sum_fine = pl.pallas_call(
        section_kernel,
        out_shape=big + [shape((64, 128), F32), shape((32, 128), F32)],
        in_specs=[pl.BlockSpec(memory_space=smem)] + [inside] * 3 + [outside] * 3,
        out_specs=[inside] * 5,
        scratch_shapes=[
            vmem((D, 3 * D), B16),
            vmem((D, D), B16),
            vmem((4 * D, D2), B16),
            pltpu.SemaphoreType.DMA((3,)),
            vmem((CELLS, CELLS + FRINGE), B16),
            vmem((CELLS, CELLS + FRINGE), B16),
            vmem((CELLS, CELLS + FRINGE), B16),
            vmem((FRINGE, CELLS), B16),
            vmem((FRINGE, CELLS), B16),
            vmem((CELLS, D), F32),
            vmem((CELLS, 3 * D), B16),
            vmem((WINDOWS, 4, 64, 256), F32),
            vmem((CELLS, D), B16),
            vmem((CELLS, D), B16),
            vmem((CELLS, 3 * D), B16),
            vmem((D, 2 * CELLS), B16),
            vmem((2 * CELLS, YHI * ZS * 128), B16),
            vmem((MERGED, 4 * D), B16),
            vmem((CELLS, D), B16),
            vmem((D, 2 * XS * MERGED), B16),
            vmem((D // 2, 2 * YS * MERGED), B16),
            vmem((XS, YLO, CORES, YHI, ZS, 32, 128), B16),
        ]
        + around_scratch() * 4
        + gather_scratch()
        + late_scratch(64)
        + late_scratch(32)
        + early_scratch(32),
        compiler_params=pltpu.CompilerParams(
            collective_id=0, has_side_effects=True, vmem_limit_bytes=56 * 2**20
        ),
    )(
        window_shift,
        tokens.reshape(CELLS, D),
        skip_grad.reshape(CELLS, D),
        merged_grad.reshape(MERGED, D2),
        w_qkv,
        w_proj,
        w_merge,
    )
    skip_out, merged_out, input_grad, dw_qkv, dw_proj, dw_merge = pl.pallas_call(
        finish_kernel,
        out_shape=big + [shape((32, 96), F32), shape((32, 32), F32), shape((64, 128), F32)],
        in_specs=[inside] * 5,
        out_specs=[inside] * 6,
    )(sum_merge, sum_fine, skip_out, merged_out, input_grad)
    return (
        skip_out.reshape(ROWS, COLS, D),
        merged_out.reshape(ROWS // 2, COLS // 2, D2),
        input_grad.reshape(ROWS, COLS, D),
        dw_qkv,
        dw_proj,
        dw_merge.T,
    )


def solution(mesh):
    in_specs = (
        P("lat", "lon", None),
        P(),
        P(),
        P(),
        P("lat", "lon", None),
        P("lat", "lon", None),
        P(),
    )
    out_specs = (
        P("lat", "lon", None),
        P("lat", "lon", None),
        P("lat", "lon", None),
        P("lon", "lat"),
        P("lon", "lat"),
        P("lon", "lat"),
    )
    return jax.shard_map(
        on_device, mesh=mesh, in_specs=in_specs, out_specs=out_specs, check_vma=False
    )
```

```python
import functools

import jax
import jax.numpy as jnp
from jax import lax
from jax.experimental import pallas as pl
from jax.experimental.pallas import tpu as pltpu
from jax.sharding import PartitionSpec as P

HEADS = 16
WIN = 8
EPSILON = 1e-05
NEGATIVE = -1e30
D = 512
D2 = 1024
ROWS, COLS = 8, 32
CELLS = ROWS * COLS
WINDOWS = COLS // WIN
FACTOR = 32 ** (-0.5)
MERGED = CELLS // 4
F32, B16 = jnp.float32, jnp.bfloat16

XS, YLO, CORES, YHI, ZS = 4, 2, 2, 2, 8
YS = YLO * YHI
MESH = pl.DeviceIdType.MESH


class Place:
    def __init__(self):
        lon = lax.axis_index("lon")
        lat = lax.axis_index("lat")
        self.lon, self.lat = lon, lat
        self.core = lon % CORES
        self.ylo = (lon // CORES) % YLO
        self.x = lon // (CORES * YLO)
        self.z = lat % ZS
        self.yhi = lat // ZS

    def at(self, x=None, ylo=None, core=None, yhi=None, z=None):
        x = self.x if x is None else x
        ylo = self.ylo if ylo is None else ylo
        core = self.core if core is None else core
        yhi = self.yhi if yhi is None else yhi
        z = self.z if z is None else z
        return ((x * YLO + ylo) * CORES + core, yhi * ZS + z)

    def beside(self, dlat, dlon):
        lons, lats = XS * YLO * CORES, YHI * ZS
        return ((self.lon + dlon) % lons, (self.lat + dlat) % lats)

    def sibling(self):
        return self.at(core=1 - self.core)

    def x_step(self, k):
        return (self.x + k) % XS

    def y_step(self, k):
        y = (self.yhi * YLO + self.ylo + k) % YS
        return (y // YLO, y % YLO)

    def z_step(self, k):
        return (self.z + k) % ZS

    def core_step(self, f):
        return 1 - self.core if f else self.core

    def partners(self):
        out = [self.sibling()]
        for k in range(1, XS):
            out += [self.at(x=self.x_step(k), core=self.core_step(f)) for f in range(2)]
        for k in range(1, YS):
            yhi, ylo = self.y_step(k)
            out += [self.at(yhi=yhi, ylo=ylo, core=self.core_step(f)) for f in range(2)]
        out += [self.at(z=self.z_step(k)) for k in range(1, ZS)]
        for dlat in (-1, 0, 1):
            for dlon in (-1, 0, 1):
                if (dlat, dlon) != (0, 0):
                    out.append(self.beside(dlat, dlon))
        return out


def device_of(pair):
    return {"lon": pair[0], "lat": pair[1]}


def greet(partners):
    barrier = pltpu.get_barrier_semaphore()
    for pair in partners:
        pl.semaphore_signal(barrier, inc=1, device_id=device_of(pair), device_id_type=MESH)


def await_greetings(partners):
    pl.semaphore_wait(pltpu.get_barrier_semaphore(), len(partners))


HALF = ZS // 2


class Copies:
    def __init__(self, place, send, recv):
        self.place, self.send, self.recv = place, send, recv
        self.used = 0
        self.flying = {}

    def copy(self, src, dst, pair):
        slot = self.used
        self.used += 1
        made = pltpu.make_async_remote_copy(
            src_ref=src,
            dst_ref=dst,
            send_sem=self.send.at[slot],
            recv_sem=self.recv.at[slot],
            device_id=device_of(pair),
            device_id_type=MESH,
        )
        made.start()
        return made

    def wait(self, name):
        for made in self.flying[name]:
            made.wait()


def path_scratch(rows, first, second):
    one, two = first[0], second
    flat = 1
    for size in two:
        flat *= size
    copies = (first[1] - 1) + (flat - 1)
    out = [
        pltpu.VMEM((*two, rows, 128), B16),
        pltpu.VMEM((flat - 1, rows, 128), B16),
        pltpu.SemaphoreType.DMA((copies,)),
        pltpu.SemaphoreType.DMA((copies,)),
    ]
    if one:
        out += [
            pltpu.VMEM((XS, YLO, YHI, rows, 128), B16),
            pltpu.VMEM((first[1] - 1, *two, rows, 128), B16),
        ]
    return out


class PathXY(Copies):
    def __init__(self, place, scratch):
        self.sum, self.late = scratch[:2]
        super().__init__(place, *scratch[2:4])
        if len(scratch) > 4:
            self.parts, self.got = scratch[4:]

    def start_first(self):
        place = self.place
        self.flying["x"] = [
            self.copy(
                self.parts.at[place.x_step(k)], self.got.at[k - 1], place.at(x=place.x_step(k))
            )
            for k in range(1, XS)
        ]

    def add_first(self):
        self.wait("x")
        for ylo in range(YLO):
            for yhi in range(YHI):
                total = self.parts[self.place.x, ylo, yhi].astype(F32)
                for k in range(XS - 1):
                    total += self.got[k, ylo, yhi].astype(F32)
                self.sum[ylo, yhi] = total.astype(B16)

    def start_second(self):
        self.flying["y"] = []
        for k in range(1, YS):
            yhi, ylo = self.place.y_step(k)
            pair = self.place.at(yhi=yhi, ylo=ylo)
            self.flying["y"].append(self.copy(self.sum.at[ylo, yhi], self.late.at[k - 1], pair))

    def add_second(self):
        self.wait("y")
        total = self.sum[self.place.ylo, self.place.yhi].astype(F32)
        for k in range(YS - 1):
            total += self.late[k].astype(F32)
        return total.astype(B16)


class PathYX(Copies):
    def __init__(self, place, scratch):
        self.sum, self.late = scratch[:2]
        super().__init__(place, *scratch[2:4])
        self.parts, self.got = scratch[4:]

    def start_first(self):
        self.flying["y"] = []
        for k in range(1, YS):
            yhi, ylo = self.place.y_step(k)
            pair = self.place.at(yhi=yhi, ylo=ylo)
            self.flying["y"].append(
                self.copy(self.parts.at[:, ylo, yhi], self.got.at[k - 1], pair)
            )

    def add_first(self):
        self.wait("y")
        for x in range(XS):
            total = self.parts[x, self.place.ylo, self.place.yhi].astype(F32)
            for k in range(YS - 1):
                total += self.got[k, x].astype(F32)
            self.sum[x] = total.astype(B16)

    def start_second(self):
        place = self.place
        self.flying["x"] = [
            self.copy(
                self.sum.at[place.x_step(k)], self.late.at[k - 1], place.at(x=place.x_step(k))
            )
            for k in range(1, XS)
        ]

    def add_second(self):
        self.wait("x")
        total = self.sum[self.place.x].astype(F32)
        for k in range(XS - 1):
            total += self.late[k].astype(F32)
        return total.astype(B16)


def last_scratch(rows):
    return [
        pltpu.VMEM((ZS, rows, 128), B16),
        pltpu.VMEM((ZS - 1, rows, 128), B16),
        pltpu.SemaphoreType.DMA((ZS - 1,)),
        pltpu.SemaphoreType.DMA((ZS - 1,)),
    ]


class Last(Copies):
    def __init__(self, place, scratch):
        self.column, self.from_z = scratch[:2]
        super().__init__(place, *scratch[2:])

    def start(self):
        place = self.place
        self.flying["z"] = [
            self.copy(
                self.column.at[place.z_step(k)],
                self.from_z.at[k - 1],
                place.at(z=place.z_step(k)),
            )
            for k in range(1, ZS)
        ]

    def add(self, out):
        self.wait("z")
        total = self.column[self.place.z].astype(F32)
        for k in range(ZS - 1):
            total += self.from_z[k].astype(F32)
        out[...] = total


def share_scratch():
    half = D // 2
    return [
        pltpu.VMEM((2, half, CELLS), B16),
        pltpu.VMEM((2, half, CELLS), B16),
        pltpu.VMEM((2, half, CELLS), B16),
        pltpu.VMEM((CELLS, D), B16),
        pltpu.VMEM((CELLS, 3 * D), B16),
        pltpu.SemaphoreType.DMA((5,)),
        pltpu.SemaphoreType.DMA((5,)),
    ]


class Share(Copies):
    def __init__(self, place, scratch):
        self.out, self.hidden, self.attended, self.total, self.packed = scratch[:5]
        super().__init__(place, *scratch[5:])

    def give(self, name, src, dst):
        self.flying.setdefault(name, []).append(self.copy(src, dst, self.place.sibling()))

    def give_features(self, name, slot, values, kept):
        core, half = self.place.core, D // 2

        def feature(n):
            m = n & (half - 1)
            owner = jnp.where(n < half, core, 1 - core)
            return ((m >> 5) * CORES + owner) * 32 + (m & 31)

        moved = dot_nt(one_hot(D, D, feature), values).astype(B16)
        kept[0] = moved[0:half]
        self.out[slot] = moved[half:D]
        self.give(name, self.out.at[slot], kept.at[1])


def gather_scratch():
    copies = 2 * (2 * XS - 1)
    return [
        pltpu.VMEM((2 * XS, MERGED, D2), B16),
        pltpu.VMEM((2 * XS, MERGED, D // 2), B16),
        pltpu.VMEM((XS, CORES, MERGED, D // 2), B16),
        pltpu.SemaphoreType.DMA((copies,)),
        pltpu.SemaphoreType.DMA((copies,)),
    ]


class Gather(Copies):
    def __init__(self, place, scratch):
        self.grad, self.hidden, self.hidden_parts = scratch[:3]
        super().__init__(place, *scratch[3:])

    def around(self):
        return [(k, f) for k in range(XS) for f in range(2) if (k, f) != (0, 0)]

    def start_grads(self):
        place = self.place
        self.flying["grads"] = []
        for k, f in self.around():
            pair = place.at(x=place.x_step(k), core=place.core_step(f))
            self.flying["grads"].append(
                self.copy(self.grad.at[0], self.grad.at[2 * k + f], pair)
            )

    def start_hidden(self, hidden):
        place = self.place
        for x in range(XS):
            for ylo in range(YLO):
                for core in range(CORES):
                    start = ((x * YLO + ylo) * CORES + core) * 128
                    self.hidden_parts[x, core, :, 128 * ylo : 128 * (ylo + 1)] = hidden[
                        :, start : start + 128
                    ]
        self.flying["hidden"] = []
        for k, f in self.around():
            x, core = place.x_step(k), place.core_step(f)
            self.flying["hidden"].append(
                self.copy(
                    self.hidden_parts.at[x, core],
                    self.hidden.at[2 * k + f],
                    place.at(x=x, core=core),
                )
            )
        self.hidden[0] = self.hidden_parts[place.x, place.core]

    def form(self, grads_t, path):
        self.wait("hidden")
        hidden = self.hidden[...].reshape(2 * XS * MERGED, D // 2)
        for yhi in range(YHI):
            block = dot(grads_t[pl.ds(D * yhi, D)], hidden).astype(B16)
            for ylo in range(YLO):
                path.sum[ylo, yhi] = block[:, 128 * ylo : 128 * (ylo + 1)]


def iota(shape, dim):
    return lax.broadcasted_iota(jnp.int32, shape, dim)


def one_hot(rows, cols, index):
    place = index(iota((rows, 1), 0))
    return jnp.where(iota((rows, cols), 1) == place, 1.0, 0.0).astype(B16)


def dot(a, b):
    return jnp.dot(a, b, preferred_element_type=F32)


def dot_nt(a, b):
    return lax.dot_general(a, b, (((1,), (1,)), ((), ())), preferred_element_type=F32)


def dot_tn(a, b):
    return lax.dot_general(a, b, (((0,), (0,)), ((), ())), preferred_element_type=F32)


def rows_at(n):
    return n >> 5, n & 31


def rows_index(i, j):
    return i * COLS + j


def merge_at(n):
    part, r, c = n >> 6, (n >> 4) & 3, n & 15
    return 2 * r + (part & 1), 2 * c + (part >> 1)


def merge_index(i, j):
    return (((j & 1) * 2 + (i & 1)) << 6) + ((i >> 1) << 4) + (j >> 1)


def window_at(n):
    return (n >> 3) & 7, ((n >> 6) << 3) + (n & 7)


def window_index(i, j):
    return ((j >> 3) << 6) + (i << 3) + (j & 7)


def fringe_at(n, deep):
    side = n < 64 * deep
    strip = n < 64 * deep + 64
    m = n & 31
    i_side = (n >> 5) + jnp.where(n < 32 * deep, 0, ROWS - 2 * deep)
    i = jnp.where(side, i_side, jnp.where(strip, m >> 2, ((n & 15) >> 2) + 4 * ((n >> 5) & 1)))
    last = jnp.where(strip, (n >> 5) & 1, (n >> 4) & 1)
    j = jnp.where(side, m, (n & 3) + last * (COLS - 4))
    return i, j


def around_index(index, i, j, deep):
    up, down, left, right = i < 0, i >= ROWS, j < 0, j >= COLS
    col4 = jnp.where(left, j + 4, j - COLS)
    north = up | down
    side = north & ~(left | right)
    strip = (left | right) & ~north
    corner = north & (left | right)
    at = index(i, j)
    row = jnp.where(up, i + 2 * deep, i - ROWS)
    at = jnp.where(side, CELLS + row * COLS + j, at)
    at = jnp.where(strip, CELLS + 64 * deep + jnp.where(left, 32, 0) + i * 4 + col4, at)
    base = CELLS + 64 * deep + 64 + jnp.where(up, 32, 0) + jnp.where(left, 16, 0)
    row4 = jnp.where(up, i + 4, i - ROWS)
    return jnp.where(corner, base + row4 * 4 + col4, at)


def normalize(values):
    center = values - jnp.mean(values, axis=-1, keepdims=True)
    inverse = lax.rsqrt(jnp.mean(center * center, axis=-1, keepdims=True) + EPSILON)
    return center * inverse, inverse


def fringe_size(deep):
    return 64 * deep + 128


def fringes(deep):
    rows, base = 32 * deep, 64 * deep
    return (
        (0, rows, -1, 0),
        (rows, rows, 1, 0),
        (base, 32, 0, -1),
        (base + 32, 32, 0, 1),
        (base + 64, 16, -1, -1),
        (base + 80, 16, -1, 1),
        (base + 96, 16, 1, -1),
        (base + 112, 16, 1, 1),
    )


def around_scratch(deep):
    return [
        pltpu.VMEM((CELLS + fringe_size(deep), D), B16),
        pltpu.VMEM((fringe_size(deep), D), B16),
        pltpu.SemaphoreType.DMA((8,)),
        pltpu.SemaphoreType.DMA((8,)),
    ]


class Around(Copies):
    def __init__(self, place, deep, scratch):
        self.block, self.fringe = scratch[:2]
        self.deep = deep
        super().__init__(place, *scratch[2:])

    def pick(self, values, picks):
        self.fringe[...] = dot(picks, values).astype(B16)

    def start(self, values):
        self.flying["fringe"] = [
            self.copy(
                self.fringe.at[pl.ds(offset, size)],
                self.block.at[pl.ds(CELLS + offset, size)],
                self.place.beside(dlat, dlon),
            )
            for offset, size, dlat, dlon in fringes(self.deep)
        ]
        self.block[pl.ds(0, CELLS)] = values

    def get(self, picks):
        self.wait("fringe")
        return dot(picks, self.block[...])


def section_kernel(
    deep,
    shift,
    tokens_hbm,
    skip_grad_hbm,
    merged_grad_hbm,
    w_qkv_hbm,
    w_proj_hbm,
    w_merge_hbm,
    skip_out,
    merged_out,
    input_grad,
    sum_merge,
    sum_fine,
    tokens,
    skip_grad,
    w_qkv,
    w_proj,
    w_merge,
    load,
    to_back,
    to_windows,
    to_output,
    pick_window,
    pick_merge,
    normed,
    packed,
    probs,
    attended,
    window_total,
    packed_grad,
    merged_hidden,
    total_grad,
    grads_t,
    *scratch,
):
    place = Place()
    partners = place.partners()
    greet(partners)
    rounds = [Around(place, deep, scratch[4 * n : 4 * n + 4]) for n in range(4)]
    scratch = scratch[16:]
    factors = Gather(place, scratch[:5])
    merge_sum = PathXY(place, scratch[5:9])
    proj_sum = PathXY(place, scratch[9:15])
    qkv_sums = PathXY(place, scratch[15:21]), PathYX(place, scratch[21:27])
    merge_last = Last(place, scratch[27:31])
    fine_last = Last(place, scratch[31:35])
    share = Share(place, scratch[35:42])
    merged_grad = factors.grad.at[0]
    loads = {}
    for n, (name, src, dst) in enumerate(
        (
            ("tokens", tokens_hbm, tokens),
            ("merged_grad", merged_grad_hbm, merged_grad),
            ("w_qkv", w_qkv_hbm, w_qkv),
            ("skip_grad", skip_grad_hbm, skip_grad),
            ("w_proj", w_proj_hbm, w_proj),
            ("w_merge", w_merge_hbm, w_merge),
        )
    ):
        loads[name] = pltpu.make_async_copy(src, dst, load.at[n])
        loads[name].start()

    a, b = shift[0], shift[1]
    down = jnp.where(a >= WIN // 2, a - WIN, a)
    right = jnp.where(b >= WIN // 2, b - WIN, b)

    def picker(index):
        return one_hot(fringe_size(deep), CELLS, lambda n: index(*fringe_at(n, deep)))

    def shifted(at, index, sign):
        def source(n):
            i, j = at(n)
            return around_index(index, i + sign * down, j + sign * right, deep)

        return one_hot(CELLS, CELLS + fringe_size(deep), source)

    from_tokens = shifted(window_at, rows_index, 1)
    pick_tokens = picker(rows_index)
    loads["tokens"].wait()
    rounds[0].pick(tokens[...], pick_tokens)
    await_greetings(partners)
    rounds[0].start(tokens[...])
    loads["merged_grad"].wait()
    factors.start_grads()

    to_back[...] = shifted(merge_at, window_index, -1)
    to_windows[...] = shifted(window_at, merge_index, 1)
    to_output[...] = shifted(rows_at, window_index, -1)
    pick_window[...] = picker(window_index)
    pick_merge[...] = picker(merge_index)
    to_merged = one_hot(CELLS, CELLS, lambda n: rows_index(*merge_at(n)))
    to_rows = one_hot(CELLS, CELLS, lambda n: merge_index(*rows_at(n)))
    own_tokens = dot(to_merged, tokens[...])
    loads["skip_grad"].wait()
    own_skip = dot(to_merged, skip_grad[...])
    loads["w_qkv"].wait()

    values, inverse = normalize(rounds[0].get(from_tokens))
    normed[...] = values
    hidden = values.astype(B16)
    for n in range(3):
        columns = pl.ds(D * n, D)
        packed[:, columns] = dot(hidden, w_qkv[:, columns]).astype(B16)

    head_mask = (iota((4 * 64, 128), 0) >> 6) == (iota((4 * 64, 128), 1) >> 5)
    head_one = jnp.where(head_mask, 1.0, 0.0)
    head_b16 = head_one.astype(B16)

    def expand(values):
        return jnp.concatenate([values] * 4, axis=0) * head_b16

    def fold(values):
        kept = values * head_one
        return (kept[0:64] + kept[64:128]) + (kept[128:192] + kept[192:256])

    def lanes(n, g):
        return pl.ds(D * n + 128 * g, 128)

    key_row = down + ((iota((64, 1), 0) >> 3) & 7)
    query_row = down + ((iota((1, 256), 1) >> 3) & 7)
    key_away = (key_row < 0) | (key_row >= ROWS)
    query_away = (query_row < 0) | (query_row >= ROWS)
    pole = place.lat == jnp.where(a >= WIN // 2, 0, YHI * ZS - 1)
    apart = jnp.where(key_away, 1, 0) != jnp.where(query_away, 1, 0)
    bias = jnp.where(apart, jnp.where(pole, NEGATIVE, 0.0), 0.0)

    def forward(w, carry):
        rows = pl.ds(pl.multiple_of(w * 64, 64), 64)
        for g in range(4):
            queries = expand(packed[rows, lanes(0, g)])
            scores = dot_nt(packed[rows, lanes(1, g)], queries) * FACTOR + bias
            raised = jnp.exp(scores - jnp.max(scores, axis=0, keepdims=True))
            prob = raised * (1.0 / jnp.sum(raised, axis=0, keepdims=True))
            probs[w, g] = prob
            output = dot_tn(prob.astype(B16), packed[rows, lanes(2, g)])
            attended[rows, pl.ds(128 * g, 128)] = fold(output).astype(B16)
        return carry

    lax.fori_loop(0, WINDOWS, forward, 0)
    rounds[1].pick(attended[...], pick_window[...])
    rounds[1].start(attended[...])

    loads["w_proj"].wait()
    loads["w_merge"].wait()
    merged_back = [
        dot_nt(merged_grad[...], w_merge[pl.ds(D * part, D)]) for part in range(4)
    ]
    share.give_features("hidden", 0, hidden, share.hidden)
    share.give_features("attended", 1, attended[...], share.attended)

    own_attended = rounds[1].get(to_back[...]).astype(B16)
    own_out = (own_tokens + dot(own_attended, w_proj[...])).astype(B16)
    merged_in = own_out.astype(F32)
    quarters = [merged_in[MERGED * n : MERGED * (n + 1)] for n in range(4)]
    wide = 1.0 / (4 * D)

    def mean(values):
        return sum(jnp.sum(v, axis=-1, keepdims=True) for v in values) * wide

    center_at = mean(quarters)
    centers = [q - center_at for q in quarters]
    merged_inverse = lax.rsqrt(mean([c * c for c in centers]) + EPSILON)
    merged_normed = [c * merged_inverse for c in centers]
    back_mean = mean(merged_back)
    back_dot = mean([g * n for g, n in zip(merged_back, merged_normed)])
    for n in range(4):
        rows = pl.ds(MERGED * n, MERGED)
        merged_hidden[:, pl.ds(D * n, D)] = merged_normed[n].astype(B16)
        delta = merged_inverse * (merged_back[n] - back_mean - merged_normed[n] * back_dot)
        total_grad[rows] = (own_skip[MERGED * n : MERGED * (n + 1)] + delta).astype(B16)
    rounds[2].pick(total_grad[...], pick_merge[...])
    rounds[2].start(total_grad[...])
    factors.start_hidden(merged_hidden)

    skip_out[...] = dot(to_rows, own_out).astype(B16)
    merged_out[...] = dot(merged_hidden[...], w_merge[...]).astype(B16)
    factors.wait("grads")
    grads_t[...] = factors.grad[...].reshape(2 * XS * MERGED, D2).T

    window_total[...] = rounds[2].get(to_windows[...]).astype(B16)
    share.give("total", window_total, share.total)
    attended[...] = dot_nt(window_total[...], w_proj[...]).astype(B16)

    def backward(w, carry):
        rows = pl.ds(pl.multiple_of(w * 64, 64), 64)
        for g in range(4):
            queries = expand(packed[rows, lanes(0, g)])
            upstream = expand(attended[rows, pl.ds(128 * g, 128)])
            key_rows, value_rows = packed[rows, lanes(1, g)], packed[rows, lanes(2, g)]
            prob = probs[w, g]
            prob_grad = dot_nt(value_rows, upstream)
            total = jnp.sum(prob * prob_grad, axis=0, keepdims=True)
            score_grad = (prob * (prob_grad - total) * FACTOR).astype(B16)
            packed_grad[rows, lanes(0, g)] = fold(dot_tn(score_grad, key_rows)).astype(B16)
            packed_grad[rows, lanes(1, g)] = dot(score_grad, queries).astype(B16)
            packed_grad[rows, lanes(2, g)] = dot(prob.astype(B16), upstream).astype(B16)
        return carry

    def give_packed(part):
        rows = pl.ds(CELLS // 2 * part, CELLS // 2)
        share.give("packed", packed_grad.at[rows], share.packed.at[rows])

    def give_packed(part):
        rows = pl.ds(CELLS // 2 * part, CELLS // 2)
        share.give("packed", packed_grad.at[rows], share.packed.at[rows])

    factors.form(grads_t, merge_sum)
    merge_sum.start_second()
    lax.fori_loop(0, WINDOWS // 2, backward, 0)
    give_packed(0)
    share.wait("attended")
    share.wait("total")
    block = dot(share.attended[0], window_total[...]) + dot(share.attended[1], share.total[...])
    block = block.astype(B16)
    for yhi in range(YHI):
        for h in range(2):
            start = 256 * yhi + 128 * h
            proj_sum.parts[:, :, yhi, pl.ds(32 * h, 32)] = block[:, start : start + 128].reshape(
                XS, YLO, 32, 128
            )
    proj_sum.start_first()
    lax.fori_loop(WINDOWS // 2, WINDOWS, backward, 0)
    give_packed(1)

    hidden_grad = dot_nt(packed_grad[...], w_qkv[...])
    proj_sum.add_first()
    proj_sum.start_second()
    share.wait("hidden")
    share.wait("packed")
    for h in range(2):
        for yhi in range(YHI):
            columns = pl.ds(768 * yhi + 384 * h, 384)
            block = dot(share.hidden[0], packed_grad[:, columns])
            block = (block + dot(share.hidden[1], share.packed[:, columns])).astype(B16)
            for m in range(3):
                qkv_sums[h].parts[:, :, yhi, pl.ds(32 * m, 32)] = block[
                    :, 128 * m : 128 * (m + 1)
                ].reshape(XS, YLO, 32, 128)
        qkv_sums[h].start_first()
    merge_last.column[...] = merge_sum.add_second().reshape(ZS, 64, 128)
    merge_last.start()

    window_input = window_total[...].astype(F32) + inverse * (
        hidden_grad
        - jnp.mean(hidden_grad, axis=-1, keepdims=True)
        - normed[...] * jnp.mean(hidden_grad * normed[...], axis=-1, keepdims=True)
    )
    window_input = window_input.astype(B16)
    rounds[3].pick(window_input, pick_window[...])

    widen_fine = one_hot(384, 512, lambda n: (n // 96) * 128 + n % 96)
    widen_proj = one_hot(128, 512, lambda n: (n >> 5) * 128 + 96 + (n & 31))
    for path in qkv_sums:
        path.add_first()
        path.start_second()
    rounds[3].start(window_input)
    proj_total = proj_sum.add_second()
    proj_wide = [dot(proj_total[32 * h : 32 * (h + 1)], widen_proj) for h in range(2)]
    for h, path in enumerate(qkv_sums):
        total = path.add_second()
        wide_rows = jnp.concatenate([total[32 * m : 32 * (m + 1)] for m in range(3)], axis=1)
        block = (dot(wide_rows, widen_fine) + proj_wide[h]).astype(B16)
        for m in range(HALF):
            fine_last.column[HALF * h + m] = block[:, 128 * m : 128 * (m + 1)]
    fine_last.start()
    merge_last.add(sum_merge)
    input_grad[...] = rounds[3].get(to_output[...]).astype(B16)
    fine_last.add(sum_fine)


def finish_kernel(sum_merge, sum_fine, *refs):
    for src, dst in zip(refs[:3], refs[3:6]):
        dst[...] = src[...]
    dw_qkv, dw_proj, dw_merge = refs[6:]
    dw_qkv[...] = sum_fine[:, 0:96]
    dw_proj[...] = sum_fine[:, 96:128]
    dw_merge[...] = sum_merge[...]


def section(deep, *args):
    vmem, smem = pltpu.VMEM, pltpu.SMEM
    inside = pl.BlockSpec(memory_space=vmem)
    outside = pl.BlockSpec(memory_space=pl.ANY)
    shape = jax.ShapeDtypeStruct
    big = [shape((CELLS, D), B16), shape((MERGED, D2), B16), shape((CELLS, D), B16)]
    fringe = fringe_size(deep)
    return pl.pallas_call(
        functools.partial(section_kernel, deep),
        out_shape=big + [shape((64, 128), F32), shape((32, 128), F32)],
        in_specs=[pl.BlockSpec(memory_space=smem)] + [outside] * 6,
        out_specs=[inside] * 5,
        scratch_shapes=[
            vmem((CELLS, D), B16),
            vmem((CELLS, D), B16),
            vmem((D, 3 * D), B16),
            vmem((D, D), B16),
            vmem((4 * D, D2), B16),
            pltpu.SemaphoreType.DMA((6,)),
            vmem((CELLS, CELLS + fringe), B16),
            vmem((CELLS, CELLS + fringe), B16),
            vmem((CELLS, CELLS + fringe), B16),
            vmem((fringe, CELLS), B16),
            vmem((fringe, CELLS), B16),
            vmem((CELLS, D), F32),
            vmem((CELLS, 3 * D), B16),
            vmem((WINDOWS, 4, 64, 256), F32),
            vmem((CELLS, D), B16),
            vmem((CELLS, D), B16),
            vmem((CELLS, 3 * D), B16),
            vmem((MERGED, 4 * D), B16),
            vmem((CELLS, D), B16),
            vmem((D2, 2 * XS * MERGED), B16),
        ]
        + around_scratch(deep) * 4
        + gather_scratch()
        + path_scratch(512, (False, 1), (YLO, YHI))
        + path_scratch(64, (True, XS), (YLO, YHI))
        + path_scratch(96, (True, XS), (YLO, YHI))
        + path_scratch(96, (True, YS), (XS,))
        + last_scratch(64)
        + last_scratch(32)
        + share_scratch(),
        compiler_params=pltpu.CompilerParams(
            collective_id=deep, has_side_effects=True, vmem_limit_bytes=56 * 2**20
        ),
    )(*args)


def on_device(tokens, w_qkv, w_proj, w_merge, skip_grad, merged_grad, window_shift):
    inside = pl.BlockSpec(memory_space=pltpu.VMEM)
    shape = jax.ShapeDtypeStruct
    big = [shape((CELLS, D), B16), shape((MERGED, D2), B16), shape((CELLS, D), B16)]
    args = (
        window_shift,
        tokens.reshape(CELLS, D),
        skip_grad.reshape(CELLS, D),
        merged_grad.reshape(MERGED, D2),
        w_qkv,
        w_proj,
        w_merge,
    )
    shift = window_shift[0]
    rows = jnp.minimum(shift, WIN - shift)
    skip_out, merged_out, input_grad, sum_merge, sum_fine = lax.switch(
        jnp.minimum(rows, 3) - 1, [functools.partial(section, deep) for deep in (1, 2, 4)], *args
    )
    skip_out, merged_out, input_grad, dw_qkv, dw_proj, dw_merge = pl.pallas_call(
        finish_kernel,
        out_shape=big + [shape((32, 96), F32), shape((32, 32), F32), shape((64, 128), F32)],
        in_specs=[inside] * 5,
        out_specs=[inside] * 6,
    )(sum_merge, sum_fine, skip_out, merged_out, input_grad)
    return (
        skip_out.reshape(ROWS, COLS, D),
        merged_out.reshape(ROWS // 2, COLS // 2, D2),
        input_grad.reshape(ROWS, COLS, D),
        dw_qkv,
        dw_proj,
        dw_merge.T,
    )


def solution(mesh):
    in_specs = (
        P("lat", "lon", None),
        P(),
        P(),
        P(),
        P("lat", "lon", None),
        P("lat", "lon", None),
        P(),
    )
    out_specs = (
        P("lat", "lon", None),
        P("lat", "lon", None),
        P("lat", "lon", None),
        P("lon", "lat"),
        P("lon", "lat"),
        P("lon", "lat"),
    )
    return jax.shard_map(
        on_device, mesh=mesh, in_specs=in_specs, out_specs=out_specs, check_vma=False
    )
```

```python
import functools

import jax
import jax.numpy as jnp
from jax import lax
from jax.experimental import pallas as pl
from jax.experimental.pallas import tpu as pltpu
from jax.sharding import PartitionSpec as P

HEADS = 16
WIN = 8
EPSILON = 1e-05
NEGATIVE = -1e30
D = 512
D2 = 1024
ROWS, COLS = 8, 32
CELLS = ROWS * COLS
WINDOWS = COLS // WIN
FACTOR = 32 ** (-0.5)
MERGED = CELLS // 4
F32, B16 = jnp.float32, jnp.bfloat16

XS, YLO, CORES, YHI, ZS = 4, 2, 2, 2, 8
YS = YLO * YHI
MESH = pl.DeviceIdType.MESH


class Place:
    def __init__(self):
        lon = lax.axis_index("lon")
        lat = lax.axis_index("lat")
        self.lon, self.lat = lon, lat
        self.core = lon % CORES
        self.ylo = (lon // CORES) % YLO
        self.x = lon // (CORES * YLO)
        self.z = lat % ZS
        self.yhi = lat // ZS

    def at(self, x=None, ylo=None, core=None, yhi=None, z=None):
        x = self.x if x is None else x
        ylo = self.ylo if ylo is None else ylo
        core = self.core if core is None else core
        yhi = self.yhi if yhi is None else yhi
        z = self.z if z is None else z
        return ((x * YLO + ylo) * CORES + core, yhi * ZS + z)

    def beside(self, dlat, dlon):
        lons, lats = XS * YLO * CORES, YHI * ZS
        return ((self.lon + dlon) % lons, (self.lat + dlat) % lats)

    def sibling(self):
        return self.at(core=1 - self.core)

    def x_step(self, k):
        return (self.x + k) % XS

    def y_step(self, k):
        y = (self.yhi * YLO + self.ylo + k) % YS
        return (y // YLO, y % YLO)

    def z_step(self, k):
        return (self.z + k) % ZS

    def core_step(self, f):
        return 1 - self.core if f else self.core

    def partners(self):
        out = [self.sibling()]
        for k in range(1, XS):
            out += [self.at(x=self.x_step(k), core=self.core_step(f)) for f in range(2)]
        for k in range(1, YS):
            yhi, ylo = self.y_step(k)
            out += [self.at(yhi=yhi, ylo=ylo, core=self.core_step(f)) for f in range(2)]
        out += [self.at(z=self.z_step(k)) for k in range(1, ZS)]
        for dlat in (-1, 0, 1):
            for dlon in (-1, 0, 1):
                if (dlat, dlon) != (0, 0):
                    out.append(self.beside(dlat, dlon))
        return out


def device_of(pair):
    return {"lon": pair[0], "lat": pair[1]}


def greet(partners):
    barrier = pltpu.get_barrier_semaphore()
    for pair in partners:
        pl.semaphore_signal(barrier, inc=1, device_id=device_of(pair), device_id_type=MESH)


def await_greetings(partners):
    pl.semaphore_wait(pltpu.get_barrier_semaphore(), len(partners))


HALF = ZS // 2


class Copies:
    def __init__(self, place, send, recv):
        self.place, self.send, self.recv = place, send, recv
        self.used = 0
        self.flying = {}

    def copy(self, src, dst, pair):
        slot = self.used
        self.used += 1
        made = pltpu.make_async_remote_copy(
            src_ref=src,
            dst_ref=dst,
            send_sem=self.send.at[slot],
            recv_sem=self.recv.at[slot],
            device_id=device_of(pair),
            device_id_type=MESH,
        )
        made.start()
        return made

    def wait(self, name):
        for made in self.flying[name]:
            made.wait()


def path_scratch(rows, first, second):
    one, two = first[0], second
    flat = 1
    for size in two:
        flat *= size
    copies = (first[1] - 1) + (flat - 1)
    out = [
        pltpu.VMEM((*two, rows, 128), B16),
        pltpu.VMEM((flat - 1, rows, 128), B16),
        pltpu.SemaphoreType.DMA((copies,)),
        pltpu.SemaphoreType.DMA((copies,)),
    ]
    if one:
        out += [
            pltpu.VMEM((XS, YLO, YHI, rows, 128), B16),
            pltpu.VMEM((first[1] - 1, *two, rows, 128), B16),
        ]
    return out


class PathXY(Copies):
    def __init__(self, place, scratch):
        self.sum, self.late = scratch[:2]
        super().__init__(place, *scratch[2:4])
        if len(scratch) > 4:
            self.parts, self.got = scratch[4:]

    def start_first(self):
        place = self.place
        self.flying["x"] = [
            self.copy(
                self.parts.at[place.x_step(k)], self.got.at[k - 1], place.at(x=place.x_step(k))
            )
            for k in range(1, XS)
        ]

    def add_first(self):
        self.wait("x")
        for ylo in range(YLO):
            for yhi in range(YHI):
                total = self.parts[self.place.x, ylo, yhi].astype(F32)
                for k in range(XS - 1):
                    total += self.got[k, ylo, yhi].astype(F32)
                self.sum[ylo, yhi] = total.astype(B16)

    def start_second(self):
        self.flying["y"] = []
        for k in range(1, YS):
            yhi, ylo = self.place.y_step(k)
            pair = self.place.at(yhi=yhi, ylo=ylo)
            self.flying["y"].append(self.copy(self.sum.at[ylo, yhi], self.late.at[k - 1], pair))

    def add_second(self):
        self.wait("y")
        total = self.sum[self.place.ylo, self.place.yhi].astype(F32)
        for k in range(YS - 1):
            total += self.late[k].astype(F32)
        return total.astype(B16)


class PathYX(Copies):
    def __init__(self, place, scratch):
        self.sum, self.late = scratch[:2]
        super().__init__(place, *scratch[2:4])
        self.parts, self.got = scratch[4:]

    def start_first(self):
        self.flying["y"] = []
        for k in range(1, YS):
            yhi, ylo = self.place.y_step(k)
            pair = self.place.at(yhi=yhi, ylo=ylo)
            self.flying["y"].append(
                self.copy(self.parts.at[:, ylo, yhi], self.got.at[k - 1], pair)
            )

    def add_first(self):
        self.wait("y")
        for x in range(XS):
            total = self.parts[x, self.place.ylo, self.place.yhi].astype(F32)
            for k in range(YS - 1):
                total += self.got[k, x].astype(F32)
            self.sum[x] = total.astype(B16)

    def start_second(self):
        place = self.place
        self.flying["x"] = [
            self.copy(
                self.sum.at[place.x_step(k)], self.late.at[k - 1], place.at(x=place.x_step(k))
            )
            for k in range(1, XS)
        ]

    def add_second(self):
        self.wait("x")
        total = self.sum[self.place.x].astype(F32)
        for k in range(XS - 1):
            total += self.late[k].astype(F32)
        return total.astype(B16)


def last_scratch(rows):
    return [
        pltpu.VMEM((ZS, rows, 128), B16),
        pltpu.VMEM((ZS - 1, rows, 128), B16),
        pltpu.SemaphoreType.DMA((ZS - 1,)),
        pltpu.SemaphoreType.DMA((ZS - 1,)),
    ]


class Last(Copies):
    def __init__(self, place, scratch):
        self.column, self.from_z = scratch[:2]
        super().__init__(place, *scratch[2:])

    def start(self):
        place = self.place
        self.flying["z"] = [
            self.copy(
                self.column.at[place.z_step(k)],
                self.from_z.at[k - 1],
                place.at(z=place.z_step(k)),
            )
            for k in range(1, ZS)
        ]

    def add(self, out):
        self.wait("z")
        total = self.column[self.place.z].astype(F32)
        for k in range(ZS - 1):
            total += self.from_z[k].astype(F32)
        out[...] = total


def share_scratch():
    half = D // 2
    return [
        pltpu.VMEM((2, half, CELLS), B16),
        pltpu.VMEM((2, half, CELLS), B16),
        pltpu.VMEM((2, half, CELLS), B16),
        pltpu.VMEM((CELLS, D), B16),
        pltpu.VMEM((CELLS, 3 * D), B16),
        pltpu.SemaphoreType.DMA((5,)),
        pltpu.SemaphoreType.DMA((5,)),
    ]


class Share(Copies):
    def __init__(self, place, scratch):
        self.out, self.hidden, self.attended, self.total, self.packed = scratch[:5]
        super().__init__(place, *scratch[5:])

    def give(self, name, src, dst):
        self.flying.setdefault(name, []).append(self.copy(src, dst, self.place.sibling()))

    def give_features(self, name, slot, values, kept):
        core, half = self.place.core, D // 2

        def feature(n):
            m = n & (half - 1)
            owner = jnp.where(n < half, core, 1 - core)
            return ((m >> 5) * CORES + owner) * 32 + (m & 31)

        moved = dot_nt(one_hot(D, D, feature), values).astype(B16)
        kept[0] = moved[0:half]
        self.out[slot] = moved[half:D]
        self.give(name, self.out.at[slot], kept.at[1])


def gather_scratch():
    copies = 2 * (2 * XS - 1)
    return [
        pltpu.VMEM((2 * XS, MERGED, D2), B16),
        pltpu.VMEM((2 * XS, MERGED, D // 2), B16),
        pltpu.VMEM((XS, CORES, MERGED, D // 2), B16),
        pltpu.SemaphoreType.DMA((copies,)),
        pltpu.SemaphoreType.DMA((copies,)),
    ]


class Gather(Copies):
    def __init__(self, place, scratch):
        self.grad, self.hidden, self.hidden_parts = scratch[:3]
        super().__init__(place, *scratch[3:])

    def around(self):
        return [(k, f) for k in range(XS) for f in range(2) if (k, f) != (0, 0)]

    def start_grads(self):
        place = self.place
        self.flying["grads"] = []
        for k, f in self.around():
            pair = place.at(x=place.x_step(k), core=place.core_step(f))
            self.flying["grads"].append(
                self.copy(self.grad.at[0], self.grad.at[2 * k + f], pair)
            )

    def start_hidden(self, hidden):
        place = self.place
        for x in range(XS):
            for ylo in range(YLO):
                for core in range(CORES):
                    start = ((x * YLO + ylo) * CORES + core) * 128
                    self.hidden_parts[x, core, :, 128 * ylo : 128 * (ylo + 1)] = hidden[
                        :, start : start + 128
                    ]
        self.flying["hidden"] = []
        for k, f in self.around():
            x, core = place.x_step(k), place.core_step(f)
            self.flying["hidden"].append(
                self.copy(
                    self.hidden_parts.at[x, core],
                    self.hidden.at[2 * k + f],
                    place.at(x=x, core=core),
                )
            )
        self.hidden[0] = self.hidden_parts[place.x, place.core]

    def form(self, grads_t, path):
        self.wait("hidden")
        hidden = self.hidden[...].reshape(2 * XS * MERGED, D // 2)

        def body(yhi, carry):
            rows = pl.ds(pl.multiple_of(D * yhi, D), D)
            block = dot(grads_t[rows], hidden).astype(B16)
            for ylo in range(YLO):
                path.sum[ylo, yhi] = block[:, 128 * ylo : 128 * (ylo + 1)]
            return carry

        lax.fori_loop(0, YHI, body, 0)


def iota(shape, dim):
    return lax.broadcasted_iota(jnp.int32, shape, dim)


def one_hot(rows, cols, index):
    place = index(iota((rows, 1), 0))
    return jnp.where(iota((rows, cols), 1) == place, 1.0, 0.0).astype(B16)


def dot(a, b):
    return jnp.dot(a, b, preferred_element_type=F32)


def dot_nt(a, b):
    return lax.dot_general(a, b, (((1,), (1,)), ((), ())), preferred_element_type=F32)


def dot_tn(a, b):
    return lax.dot_general(a, b, (((0,), (0,)), ((), ())), preferred_element_type=F32)


def rows_at(n):
    return n >> 5, n & 31


def rows_index(i, j):
    return i * COLS + j


def merge_at(n):
    part, r, c = n >> 6, (n >> 4) & 3, n & 15
    return 2 * r + (part & 1), 2 * c + (part >> 1)


def merge_index(i, j):
    return (((j & 1) * 2 + (i & 1)) << 6) + ((i >> 1) << 4) + (j >> 1)


def window_at(n):
    return (n >> 3) & 7, ((n >> 6) << 3) + (n & 7)


def window_index(i, j):
    return ((j >> 3) << 6) + (i << 3) + (j & 7)


def fringe_at(n, deep):
    side = n < 64 * deep
    strip = n < 64 * deep + 64
    m = n & 31
    i_side = (n >> 5) + jnp.where(n < 32 * deep, 0, ROWS - 2 * deep)
    i = jnp.where(side, i_side, jnp.where(strip, m >> 2, ((n & 15) >> 2) + 4 * ((n >> 5) & 1)))
    last = jnp.where(strip, (n >> 5) & 1, (n >> 4) & 1)
    j = jnp.where(side, m, (n & 3) + last * (COLS - 4))
    return i, j


def around_index(index, i, j, deep):
    up, down, left, right = i < 0, i >= ROWS, j < 0, j >= COLS
    col4 = jnp.where(left, j + 4, j - COLS)
    north = up | down
    side = north & ~(left | right)
    strip = (left | right) & ~north
    corner = north & (left | right)
    at = index(i, j)
    row = jnp.where(up, i + 2 * deep, i - ROWS)
    at = jnp.where(side, CELLS + row * COLS + j, at)
    at = jnp.where(strip, CELLS + 64 * deep + jnp.where(left, 32, 0) + i * 4 + col4, at)
    base = CELLS + 64 * deep + 64 + jnp.where(up, 32, 0) + jnp.where(left, 16, 0)
    row4 = jnp.where(up, i + 4, i - ROWS)
    return jnp.where(corner, base + row4 * 4 + col4, at)


def normalize(values):
    center = values - jnp.mean(values, axis=-1, keepdims=True)
    inverse = lax.rsqrt(jnp.mean(center * center, axis=-1, keepdims=True) + EPSILON)
    return center * inverse, inverse


def fringe_size(deep):
    return 64 * deep + 128


def fringes(deep):
    rows, base = 32 * deep, 64 * deep
    return (
        (0, rows, -1, 0),
        (rows, rows, 1, 0),
        (base, 32, 0, -1),
        (base + 32, 32, 0, 1),
        (base + 64, 16, -1, -1),
        (base + 80, 16, -1, 1),
        (base + 96, 16, 1, -1),
        (base + 112, 16, 1, 1),
    )


def around_scratch(deep):
    return [
        pltpu.VMEM((CELLS + fringe_size(deep), D), B16),
        pltpu.VMEM((fringe_size(deep), D), B16),
        pltpu.SemaphoreType.DMA((8,)),
        pltpu.SemaphoreType.DMA((8,)),
    ]


class Around(Copies):
    def __init__(self, place, deep, scratch):
        self.block, self.fringe = scratch[:2]
        self.deep = deep
        super().__init__(place, *scratch[2:])

    def pick(self, values, picks):
        self.fringe[...] = dot(picks, values).astype(B16)

    def start(self, values):
        self.flying["fringe"] = [
            self.copy(
                self.fringe.at[pl.ds(offset, size)],
                self.block.at[pl.ds(CELLS + offset, size)],
                self.place.beside(dlat, dlon),
            )
            for offset, size, dlat, dlon in fringes(self.deep)
        ]
        self.block[pl.ds(0, CELLS)] = values

    def get(self, picks):
        self.wait("fringe")
        return dot(picks, self.block[...])


def section_kernel(
    deep,
    shift,
    tokens_hbm,
    skip_grad_hbm,
    merged_grad_hbm,
    w_qkv_hbm,
    w_proj_hbm,
    w_merge_hbm,
    skip_out,
    merged_out,
    input_grad,
    sum_merge,
    sum_fine,
    tokens,
    skip_grad,
    w_qkv,
    w_proj,
    w_merge,
    load,
    to_back,
    to_windows,
    to_output,
    pick_window,
    pick_merge,
    normed,
    packed,
    probs,
    attended,
    window_total,
    packed_grad,
    merged_hidden,
    total_grad,
    grads_t,
    own_part,
    back,
    *scratch,
):
    place = Place()
    partners = place.partners()
    greet(partners)
    rounds = [Around(place, deep, scratch[4 * n : 4 * n + 4]) for n in range(4)]
    scratch = scratch[16:]
    factors = Gather(place, scratch[:5])
    merge_sum = PathXY(place, scratch[5:9])
    proj_sum = PathXY(place, scratch[9:15])
    qkv_sums = PathXY(place, scratch[15:21]), PathYX(place, scratch[21:27])
    merge_last = Last(place, scratch[27:31])
    fine_last = Last(place, scratch[31:35])
    share = Share(place, scratch[35:42])
    merged_grad = factors.grad.at[0]
    loads = {}
    for n, (name, src, dst) in enumerate(
        (
            ("tokens", tokens_hbm, tokens),
            ("merged_grad", merged_grad_hbm, merged_grad),
            ("w_qkv", w_qkv_hbm, w_qkv),
            ("skip_grad", skip_grad_hbm, skip_grad),
            ("w_proj", w_proj_hbm, w_proj),
            ("w_merge", w_merge_hbm, w_merge),
        )
    ):
        loads[name] = pltpu.make_async_copy(src, dst, load.at[n])
        loads[name].start()

    a, b = shift[0], shift[1]
    down = jnp.where(a >= WIN // 2, a - WIN, a)
    right = jnp.where(b >= WIN // 2, b - WIN, b)

    def picker(index):
        return one_hot(fringe_size(deep), CELLS, lambda n: index(*fringe_at(n, deep)))

    def shifted(at, index, sign):
        def source(n):
            i, j = at(n)
            return around_index(index, i + sign * down, j + sign * right, deep)

        return one_hot(CELLS, CELLS + fringe_size(deep), source)

    from_tokens = shifted(window_at, rows_index, 1)
    pick_tokens = picker(rows_index)
    loads["tokens"].wait()
    rounds[0].pick(tokens[...], pick_tokens)
    await_greetings(partners)
    rounds[0].start(tokens[...])
    loads["merged_grad"].wait()
    factors.start_grads()

    to_back[...] = shifted(merge_at, window_index, -1)
    to_windows[...] = shifted(window_at, merge_index, 1)
    to_output[...] = shifted(rows_at, window_index, -1)
    pick_window[...] = picker(window_index)
    pick_merge[...] = picker(merge_index)
    to_merged = one_hot(CELLS, CELLS, lambda n: rows_index(*merge_at(n)))
    to_rows = one_hot(CELLS, CELLS, lambda n: merge_index(*rows_at(n)))
    own_tokens = dot(to_merged, tokens[...])
    loads["skip_grad"].wait()
    own_skip = dot(to_merged, skip_grad[...])
    loads["w_qkv"].wait()

    values, inverse = normalize(rounds[0].get(from_tokens))
    normed[...] = values
    hidden = values.astype(B16)

    def project(n, carry):
        columns = pl.ds(pl.multiple_of(D * n, D), D)
        packed[:, columns] = dot(hidden, w_qkv[:, columns]).astype(B16)
        return carry

    lax.fori_loop(0, 3, project, 0)

    head_mask = (iota((4 * 64, 128), 0) >> 6) == (iota((4 * 64, 128), 1) >> 5)
    head_one = jnp.where(head_mask, 1.0, 0.0)
    head_b16 = head_one.astype(B16)

    def expand(values):
        return jnp.concatenate([values] * 4, axis=0) * head_b16

    def fold(values):
        kept = values * head_one
        return (kept[0:64] + kept[64:128]) + (kept[128:192] + kept[192:256])

    def lanes(n, g):
        return pl.ds(D * n + 128 * g, 128)

    key_row = down + ((iota((64, 1), 0) >> 3) & 7)
    query_row = down + ((iota((1, 256), 1) >> 3) & 7)
    key_away = (key_row < 0) | (key_row >= ROWS)
    query_away = (query_row < 0) | (query_row >= ROWS)
    pole = place.lat == jnp.where(a >= WIN // 2, 0, YHI * ZS - 1)
    apart = jnp.where(key_away, 1, 0) != jnp.where(query_away, 1, 0)
    bias = jnp.where(apart, jnp.where(pole, NEGATIVE, 0.0), 0.0)

    def forward(w, carry):
        rows = pl.ds(pl.multiple_of(w * 64, 64), 64)
        for g in range(4):
            queries = expand(packed[rows, lanes(0, g)])
            scores = dot_nt(packed[rows, lanes(1, g)], queries) * FACTOR + bias
            raised = jnp.exp(scores - jnp.max(scores, axis=0, keepdims=True))
            prob = raised * (1.0 / jnp.sum(raised, axis=0, keepdims=True))
            probs[w, g] = prob
            output = dot_tn(prob.astype(B16), packed[rows, lanes(2, g)])
            attended[rows, pl.ds(128 * g, 128)] = fold(output).astype(B16)
        return carry

    lax.fori_loop(0, WINDOWS, forward, 0, unroll=2)
    rounds[1].pick(attended[...], pick_window[...])
    rounds[1].start(attended[...])

    loads["w_proj"].wait()
    loads["w_merge"].wait()

    def merge_back(part, carry):
        rows = pl.ds(pl.multiple_of(D * part, D), D)
        back[part] = dot_nt(merged_grad[...], w_merge[rows])
        return carry

    lax.fori_loop(0, 4, merge_back, 0)
    share.give_features("hidden", 0, hidden, share.hidden)
    share.give_features("attended", 1, attended[...], share.attended)

    own_attended = rounds[1].get(to_back[...]).astype(B16)
    merged_back = [back[part] for part in range(4)]
    own_out = (own_tokens + dot(own_attended, w_proj[...])).astype(B16)
    merged_in = own_out.astype(F32)
    quarters = [merged_in[MERGED * n : MERGED * (n + 1)] for n in range(4)]
    wide = 1.0 / (4 * D)

    def mean(values):
        return sum(jnp.sum(v, axis=-1, keepdims=True) for v in values) * wide

    center_at = mean(quarters)
    centers = [q - center_at for q in quarters]
    merged_inverse = lax.rsqrt(mean([c * c for c in centers]) + EPSILON)
    merged_normed = [c * merged_inverse for c in centers]
    back_mean = mean(merged_back)
    back_dot = mean([g * n for g, n in zip(merged_back, merged_normed)])
    for n in range(4):
        rows = pl.ds(MERGED * n, MERGED)
        merged_hidden[:, pl.ds(D * n, D)] = merged_normed[n].astype(B16)
        delta = merged_inverse * (merged_back[n] - back_mean - merged_normed[n] * back_dot)
        total_grad[rows] = (own_skip[MERGED * n : MERGED * (n + 1)] + delta).astype(B16)
    rounds[2].pick(total_grad[...], pick_merge[...])
    rounds[2].start(total_grad[...])
    factors.start_hidden(merged_hidden)

    skip_out[...] = dot(to_rows, own_out).astype(B16)
    merged_out[...] = dot(merged_hidden[...], w_merge[...]).astype(B16)
    factors.wait("grads")
    grads_t[...] = factors.grad[...].reshape(2 * XS * MERGED, D2).T

    window_total[...] = rounds[2].get(to_windows[...]).astype(B16)
    share.give("total", window_total, share.total)
    attended[...] = dot_nt(window_total[...], w_proj[...]).astype(B16)

    def backward(w, carry):
        rows = pl.ds(pl.multiple_of(w * 64, 64), 64)
        for g in range(4):
            queries = expand(packed[rows, lanes(0, g)])
            upstream = expand(attended[rows, pl.ds(128 * g, 128)])
            key_rows, value_rows = packed[rows, lanes(1, g)], packed[rows, lanes(2, g)]
            prob = probs[w, g]
            prob_grad = dot_nt(value_rows, upstream)
            total = jnp.sum(prob * prob_grad, axis=0, keepdims=True)
            score_grad = (prob * (prob_grad - total) * FACTOR).astype(B16)
            packed_grad[rows, lanes(0, g)] = fold(dot_tn(score_grad, key_rows)).astype(B16)
            packed_grad[rows, lanes(1, g)] = dot(score_grad, queries).astype(B16)
            packed_grad[rows, lanes(2, g)] = dot(prob.astype(B16), upstream).astype(B16)
        return carry

    def give_packed(part):
        rows = pl.ds(CELLS // 2 * part, CELLS // 2)
        share.give("packed", packed_grad.at[rows], share.packed.at[rows])

    def give_packed(part):
        rows = pl.ds(CELLS // 2 * part, CELLS // 2)
        share.give("packed", packed_grad.at[rows], share.packed.at[rows])

    factors.form(grads_t, merge_sum)
    merge_sum.start_second()
    lax.fori_loop(0, WINDOWS // 2, backward, 0, unroll=2)
    give_packed(0)
    share.wait("attended")
    share.wait("total")
    block = dot(share.attended[0], window_total[...]) + dot(share.attended[1], share.total[...])
    block = block.astype(B16)
    for yhi in range(YHI):
        for h in range(2):
            start = 256 * yhi + 128 * h
            proj_sum.parts[:, :, yhi, pl.ds(32 * h, 32)] = block[:, start : start + 128].reshape(
                XS, YLO, 32, 128
            )
    proj_sum.start_first()
    lax.fori_loop(WINDOWS // 2, WINDOWS, backward, 0, unroll=2)
    give_packed(1)

    share.wait("hidden")

    def form_own(n, carry):
        columns = pl.ds(pl.multiple_of(D * n, D), D)
        own_part[:, columns] = dot(share.hidden[0], packed_grad[:, columns])
        return carry

    lax.fori_loop(0, 3, form_own, 0)
    share.wait("packed")
    for h in range(2):

        def form_both(yhi, carry):
            columns = pl.ds(pl.multiple_of(768 * yhi + 384 * h, 128), 384)
            block = own_part[:, columns] + dot(share.hidden[1], share.packed[:, columns])
            block = block.astype(B16)
            for m in range(3):
                qkv_sums[h].parts[:, :, yhi, pl.ds(32 * m, 32)] = block[
                    :, 128 * m : 128 * (m + 1)
                ].reshape(XS, YLO, 32, 128)
            return carry

        lax.fori_loop(0, YHI, form_both, 0)
        qkv_sums[h].start_first()
    proj_sum.add_first()
    proj_sum.start_second()
    merge_last.column[...] = merge_sum.add_second().reshape(ZS, 64, 128)
    merge_last.start()

    hidden_grad = dot_nt(packed_grad[...], w_qkv[...])
    window_input = window_total[...].astype(F32) + inverse * (
        hidden_grad
        - jnp.mean(hidden_grad, axis=-1, keepdims=True)
        - normed[...] * jnp.mean(hidden_grad * normed[...], axis=-1, keepdims=True)
    )
    window_input = window_input.astype(B16)
    rounds[3].pick(window_input, pick_window[...])

    widen_fine = one_hot(384, 512, lambda n: (n // 96) * 128 + n % 96)
    widen_proj = one_hot(128, 512, lambda n: (n >> 5) * 128 + 96 + (n & 31))
    for path in qkv_sums:
        path.add_first()
        path.start_second()
    rounds[3].start(window_input)
    proj_total = proj_sum.add_second()
    proj_wide = [dot(proj_total[32 * h : 32 * (h + 1)], widen_proj) for h in range(2)]
    for h, path in enumerate(qkv_sums):
        total = path.add_second()
        wide_rows = jnp.concatenate([total[32 * m : 32 * (m + 1)] for m in range(3)], axis=1)
        block = (dot(wide_rows, widen_fine) + proj_wide[h]).astype(B16)
        for m in range(HALF):
            fine_last.column[HALF * h + m] = block[:, 128 * m : 128 * (m + 1)]
    fine_last.start()
    merge_last.add(sum_merge)
    input_grad[...] = rounds[3].get(to_output[...]).astype(B16)
    fine_last.add(sum_fine)


def finish_kernel(sum_merge, sum_fine, *refs):
    for src, dst in zip(refs[:3], refs[3:6]):
        dst[...] = src[...]
    dw_qkv, dw_proj, dw_merge = refs[6:]
    dw_qkv[...] = sum_fine[:, 0:96]
    dw_proj[...] = sum_fine[:, 96:128]
    dw_merge[...] = sum_merge[...]


def section(deep, *args):
    vmem, smem = pltpu.VMEM, pltpu.SMEM
    inside = pl.BlockSpec(memory_space=vmem)
    outside = pl.BlockSpec(memory_space=pl.ANY)
    shape = jax.ShapeDtypeStruct
    big = [shape((CELLS, D), B16), shape((MERGED, D2), B16), shape((CELLS, D), B16)]
    fringe = fringe_size(deep)
    return pl.pallas_call(
        functools.partial(section_kernel, deep),
        out_shape=big + [shape((64, 128), F32), shape((32, 128), F32)],
        in_specs=[pl.BlockSpec(memory_space=smem)] + [outside] * 6,
        out_specs=[inside] * 5,
        scratch_shapes=[
            vmem((CELLS, D), B16),
            vmem((CELLS, D), B16),
            vmem((D, 3 * D), B16),
            vmem((D, D), B16),
            vmem((4 * D, D2), B16),
            pltpu.SemaphoreType.DMA((6,)),
            vmem((CELLS, CELLS + fringe), B16),
            vmem((CELLS, CELLS + fringe), B16),
            vmem((CELLS, CELLS + fringe), B16),
            vmem((fringe, CELLS), B16),
            vmem((fringe, CELLS), B16),
            vmem((CELLS, D), F32),
            vmem((CELLS, 3 * D), B16),
            vmem((WINDOWS, 4, 64, 256), F32),
            vmem((CELLS, D), B16),
            vmem((CELLS, D), B16),
            vmem((CELLS, 3 * D), B16),
            vmem((MERGED, 4 * D), B16),
            vmem((CELLS, D), B16),
            vmem((D2, 2 * XS * MERGED), B16),
            vmem((D // 2, 3 * D), F32),
            vmem((4, MERGED, D), F32),
        ]
        + around_scratch(deep) * 4
        + gather_scratch()
        + path_scratch(512, (False, 1), (YLO, YHI))
        + path_scratch(64, (True, XS), (YLO, YHI))
        + path_scratch(96, (True, XS), (YLO, YHI))
        + path_scratch(96, (True, YS), (XS,))
        + last_scratch(64)
        + last_scratch(32)
        + share_scratch(),
        compiler_params=pltpu.CompilerParams(
            collective_id=deep, has_side_effects=True, vmem_limit_bytes=56 * 2**20
        ),
    )(*args)


def on_device(tokens, w_qkv, w_proj, w_merge, skip_grad, merged_grad, window_shift):
    inside = pl.BlockSpec(memory_space=pltpu.VMEM)
    shape = jax.ShapeDtypeStruct
    big = [shape((CELLS, D), B16), shape((MERGED, D2), B16), shape((CELLS, D), B16)]
    args = (
        window_shift,
        tokens.reshape(CELLS, D),
        skip_grad.reshape(CELLS, D),
        merged_grad.reshape(MERGED, D2),
        w_qkv,
        w_proj,
        w_merge,
    )
    shift = window_shift[0]
    rows = jnp.minimum(shift, WIN - shift)
    skip_out, merged_out, input_grad, sum_merge, sum_fine = lax.switch(
        jnp.minimum(rows, 3) - 1, [functools.partial(section, deep) for deep in (1, 2, 4)], *args
    )
    skip_out, merged_out, input_grad, dw_qkv, dw_proj, dw_merge = pl.pallas_call(
        finish_kernel,
        out_shape=big + [shape((32, 96), F32), shape((32, 32), F32), shape((64, 128), F32)],
        in_specs=[inside] * 5,
        out_specs=[inside] * 6,
    )(sum_merge, sum_fine, skip_out, merged_out, input_grad)
    return (
        skip_out.reshape(ROWS, COLS, D),
        merged_out.reshape(ROWS // 2, COLS // 2, D2),
        input_grad.reshape(ROWS, COLS, D),
        dw_qkv,
        dw_proj,
        dw_merge.T,
    )


def solution(mesh):
    in_specs = (
        P("lat", "lon", None),
        P(),
        P(),
        P(),
        P("lat", "lon", None),
        P("lat", "lon", None),
        P(),
    )
    out_specs = (
        P("lat", "lon", None),
        P("lat", "lon", None),
        P("lat", "lon", None),
        P("lon", "lat"),
        P("lon", "lat"),
        P("lon", "lat"),
    )
    return jax.shard_map(
        on_device, mesh=mesh, in_specs=in_specs, out_specs=out_specs, check_vma=False
    )
```

```python
import functools

import jax
import jax.numpy as jnp
from jax import lax
from jax.experimental import pallas as pl
from jax.experimental.pallas import tpu as pltpu
from jax.sharding import PartitionSpec as P

HEADS = 16
WIN = 8
EPSILON = 1e-05
NEGATIVE = -1e30
D = 512
D2 = 1024
ROWS, COLS = 8, 32
CELLS = ROWS * COLS
WINDOWS = COLS // WIN
FACTOR = 32 ** (-0.5)
LOG2E = 1.4426950408889634
MERGED = CELLS // 4
F32, B16 = jnp.float32, jnp.bfloat16

XS, YLO, CORES, YHI, ZS = 4, 2, 2, 2, 8
YS = YLO * YHI
MESH = pl.DeviceIdType.MESH


class Place:
    def __init__(self):
        lon = lax.axis_index("lon")
        lat = lax.axis_index("lat")
        self.lon, self.lat = lon, lat
        self.core = lon % CORES
        self.ylo = (lon // CORES) % YLO
        self.x = lon // (CORES * YLO)
        self.z = lat % ZS
        self.yhi = lat // ZS

    def at(self, x=None, ylo=None, core=None, yhi=None, z=None):
        x = self.x if x is None else x
        ylo = self.ylo if ylo is None else ylo
        core = self.core if core is None else core
        yhi = self.yhi if yhi is None else yhi
        z = self.z if z is None else z
        return ((x * YLO + ylo) * CORES + core, yhi * ZS + z)

    def beside(self, dlat, dlon):
        lons, lats = XS * YLO * CORES, YHI * ZS
        return ((self.lon + dlon) % lons, (self.lat + dlat) % lats)

    def sibling(self):
        return self.at(core=1 - self.core)

    def x_step(self, k):
        return (self.x + k) % XS

    def y_step(self, k):
        y = (self.yhi * YLO + self.ylo + k) % YS
        return (y // YLO, y % YLO)

    def z_step(self, k):
        return (self.z + k) % ZS

    def core_step(self, f):
        return 1 - self.core if f else self.core

    def partners(self):
        out = [self.sibling()]
        for k in range(1, XS):
            out += [self.at(x=self.x_step(k), core=self.core_step(f)) for f in range(2)]
        for k in range(1, YS):
            yhi, ylo = self.y_step(k)
            out += [self.at(yhi=yhi, ylo=ylo, core=self.core_step(f)) for f in range(2)]
        out += [self.at(z=self.z_step(k)) for k in range(1, ZS)]
        for dlat in (-1, 0, 1):
            for dlon in (-1, 0, 1):
                if (dlat, dlon) != (0, 0):
                    out.append(self.beside(dlat, dlon))
        return out


def device_of(pair):
    return {"lon": pair[0], "lat": pair[1]}


def greet(partners):
    barrier = pltpu.get_barrier_semaphore()
    for pair in partners:
        pl.semaphore_signal(barrier, inc=1, device_id=device_of(pair), device_id_type=MESH)


def await_greetings(partners):
    pl.semaphore_wait(pltpu.get_barrier_semaphore(), len(partners))


HALF = ZS // 2


class Copies:
    def __init__(self, place, send, recv):
        self.place, self.send, self.recv = place, send, recv
        self.used = 0
        self.flying = {}

    def copy(self, src, dst, pair):
        slot = self.used
        self.used += 1
        made = pltpu.make_async_remote_copy(
            src_ref=src,
            dst_ref=dst,
            send_sem=self.send.at[slot],
            recv_sem=self.recv.at[slot],
            device_id=device_of(pair),
            device_id_type=MESH,
        )
        made.start()
        return made

    def wait(self, name):
        for made in self.flying[name]:
            made.wait()


def path_scratch(rows, first, second):
    one, two = first[0], second
    flat = 1
    for size in two:
        flat *= size
    copies = (first[1] - 1) + (flat - 1)
    out = [
        pltpu.VMEM((*two, rows, 128), B16),
        pltpu.VMEM((flat - 1, rows, 128), B16),
        pltpu.SemaphoreType.DMA((copies,)),
        pltpu.SemaphoreType.DMA((copies,)),
    ]
    if one:
        out += [
            pltpu.VMEM((XS, YLO, YHI, rows, 128), B16),
            pltpu.VMEM((first[1] - 1, *two, rows, 128), B16),
        ]
    return out


class PathXY(Copies):
    def __init__(self, place, scratch):
        self.sum, self.late = scratch[:2]
        super().__init__(place, *scratch[2:4])
        if len(scratch) > 4:
            self.parts, self.got = scratch[4:]

    def start_first(self):
        place = self.place
        self.flying["x"] = [
            self.copy(
                self.parts.at[place.x_step(k)], self.got.at[k - 1], place.at(x=place.x_step(k))
            )
            for k in range(1, XS)
        ]

    def add_first(self):
        self.wait("x")
        for ylo in range(YLO):
            for yhi in range(YHI):
                total = self.parts[self.place.x, ylo, yhi].astype(F32)
                for k in range(XS - 1):
                    total += self.got[k, ylo, yhi].astype(F32)
                self.sum[ylo, yhi] = total.astype(B16)

    def start_second(self):
        self.flying["y"] = []
        for k in range(1, YS):
            yhi, ylo = self.place.y_step(k)
            pair = self.place.at(yhi=yhi, ylo=ylo)
            self.flying["y"].append(self.copy(self.sum.at[ylo, yhi], self.late.at[k - 1], pair))

    def add_second(self):
        self.wait("y")
        total = self.sum[self.place.ylo, self.place.yhi].astype(F32)
        for k in range(YS - 1):
            total += self.late[k].astype(F32)
        return total.astype(B16)


class PathYX(Copies):
    def __init__(self, place, scratch):
        self.sum, self.late = scratch[:2]
        super().__init__(place, *scratch[2:4])
        self.parts, self.got = scratch[4:]

    def start_first(self):
        self.flying["y"] = []
        for k in range(1, YS):
            yhi, ylo = self.place.y_step(k)
            pair = self.place.at(yhi=yhi, ylo=ylo)
            self.flying["y"].append(
                self.copy(self.parts.at[:, ylo, yhi], self.got.at[k - 1], pair)
            )

    def add_first(self):
        self.wait("y")
        for x in range(XS):
            total = self.parts[x, self.place.ylo, self.place.yhi].astype(F32)
            for k in range(YS - 1):
                total += self.got[k, x].astype(F32)
            self.sum[x] = total.astype(B16)

    def start_second(self):
        place = self.place
        self.flying["x"] = [
            self.copy(
                self.sum.at[place.x_step(k)], self.late.at[k - 1], place.at(x=place.x_step(k))
            )
            for k in range(1, XS)
        ]

    def add_second(self):
        self.wait("x")
        total = self.sum[self.place.x].astype(F32)
        for k in range(XS - 1):
            total += self.late[k].astype(F32)
        return total.astype(B16)


def last_scratch(rows):
    return [
        pltpu.VMEM((ZS, rows, 128), B16),
        pltpu.VMEM((ZS - 1, rows, 128), B16),
        pltpu.SemaphoreType.DMA((ZS - 1,)),
        pltpu.SemaphoreType.DMA((ZS - 1,)),
    ]


class Last(Copies):
    def __init__(self, place, scratch):
        self.column, self.from_z = scratch[:2]
        super().__init__(place, *scratch[2:])

    def start(self):
        place = self.place
        self.flying["z"] = [
            self.copy(
                self.column.at[place.z_step(k)],
                self.from_z.at[k - 1],
                place.at(z=place.z_step(k)),
            )
            for k in range(1, ZS)
        ]

    def add(self, out):
        self.wait("z")
        total = self.column[self.place.z].astype(F32)
        for k in range(ZS - 1):
            total += self.from_z[k].astype(F32)
        out[...] = total


def share_scratch():
    half = D // 2
    return [
        pltpu.VMEM((2, half, CELLS), B16),
        pltpu.VMEM((2, half, CELLS), B16),
        pltpu.VMEM((2, half, CELLS), B16),
        pltpu.VMEM((CELLS, D), B16),
        pltpu.VMEM((CELLS, 3 * D), B16),
        pltpu.SemaphoreType.DMA((5,)),
        pltpu.SemaphoreType.DMA((5,)),
    ]


class Share(Copies):
    def __init__(self, place, scratch):
        self.out, self.hidden, self.attended, self.total, self.packed = scratch[:5]
        super().__init__(place, *scratch[5:])

    def give(self, name, src, dst):
        self.flying.setdefault(name, []).append(self.copy(src, dst, self.place.sibling()))

    def give_features(self, name, slot, values, kept):
        core, half = self.place.core, D // 2

        def feature(n):
            m = n & (half - 1)
            owner = jnp.where(n < half, core, 1 - core)
            return ((m >> 5) * CORES + owner) * 32 + (m & 31)

        moved = dot_nt(one_hot(D, D, feature), values).astype(B16)
        kept[0] = moved[0:half]
        self.out[slot] = moved[half:D]
        self.give(name, self.out.at[slot], kept.at[1])


def gather_scratch():
    copies = 2 * (2 * XS - 1)
    return [
        pltpu.VMEM((2 * XS, MERGED, D2), B16),
        pltpu.VMEM((2 * XS, MERGED, D // 2), B16),
        pltpu.VMEM((XS, CORES, MERGED, D // 2), B16),
        pltpu.SemaphoreType.DMA((copies,)),
        pltpu.SemaphoreType.DMA((copies,)),
    ]


class Gather(Copies):
    def __init__(self, place, scratch):
        self.grad, self.hidden, self.hidden_parts = scratch[:3]
        super().__init__(place, *scratch[3:])

    def around(self):
        return [(k, f) for k in range(XS) for f in range(2) if (k, f) != (0, 0)]

    def start_grads(self):
        place = self.place
        self.flying["grads"] = [
            self.copy(self.grad.at[0], self.grad.at[2 * k], place.at(x=place.x_step(k)))
            for k in range(1, XS)
        ]
        self.flying["passed"] = [
            self.copy(self.grad.at[0], self.grad.at[1], place.sibling())
        ]

    def pass_grads(self):
        self.wait("grads")
        for k in range(1, XS):
            self.flying["passed"].append(
                self.copy(self.grad.at[2 * k], self.grad.at[2 * k + 1], self.place.sibling())
            )

    def start_hidden(self, hidden):
        place = self.place
        for x in range(XS):
            for ylo in range(YLO):
                for core in range(CORES):
                    start = ((x * YLO + ylo) * CORES + core) * 128
                    self.hidden_parts[x, core, :, 128 * ylo : 128 * (ylo + 1)] = hidden[
                        :, start : start + 128
                    ]
        self.flying["hidden"] = []
        for k, f in self.around():
            x, core = place.x_step(k), place.core_step(f)
            self.flying["hidden"].append(
                self.copy(
                    self.hidden_parts.at[x, core],
                    self.hidden.at[2 * k + f],
                    place.at(x=x, core=core),
                )
            )
        self.hidden[0] = self.hidden_parts[place.x, place.core]

    def form(self, grads_t, path):
        self.wait("hidden")
        hidden = self.hidden[...].reshape(2 * XS * MERGED, D // 2)

        def body(yhi, carry):
            rows = pl.ds(pl.multiple_of(D * yhi, D), D)
            block = dot(grads_t[rows], hidden).astype(B16)
            for ylo in range(YLO):
                path.sum[ylo, yhi] = block[:, 128 * ylo : 128 * (ylo + 1)]
            return carry

        lax.fori_loop(0, YHI, body, 0)


def iota(shape, dim):
    return lax.broadcasted_iota(jnp.int32, shape, dim)


def one_hot(rows, cols, index):
    place = index(iota((rows, 1), 0))
    return jnp.where(iota((rows, cols), 1) == place, 1.0, 0.0).astype(B16)


def dot(a, b):
    return jnp.dot(a, b, preferred_element_type=F32)


def dot_nt(a, b):
    return lax.dot_general(a, b, (((1,), (1,)), ((), ())), preferred_element_type=F32)


def dot_tn(a, b):
    return lax.dot_general(a, b, (((0,), (0,)), ((), ())), preferred_element_type=F32)


def rows_at(n):
    return n >> 5, n & 31


def rows_index(i, j):
    return i * COLS + j


def merge_at(n):
    part, r, c = n >> 6, (n >> 4) & 3, n & 15
    return 2 * r + (part & 1), 2 * c + (part >> 1)


def merge_index(i, j):
    return (((j & 1) * 2 + (i & 1)) << 6) + ((i >> 1) << 4) + (j >> 1)


def window_at(n):
    return (n >> 3) & 7, ((n >> 6) << 3) + (n & 7)


def window_index(i, j):
    return ((j >> 3) << 6) + (i << 3) + (j & 7)


def fringe_at(n, deep):
    side = n < 64 * deep
    strip = n < 64 * deep + 64
    m = n & 31
    i_side = (n >> 5) + jnp.where(n < 32 * deep, 0, ROWS - 2 * deep)
    i = jnp.where(side, i_side, jnp.where(strip, m >> 2, ((n & 15) >> 2) + 4 * ((n >> 5) & 1)))
    last = jnp.where(strip, (n >> 5) & 1, (n >> 4) & 1)
    j = jnp.where(side, m, (n & 3) + last * (COLS - 4))
    return i, j


def around_index(index, i, j, deep):
    up, down, left, right = i < 0, i >= ROWS, j < 0, j >= COLS
    col4 = jnp.where(left, j + 4, j - COLS)
    north = up | down
    side = north & ~(left | right)
    strip = (left | right) & ~north
    corner = north & (left | right)
    at = index(i, j)
    row = jnp.where(up, i + 2 * deep, i - ROWS)
    at = jnp.where(side, CELLS + row * COLS + j, at)
    at = jnp.where(strip, CELLS + 64 * deep + jnp.where(left, 32, 0) + i * 4 + col4, at)
    base = CELLS + 64 * deep + 64 + jnp.where(up, 32, 0) + jnp.where(left, 16, 0)
    row4 = jnp.where(up, i + 4, i - ROWS)
    return jnp.where(corner, base + row4 * 4 + col4, at)


def normalize(values):
    center = values - jnp.mean(values, axis=-1, keepdims=True)
    inverse = lax.rsqrt(jnp.mean(center * center, axis=-1, keepdims=True) + EPSILON)
    return center * inverse, inverse


def fringe_size(deep):
    return 64 * deep + 128


def fringes(deep):
    rows, base = 32 * deep, 64 * deep
    return (
        (0, rows, -1, 0),
        (rows, rows, 1, 0),
        (base, 32, 0, -1),
        (base + 32, 32, 0, 1),
        (base + 64, 16, -1, -1),
        (base + 80, 16, -1, 1),
        (base + 96, 16, 1, -1),
        (base + 112, 16, 1, 1),
    )


def around_scratch(deep):
    return [
        pltpu.VMEM((CELLS + fringe_size(deep), D), B16),
        pltpu.VMEM((fringe_size(deep), D), B16),
        pltpu.SemaphoreType.DMA((8,)),
        pltpu.SemaphoreType.DMA((8,)),
    ]


class Around(Copies):
    def __init__(self, place, deep, scratch):
        self.block, self.fringe = scratch[:2]
        self.deep = deep
        super().__init__(place, *scratch[2:])

    def pick(self, values, picks):
        self.fringe[...] = dot(picks, values).astype(B16)

    def start(self, values):
        self.flying["fringe"] = [
            self.copy(
                self.fringe.at[pl.ds(offset, size)],
                self.block.at[pl.ds(CELLS + offset, size)],
                self.place.beside(dlat, dlon),
            )
            for offset, size, dlat, dlon in fringes(self.deep)
        ]
        self.block[pl.ds(0, CELLS)] = values

    def get(self, picks):
        self.wait("fringe")
        return dot(picks, self.block[...])


def section_kernel(
    deep,
    shift,
    tokens_hbm,
    skip_grad_hbm,
    merged_grad_hbm,
    w_qkv_hbm,
    w_proj_hbm,
    w_merge_hbm,
    skip_out,
    merged_out,
    input_grad,
    sum_merge,
    sum_fine,
    tokens,
    skip_grad,
    w_qkv,
    w_proj,
    w_merge,
    load,
    to_back,
    to_windows,
    to_output,
    pick_window,
    pick_merge,
    normed,
    packed,
    probs,
    rounded_probs,
    attended,
    window_total,
    packed_grad,
    merged_hidden,
    total_grad,
    grads_t,
    own_part,
    back,
    *scratch,
):
    place = Place()
    partners = place.partners()
    greet(partners)
    rounds = [Around(place, deep, scratch[4 * n : 4 * n + 4]) for n in range(4)]
    scratch = scratch[16:]
    factors = Gather(place, scratch[:5])
    merge_sum = PathXY(place, scratch[5:9])
    proj_sum = PathXY(place, scratch[9:15])
    qkv_sums = PathXY(place, scratch[15:21]), PathYX(place, scratch[21:27])
    merge_last = Last(place, scratch[27:31])
    fine_last = Last(place, scratch[31:35])
    share = Share(place, scratch[35:42])
    merged_grad = factors.grad.at[0]
    loads = {}
    for n, (name, src, dst) in enumerate(
        (
            ("tokens", tokens_hbm, tokens),
            ("merged_grad", merged_grad_hbm, merged_grad),
            ("w_qkv", w_qkv_hbm, w_qkv),
            ("skip_grad", skip_grad_hbm, skip_grad),
            ("w_proj", w_proj_hbm, w_proj),
            ("w_merge", w_merge_hbm, w_merge),
        )
    ):
        loads[name] = pltpu.make_async_copy(src, dst, load.at[n])
        loads[name].start()

    a, b = shift[0], shift[1]
    down = jnp.where(a >= WIN // 2, a - WIN, a)
    right = jnp.where(b >= WIN // 2, b - WIN, b)

    def picker(index):
        return one_hot(fringe_size(deep), CELLS, lambda n: index(*fringe_at(n, deep)))

    def shifted(at, index, sign):
        def source(n):
            i, j = at(n)
            return around_index(index, i + sign * down, j + sign * right, deep)

        return one_hot(CELLS, CELLS + fringe_size(deep), source)

    from_tokens = shifted(window_at, rows_index, 1)
    pick_tokens = picker(rows_index)
    loads["tokens"].wait()
    rounds[0].pick(tokens[...], pick_tokens)
    await_greetings(partners)
    rounds[0].start(tokens[...])
    loads["merged_grad"].wait()
    factors.start_grads()

    to_back[...] = shifted(merge_at, window_index, -1)
    to_windows[...] = shifted(window_at, merge_index, 1)
    to_output[...] = shifted(rows_at, window_index, -1)
    pick_window[...] = picker(window_index)
    pick_merge[...] = picker(merge_index)
    to_merged = one_hot(CELLS, CELLS, lambda n: rows_index(*merge_at(n)))
    to_rows = one_hot(CELLS, CELLS, lambda n: merge_index(*rows_at(n)))
    own_tokens = dot(to_merged, tokens[...])
    loads["skip_grad"].wait()
    own_skip = dot(to_merged, skip_grad[...])
    loads["w_qkv"].wait()

    values, inverse = normalize(rounds[0].get(from_tokens))
    normed[...] = values
    hidden = values.astype(B16)

    def project(n, carry):
        columns = pl.ds(pl.multiple_of(D * n, D), D)
        packed[:, columns] = dot(hidden, w_qkv[:, columns]).astype(B16)
        return carry

    lax.fori_loop(0, 3, project, 0)

    head_mask = (iota((4 * 64, 128), 0) >> 6) == (iota((4 * 64, 128), 1) >> 5)
    head_one = jnp.where(head_mask, 1.0, 0.0)
    head_b16 = head_one.astype(B16)

    def expand(values):
        return jnp.concatenate([values] * 4, axis=0) * head_b16

    def fold(values):
        kept = values * head_one
        return (kept[0:64] + kept[64:128]) + (kept[128:192] + kept[192:256])

    def lanes(n, g):
        return pl.ds(D * n + 128 * g, 128)

    key_row = down + ((iota((64, 1), 0) >> 3) & 7)
    query_row = down + ((iota((1, 256), 1) >> 3) & 7)
    key_away = (key_row < 0) | (key_row >= ROWS)
    query_away = (query_row < 0) | (query_row >= ROWS)
    pole = place.lat == jnp.where(a >= WIN // 2, 0, YHI * ZS - 1)
    apart = jnp.where(key_away, 1, 0) != jnp.where(query_away, 1, 0)
    bias = jnp.where(apart, jnp.where(pole, NEGATIVE, 0.0), 0.0)

    def forward(w, carry):
        rows = pl.ds(pl.multiple_of(w * 64, 64), 64)
        for g in range(4):
            queries = expand(packed[rows, lanes(0, g)])
            scores = dot_nt(packed[rows, lanes(1, g)], queries) * (FACTOR * LOG2E) + bias
            raised = jnp.exp2(scores - jnp.max(scores, axis=0, keepdims=True))
            prob = raised * (1.0 / jnp.sum(raised, axis=0, keepdims=True))
            rounded = prob.astype(B16)
            probs[w, g] = prob
            rounded_probs[w, g] = rounded
            output = dot_tn(rounded, packed[rows, lanes(2, g)])
            attended[rows, pl.ds(128 * g, 128)] = fold(output).astype(B16)
        return carry

    lax.fori_loop(0, WINDOWS, forward, 0, unroll=2)
    rounds[1].pick(attended[...], pick_window[...])
    rounds[1].start(attended[...])

    loads["w_proj"].wait()
    loads["w_merge"].wait()

    def merge_back(part, carry):
        rows = pl.ds(pl.multiple_of(D * part, D), D)
        back[part] = dot_nt(merged_grad[...], w_merge[rows])
        return carry

    lax.fori_loop(0, 4, merge_back, 0)
    share.give_features("hidden", 0, hidden, share.hidden)
    share.give_features("attended", 1, attended[...], share.attended)
    factors.pass_grads()

    own_attended = rounds[1].get(to_back[...]).astype(B16)
    merged_back = [back[part] for part in range(4)]
    own_out = (own_tokens + dot(own_attended, w_proj[...])).astype(B16)
    merged_in = own_out.astype(F32)
    quarters = [merged_in[MERGED * n : MERGED * (n + 1)] for n in range(4)]
    wide = 1.0 / (4 * D)

    def mean(values):
        return sum(jnp.sum(v, axis=-1, keepdims=True) for v in values) * wide

    center_at = mean(quarters)
    centers = [q - center_at for q in quarters]
    merged_inverse = lax.rsqrt(mean([c * c for c in centers]) + EPSILON)
    merged_normed = [c * merged_inverse for c in centers]
    back_mean = mean(merged_back)
    back_dot = mean([g * n for g, n in zip(merged_back, merged_normed)])
    for n in range(4):
        rows = pl.ds(MERGED * n, MERGED)
        merged_hidden[:, pl.ds(D * n, D)] = merged_normed[n].astype(B16)
        delta = merged_inverse * (merged_back[n] - back_mean - merged_normed[n] * back_dot)
        total_grad[rows] = (own_skip[MERGED * n : MERGED * (n + 1)] + delta).astype(B16)
    rounds[2].pick(total_grad[...], pick_merge[...])
    rounds[2].start(total_grad[...])
    factors.start_hidden(merged_hidden)

    skip_out[...] = dot(to_rows, own_out).astype(B16)
    merged_out[...] = dot(merged_hidden[...], w_merge[...]).astype(B16)
    factors.wait("passed")
    grads_t[...] = factors.grad[...].reshape(2 * XS * MERGED, D2).T

    window_total[...] = rounds[2].get(to_windows[...]).astype(B16)
    share.give("total", window_total, share.total)
    attended[...] = dot_nt(window_total[...], w_proj[...]).astype(B16)

    def backward(w, carry):
        rows = pl.ds(pl.multiple_of(w * 64, 64), 64)
        for g in range(4):
            queries = expand(packed[rows, lanes(0, g)])
            upstream = expand(attended[rows, pl.ds(128 * g, 128)])
            key_rows, value_rows = packed[rows, lanes(1, g)], packed[rows, lanes(2, g)]
            prob = probs[w, g]
            prob_grad = dot_nt(value_rows, upstream)
            total = jnp.sum(prob * prob_grad, axis=0, keepdims=True)
            score_grad = (prob * (prob_grad - total) * FACTOR).astype(B16)
            packed_grad[rows, lanes(0, g)] = fold(dot_tn(score_grad, key_rows)).astype(B16)
            packed_grad[rows, lanes(1, g)] = dot(score_grad, queries).astype(B16)
            packed_grad[rows, lanes(2, g)] = dot(rounded_probs[w, g], upstream).astype(B16)
        return carry

    def give_packed(part):
        rows = pl.ds(CELLS // 2 * part, CELLS // 2)
        share.give("packed", packed_grad.at[rows], share.packed.at[rows])

    def give_packed(part):
        rows = pl.ds(CELLS // 2 * part, CELLS // 2)
        share.give("packed", packed_grad.at[rows], share.packed.at[rows])

    factors.form(grads_t, merge_sum)
    merge_sum.start_second()
    lax.fori_loop(0, WINDOWS // 2, backward, 0, unroll=2)
    give_packed(0)
    share.wait("attended")
    share.wait("total")
    block = dot(share.attended[0], window_total[...]) + dot(share.attended[1], share.total[...])
    block = block.astype(B16)
    for yhi in range(YHI):
        for h in range(2):
            start = 256 * yhi + 128 * h
            proj_sum.parts[:, :, yhi, pl.ds(32 * h, 32)] = block[:, start : start + 128].reshape(
                XS, YLO, 32, 128
            )
    proj_sum.start_first()
    lax.fori_loop(WINDOWS // 2, WINDOWS, backward, 0, unroll=2)
    give_packed(1)

    share.wait("hidden")

    def form_own(n, carry):
        columns = pl.ds(pl.multiple_of(D * n, D), D)
        own_part[:, columns] = dot(share.hidden[0], packed_grad[:, columns])
        return carry

    lax.fori_loop(0, 3, form_own, 0)
    share.wait("packed")
    for h in range(2):

        def form_both(yhi, carry):
            columns = pl.ds(pl.multiple_of(768 * yhi + 384 * h, 128), 384)
            block = own_part[:, columns] + dot(share.hidden[1], share.packed[:, columns])
            block = block.astype(B16)
            for m in range(3):
                qkv_sums[h].parts[:, :, yhi, pl.ds(32 * m, 32)] = block[
                    :, 128 * m : 128 * (m + 1)
                ].reshape(XS, YLO, 32, 128)
            return carry

        lax.fori_loop(0, YHI, form_both, 0)
        qkv_sums[h].start_first()
    proj_sum.add_first()
    proj_sum.start_second()
    merge_last.column[...] = merge_sum.add_second().reshape(ZS, 64, 128)
    merge_last.start()

    hidden_grad = dot_nt(packed_grad[...], w_qkv[...])
    window_input = window_total[...].astype(F32) + inverse * (
        hidden_grad
        - jnp.mean(hidden_grad, axis=-1, keepdims=True)
        - normed[...] * jnp.mean(hidden_grad * normed[...], axis=-1, keepdims=True)
    )
    window_input = window_input.astype(B16)
    rounds[3].pick(window_input, pick_window[...])

    widen_fine = one_hot(384, 512, lambda n: (n // 96) * 128 + n % 96)
    widen_proj = one_hot(128, 512, lambda n: (n >> 5) * 128 + 96 + (n & 31))
    for path in qkv_sums:
        path.add_first()
        path.start_second()
    rounds[3].start(window_input)
    proj_total = proj_sum.add_second()
    proj_wide = [dot(proj_total[32 * h : 32 * (h + 1)], widen_proj) for h in range(2)]
    for h, path in enumerate(qkv_sums):
        total = path.add_second()
        wide_rows = jnp.concatenate([total[32 * m : 32 * (m + 1)] for m in range(3)], axis=1)
        block = (dot(wide_rows, widen_fine) + proj_wide[h]).astype(B16)
        for m in range(HALF):
            fine_last.column[HALF * h + m] = block[:, 128 * m : 128 * (m + 1)]
    fine_last.start()
    merge_last.add(sum_merge)
    input_grad[...] = rounds[3].get(to_output[...]).astype(B16)
    fine_last.add(sum_fine)


def finish_kernel(sum_merge, sum_fine, *refs):
    for src, dst in zip(refs[:3], refs[3:6]):
        dst[...] = src[...]
    dw_qkv, dw_proj, dw_merge = refs[6:]
    dw_qkv[...] = sum_fine[:, 0:96]
    dw_proj[...] = sum_fine[:, 96:128]
    dw_merge[...] = sum_merge[...]


def section(deep, *args):
    vmem, smem = pltpu.VMEM, pltpu.SMEM
    inside = pl.BlockSpec(memory_space=vmem)
    outside = pl.BlockSpec(memory_space=pl.ANY)
    shape = jax.ShapeDtypeStruct
    big = [shape((CELLS, D), B16), shape((MERGED, D2), B16), shape((CELLS, D), B16)]
    fringe = fringe_size(deep)
    return pl.pallas_call(
        functools.partial(section_kernel, deep),
        out_shape=big + [shape((64, 128), F32), shape((32, 128), F32)],
        in_specs=[pl.BlockSpec(memory_space=smem)] + [outside] * 6,
        out_specs=[inside] * 5,
        scratch_shapes=[
            vmem((CELLS, D), B16),
            vmem((CELLS, D), B16),
            vmem((D, 3 * D), B16),
            vmem((D, D), B16),
            vmem((4 * D, D2), B16),
            pltpu.SemaphoreType.DMA((6,)),
            vmem((CELLS, CELLS + fringe), B16),
            vmem((CELLS, CELLS + fringe), B16),
            vmem((CELLS, CELLS + fringe), B16),
            vmem((fringe, CELLS), B16),
            vmem((fringe, CELLS), B16),
            vmem((CELLS, D), F32),
            vmem((CELLS, 3 * D), B16),
            vmem((WINDOWS, 4, 64, 256), F32),
            vmem((WINDOWS, 4, 64, 256), B16),
            vmem((CELLS, D), B16),
            vmem((CELLS, D), B16),
            vmem((CELLS, 3 * D), B16),
            vmem((MERGED, 4 * D), B16),
            vmem((CELLS, D), B16),
            vmem((D2, 2 * XS * MERGED), B16),
            vmem((D // 2, 3 * D), F32),
            vmem((4, MERGED, D), F32),
        ]
        + around_scratch(deep) * 4
        + gather_scratch()
        + path_scratch(512, (False, 1), (YLO, YHI))
        + path_scratch(64, (True, XS), (YLO, YHI))
        + path_scratch(96, (True, XS), (YLO, YHI))
        + path_scratch(96, (True, YS), (XS,))
        + last_scratch(64)
        + last_scratch(32)
        + share_scratch(),
        compiler_params=pltpu.CompilerParams(
            collective_id=deep, has_side_effects=True, vmem_limit_bytes=56 * 2**20
        ),
    )(*args)


def on_device(tokens, w_qkv, w_proj, w_merge, skip_grad, merged_grad, window_shift):
    inside = pl.BlockSpec(memory_space=pltpu.VMEM)
    shape = jax.ShapeDtypeStruct
    big = [shape((CELLS, D), B16), shape((MERGED, D2), B16), shape((CELLS, D), B16)]
    args = (
        window_shift,
        tokens.reshape(CELLS, D),
        skip_grad.reshape(CELLS, D),
        merged_grad.reshape(MERGED, D2),
        w_qkv,
        w_proj,
        w_merge,
    )
    shift = window_shift[0]
    rows = jnp.minimum(shift, WIN - shift)
    skip_out, merged_out, input_grad, sum_merge, sum_fine = lax.switch(
        jnp.minimum(rows, 3) - 1, [functools.partial(section, deep) for deep in (1, 2, 4)], *args
    )
    skip_out, merged_out, input_grad, dw_qkv, dw_proj, dw_merge = pl.pallas_call(
        finish_kernel,
        out_shape=big + [shape((32, 96), F32), shape((32, 32), F32), shape((64, 128), F32)],
        in_specs=[inside] * 5,
        out_specs=[inside] * 6,
    )(sum_merge, sum_fine, skip_out, merged_out, input_grad)
    return (
        skip_out.reshape(ROWS, COLS, D),
        merged_out.reshape(ROWS // 2, COLS // 2, D2),
        input_grad.reshape(ROWS, COLS, D),
        dw_qkv,
        dw_proj,
        dw_merge.T,
    )


def solution(mesh):
    in_specs = (
        P("lat", "lon", None),
        P(),
        P(),
        P(),
        P("lat", "lon", None),
        P("lat", "lon", None),
        P(),
    )
    out_specs = (
        P("lat", "lon", None),
        P("lat", "lon", None),
        P("lat", "lon", None),
        P("lon", "lat"),
        P("lon", "lat"),
        P("lon", "lat"),
    )
    return jax.shard_map(
        on_device, mesh=mesh, in_specs=in_specs, out_specs=out_specs, check_vma=False
    )
```

```python
import functools

import jax
import jax.numpy as jnp
from jax import lax
from jax.experimental import pallas as pl
from jax.experimental.pallas import tpu as pltpu
from jax.sharding import PartitionSpec as P

HEADS = 16
WIN = 8
EPSILON = 1e-05
NEGATIVE = -1e30
D = 512
D2 = 1024
ROWS, COLS = 8, 32
CELLS = ROWS * COLS
WINDOWS = COLS // WIN
FACTOR = 32 ** (-0.5)
LOG2E = 1.4426950408889634
MERGED = CELLS // 4
F32, B16 = jnp.float32, jnp.bfloat16

XS, YLO, CORES, YHI, ZS = 4, 2, 2, 2, 8
YS = YLO * YHI
MESH = pl.DeviceIdType.MESH


class Place:
    def __init__(self):
        lon = lax.axis_index("lon")
        lat = lax.axis_index("lat")
        self.lon, self.lat = lon, lat
        self.core = lon % CORES
        self.ylo = (lon // CORES) % YLO
        self.x = lon // (CORES * YLO)
        self.z = lat % ZS
        self.yhi = lat // ZS

    def at(self, x=None, ylo=None, core=None, yhi=None, z=None):
        x = self.x if x is None else x
        ylo = self.ylo if ylo is None else ylo
        core = self.core if core is None else core
        yhi = self.yhi if yhi is None else yhi
        z = self.z if z is None else z
        return ((x * YLO + ylo) * CORES + core, yhi * ZS + z)

    def beside(self, dlat, dlon):
        lons, lats = XS * YLO * CORES, YHI * ZS
        return ((self.lon + dlon) % lons, (self.lat + dlat) % lats)

    def sibling(self):
        return self.at(core=1 - self.core)

    def x_step(self, k):
        return (self.x + k) % XS

    def y_step(self, k):
        y = (self.yhi * YLO + self.ylo + k) % YS
        return (y // YLO, y % YLO)

    def z_step(self, k):
        return (self.z + k) % ZS

    def core_step(self, f):
        return 1 - self.core if f else self.core

    def partners(self):
        out = [self.sibling()]
        for k in range(1, XS):
            out += [self.at(x=self.x_step(k), core=self.core_step(f)) for f in range(2)]
        for k in range(1, YS):
            yhi, ylo = self.y_step(k)
            out += [self.at(yhi=yhi, ylo=ylo, core=self.core_step(f)) for f in range(2)]
        out += [self.at(z=self.z_step(k)) for k in range(1, ZS)]
        for dlat in (-1, 0, 1):
            for dlon in (-1, 0, 1):
                if (dlat, dlon) != (0, 0):
                    out.append(self.beside(dlat, dlon))
        return out


def device_of(pair):
    return {"lon": pair[0], "lat": pair[1]}


def greet(partners):
    barrier = pltpu.get_barrier_semaphore()
    for pair in partners:
        pl.semaphore_signal(barrier, inc=1, device_id=device_of(pair), device_id_type=MESH)


def await_greetings(partners):
    pl.semaphore_wait(pltpu.get_barrier_semaphore(), len(partners))


HALF = ZS // 2
FARTHEST_Z = (4, 3, 5, 2, 6, 1, 7)


class Copies:
    def __init__(self, place, send, recv):
        self.place, self.send, self.recv = place, send, recv
        self.used = 0
        self.flying = {}

    def copy(self, src, dst, pair):
        slot = self.used
        self.used += 1
        made = pltpu.make_async_remote_copy(
            src_ref=src,
            dst_ref=dst,
            send_sem=self.send.at[slot],
            recv_sem=self.recv.at[slot],
            device_id=device_of(pair),
            device_id_type=MESH,
        )
        made.start()
        return made

    def wait(self, name):
        for made in self.flying[name]:
            made.wait()


def path_scratch(rows, first, second):
    one, two = first[0], second
    flat = 1
    for size in two:
        flat *= size
    copies = (first[1] - 1) + (flat - 1)
    out = [
        pltpu.VMEM((*two, rows, 128), B16),
        pltpu.VMEM((flat - 1, rows, 128), B16),
        pltpu.SemaphoreType.DMA((copies,)),
        pltpu.SemaphoreType.DMA((copies,)),
    ]
    if one:
        out += [
            pltpu.VMEM((XS, YLO, YHI, rows, 128), B16),
            pltpu.VMEM((first[1] - 1, *two, rows, 128), B16),
        ]
    return out


class PathXY(Copies):
    def __init__(self, place, scratch):
        self.sum, self.late = scratch[:2]
        super().__init__(place, *scratch[2:4])
        if len(scratch) > 4:
            self.parts, self.got = scratch[4:]

    def start_first(self):
        place = self.place
        self.flying["x"] = [
            self.copy(
                self.parts.at[place.x_step(k)], self.got.at[k - 1], place.at(x=place.x_step(k))
            )
            for k in (2, 1, 3)
        ]

    def add_first(self):
        self.wait("x")
        for ylo in range(YLO):
            for yhi in range(YHI):
                total = self.parts[self.place.x, ylo, yhi].astype(F32)
                for k in range(XS - 1):
                    total += self.got[k, ylo, yhi].astype(F32)
                self.sum[ylo, yhi] = total.astype(B16)

    def start_second(self):
        self.flying["y"] = []
        for k in (2, 1, 3):
            yhi, ylo = self.place.y_step(k)
            pair = self.place.at(yhi=yhi, ylo=ylo)
            self.flying["y"].append(self.copy(self.sum.at[ylo, yhi], self.late.at[k - 1], pair))

    def add_second(self):
        self.wait("y")
        total = self.sum[self.place.ylo, self.place.yhi].astype(F32)
        for k in range(YS - 1):
            total += self.late[k].astype(F32)
        return total.astype(B16)


class PathYX(Copies):
    def __init__(self, place, scratch):
        self.sum, self.late = scratch[:2]
        super().__init__(place, *scratch[2:4])
        self.parts, self.got = scratch[4:]

    def start_first(self):
        self.flying["y"] = []
        for k in (2, 1, 3):
            yhi, ylo = self.place.y_step(k)
            pair = self.place.at(yhi=yhi, ylo=ylo)
            self.flying["y"].append(
                self.copy(self.parts.at[:, ylo, yhi], self.got.at[k - 1], pair)
            )

    def add_first(self):
        self.wait("y")
        for x in range(XS):
            total = self.parts[x, self.place.ylo, self.place.yhi].astype(F32)
            for k in range(YS - 1):
                total += self.got[k, x].astype(F32)
            self.sum[x] = total.astype(B16)

    def start_second(self):
        place = self.place
        self.flying["x"] = [
            self.copy(
                self.sum.at[place.x_step(k)], self.late.at[k - 1], place.at(x=place.x_step(k))
            )
            for k in (2, 1, 3)
        ]

    def add_second(self):
        self.wait("x")
        total = self.sum[self.place.x].astype(F32)
        for k in range(XS - 1):
            total += self.late[k].astype(F32)
        return total.astype(B16)


def last_scratch(rows):
    return [
        pltpu.VMEM((ZS, rows, 128), B16),
        pltpu.VMEM((ZS - 1, rows, 128), B16),
        pltpu.SemaphoreType.DMA((ZS - 1,)),
        pltpu.SemaphoreType.DMA((ZS - 1,)),
    ]


class Last(Copies):
    def __init__(self, place, scratch):
        self.column, self.from_z = scratch[:2]
        super().__init__(place, *scratch[2:])

    def start(self):
        place = self.place
        self.flying["z"] = [
            self.copy(
                self.column.at[place.z_step(k)],
                self.from_z.at[k - 1],
                place.at(z=place.z_step(k)),
            )
            for k in FARTHEST_Z
        ]

    def add(self, out):
        self.wait("z")
        total = self.column[self.place.z].astype(F32)
        for k in range(ZS - 1):
            total += self.from_z[k].astype(F32)
        out[...] = total


def share_scratch():
    half = D // 2
    return [
        pltpu.VMEM((2, half, CELLS), B16),
        pltpu.VMEM((2, half, CELLS), B16),
        pltpu.VMEM((2, half, CELLS), B16),
        pltpu.VMEM((CELLS, D), B16),
        pltpu.VMEM((CELLS, 3 * D), B16),
        pltpu.SemaphoreType.DMA((5,)),
        pltpu.SemaphoreType.DMA((5,)),
    ]


class Share(Copies):
    def __init__(self, place, scratch):
        self.out, self.hidden, self.attended, self.total, self.packed = scratch[:5]
        super().__init__(place, *scratch[5:])

    def give(self, name, src, dst):
        self.flying.setdefault(name, []).append(self.copy(src, dst, self.place.sibling()))

    def give_features(self, name, slot, values, kept):
        core, half = self.place.core, D // 2

        def feature(n):
            m = n & (half - 1)
            owner = jnp.where(n < half, core, 1 - core)
            return ((m >> 5) * CORES + owner) * 32 + (m & 31)

        moved = dot_nt(one_hot(D, D, feature), values).astype(B16)
        kept[0] = moved[0:half]
        self.out[slot] = moved[half:D]
        self.give(name, self.out.at[slot], kept.at[1])


def gather_scratch():
    copies = 2 * (2 * XS - 1)
    return [
        pltpu.VMEM((2 * XS, MERGED, D2), B16),
        pltpu.VMEM((2 * XS, MERGED, D // 2), B16),
        pltpu.VMEM((XS, CORES, MERGED, D // 2), B16),
        pltpu.SemaphoreType.DMA((copies,)),
        pltpu.SemaphoreType.DMA((copies,)),
    ]


class Gather(Copies):
    def __init__(self, place, scratch):
        self.grad, self.hidden, self.hidden_parts = scratch[:3]
        super().__init__(place, *scratch[3:])

    def around(self):
        return [(k, f) for k in range(XS) for f in range(2) if (k, f) != (0, 0)]

    def start_grads(self):
        place = self.place
        self.flying["grads"] = [
            self.copy(self.grad.at[0], self.grad.at[2 * k], place.at(x=place.x_step(k)))
            for k in range(1, XS)
        ]
        self.flying["passed"] = [
            self.copy(self.grad.at[0], self.grad.at[1], place.sibling())
        ]

    def pass_grads(self):
        self.wait("grads")
        for k in range(1, XS):
            self.flying["passed"].append(
                self.copy(self.grad.at[2 * k], self.grad.at[2 * k + 1], self.place.sibling())
            )

    def start_hidden(self, hidden):
        place = self.place
        for x in range(XS):
            for ylo in range(YLO):
                for core in range(CORES):
                    start = ((x * YLO + ylo) * CORES + core) * 128
                    self.hidden_parts[x, core, :, 128 * ylo : 128 * (ylo + 1)] = hidden[
                        :, start : start + 128
                    ]
        self.flying["hidden"] = []
        for k, f in self.around():
            x, core = place.x_step(k), place.core_step(f)
            self.flying["hidden"].append(
                self.copy(
                    self.hidden_parts.at[x, core],
                    self.hidden.at[2 * k + f],
                    place.at(x=x, core=core),
                )
            )
        self.hidden[0] = self.hidden_parts[place.x, place.core]

    def form(self, grads_t, path):
        self.wait("hidden")
        hidden = self.hidden[...].reshape(2 * XS * MERGED, D // 2)

        def body(yhi, carry):
            rows = pl.ds(pl.multiple_of(D * yhi, D), D)
            block = dot(grads_t[rows], hidden).astype(B16)
            for ylo in range(YLO):
                path.sum[ylo, yhi] = block[:, 128 * ylo : 128 * (ylo + 1)]
            return carry

        lax.fori_loop(0, YHI, body, 0)


def iota(shape, dim):
    return lax.broadcasted_iota(jnp.int32, shape, dim)


def one_hot(rows, cols, index):
    place = index(iota((rows, 1), 0))
    return jnp.where(iota((rows, cols), 1) == place, 1.0, 0.0).astype(B16)


def dot(a, b):
    return jnp.dot(a, b, preferred_element_type=F32)


def dot_nt(a, b):
    return lax.dot_general(a, b, (((1,), (1,)), ((), ())), preferred_element_type=F32)


def dot_tn(a, b):
    return lax.dot_general(a, b, (((0,), (0,)), ((), ())), preferred_element_type=F32)


def rows_at(n):
    return n >> 5, n & 31


def rows_index(i, j):
    return i * COLS + j


def merge_at(n):
    part, r, c = n >> 6, (n >> 4) & 3, n & 15
    return 2 * r + (part & 1), 2 * c + (part >> 1)


def merge_index(i, j):
    return (((j & 1) * 2 + (i & 1)) << 6) + ((i >> 1) << 4) + (j >> 1)


def window_at(n):
    return (n >> 3) & 7, ((n >> 6) << 3) + (n & 7)


def window_index(i, j):
    return ((j >> 3) << 6) + (i << 3) + (j & 7)


def fringe_at(n, deep):
    side = n < 64 * deep
    strip = n < 64 * deep + 64
    m = n & 31
    i_side = (n >> 5) + jnp.where(n < 32 * deep, 0, ROWS - 2 * deep)
    i = jnp.where(side, i_side, jnp.where(strip, m >> 2, ((n & 15) >> 2) + 4 * ((n >> 5) & 1)))
    last = jnp.where(strip, (n >> 5) & 1, (n >> 4) & 1)
    j = jnp.where(side, m, (n & 3) + last * (COLS - 4))
    return i, j


def around_index(index, i, j, deep):
    up, down, left, right = i < 0, i >= ROWS, j < 0, j >= COLS
    col4 = jnp.where(left, j + 4, j - COLS)
    north = up | down
    side = north & ~(left | right)
    strip = (left | right) & ~north
    corner = north & (left | right)
    at = index(i, j)
    row = jnp.where(up, i + 2 * deep, i - ROWS)
    at = jnp.where(side, CELLS + row * COLS + j, at)
    at = jnp.where(strip, CELLS + 64 * deep + jnp.where(left, 32, 0) + i * 4 + col4, at)
    base = CELLS + 64 * deep + 64 + jnp.where(up, 32, 0) + jnp.where(left, 16, 0)
    row4 = jnp.where(up, i + 4, i - ROWS)
    return jnp.where(corner, base + row4 * 4 + col4, at)


def normalize(values):
    center = values - jnp.mean(values, axis=-1, keepdims=True)
    inverse = lax.rsqrt(jnp.mean(center * center, axis=-1, keepdims=True) + EPSILON)
    return center * inverse, inverse


def fringe_size(deep):
    return 64 * deep + 128


def fringes(deep):
    rows, base = 32 * deep, 64 * deep
    return (
        (0, rows, -1, 0),
        (rows, rows, 1, 0),
        (base, 32, 0, -1),
        (base + 32, 32, 0, 1),
        (base + 64, 16, -1, -1),
        (base + 80, 16, -1, 1),
        (base + 96, 16, 1, -1),
        (base + 112, 16, 1, 1),
    )


def around_scratch(deep):
    return [
        pltpu.VMEM((CELLS + fringe_size(deep), D), B16),
        pltpu.VMEM((fringe_size(deep), D), B16),
        pltpu.SemaphoreType.DMA((8,)),
        pltpu.SemaphoreType.DMA((8,)),
    ]


class Around(Copies):
    def __init__(self, place, deep, scratch):
        self.block, self.fringe = scratch[:2]
        self.deep = deep
        super().__init__(place, *scratch[2:])

    def pick(self, values, picks):
        self.fringe[...] = dot(picks, values).astype(B16)

    def start(self, values):
        self.flying["fringe"] = [
            self.copy(
                self.fringe.at[pl.ds(offset, size)],
                self.block.at[pl.ds(CELLS + offset, size)],
                self.place.beside(dlat, dlon),
            )
            for offset, size, dlat, dlon in fringes(self.deep)
        ]
        self.block[pl.ds(0, CELLS)] = values

    def get(self, picks):
        self.wait("fringe")
        return dot(picks, self.block[...])


def section_kernel(
    deep,
    shift,
    tokens_hbm,
    skip_grad_hbm,
    merged_grad_hbm,
    w_qkv_hbm,
    w_proj_hbm,
    w_merge_hbm,
    skip_out,
    merged_out,
    input_grad,
    sum_merge,
    sum_fine,
    tokens,
    skip_grad,
    w_qkv,
    w_proj,
    w_merge,
    load,
    to_back,
    to_windows,
    to_output,
    pick_window,
    pick_merge,
    normed,
    packed,
    probs,
    rounded_probs,
    attended,
    window_total,
    packed_grad,
    merged_hidden,
    total_grad,
    grads_t,
    own_part,
    back,
    *scratch,
):
    place = Place()
    partners = place.partners()
    greet(partners)
    rounds = [Around(place, deep, scratch[4 * n : 4 * n + 4]) for n in range(4)]
    scratch = scratch[16:]
    factors = Gather(place, scratch[:5])
    merge_sum = PathXY(place, scratch[5:9])
    proj_sum = PathXY(place, scratch[9:15])
    qkv_sums = PathXY(place, scratch[15:21]), PathYX(place, scratch[21:27])
    merge_last = Last(place, scratch[27:31])
    fine_last = Last(place, scratch[31:35])
    share = Share(place, scratch[35:42])
    merged_grad = factors.grad.at[0]
    loads = {}
    for n, (name, src, dst) in enumerate(
        (
            ("tokens", tokens_hbm, tokens),
            ("merged_grad", merged_grad_hbm, merged_grad),
            ("w_qkv", w_qkv_hbm, w_qkv),
            ("skip_grad", skip_grad_hbm, skip_grad),
            ("w_proj", w_proj_hbm, w_proj),
            ("w_merge", w_merge_hbm, w_merge),
        )
    ):
        loads[name] = pltpu.make_async_copy(src, dst, load.at[n])
        loads[name].start()

    a, b = shift[0], shift[1]
    down = jnp.where(a >= WIN // 2, a - WIN, a)
    right = jnp.where(b >= WIN // 2, b - WIN, b)

    def picker(index):
        return one_hot(fringe_size(deep), CELLS, lambda n: index(*fringe_at(n, deep)))

    def shifted(at, index, sign):
        def source(n):
            i, j = at(n)
            return around_index(index, i + sign * down, j + sign * right, deep)

        return one_hot(CELLS, CELLS + fringe_size(deep), source)

    from_tokens = shifted(window_at, rows_index, 1)
    pick_tokens = picker(rows_index)
    loads["tokens"].wait()
    rounds[0].pick(tokens[...], pick_tokens)
    await_greetings(partners)
    rounds[0].start(tokens[...])
    loads["merged_grad"].wait()
    factors.start_grads()

    to_back[...] = shifted(merge_at, window_index, -1)
    to_windows[...] = shifted(window_at, merge_index, 1)
    to_output[...] = shifted(rows_at, window_index, -1)
    pick_window[...] = picker(window_index)
    pick_merge[...] = picker(merge_index)
    to_merged = one_hot(CELLS, CELLS, lambda n: rows_index(*merge_at(n)))
    to_rows = one_hot(CELLS, CELLS, lambda n: merge_index(*rows_at(n)))
    own_tokens = dot(to_merged, tokens[...])
    loads["skip_grad"].wait()
    own_skip = dot(to_merged, skip_grad[...])
    loads["w_qkv"].wait()

    values, inverse = normalize(rounds[0].get(from_tokens))
    normed[...] = values
    hidden = values.astype(B16)

    def project(n, carry):
        columns = pl.ds(pl.multiple_of(D * n, D), D)
        packed[:, columns] = dot(hidden, w_qkv[:, columns]).astype(B16)
        return carry

    lax.fori_loop(0, 3, project, 0)

    head_mask = (iota((4 * 64, 128), 0) >> 6) == (iota((4 * 64, 128), 1) >> 5)
    head_one = jnp.where(head_mask, 1.0, 0.0)
    head_b16 = head_one.astype(B16)

    def expand(values):
        return jnp.concatenate([values] * 4, axis=0) * head_b16

    def fold(values):
        kept = values * head_one
        return (kept[0:64] + kept[64:128]) + (kept[128:192] + kept[192:256])

    def lanes(n, g):
        return pl.ds(D * n + 128 * g, 128)

    key_row = down + ((iota((64, 1), 0) >> 3) & 7)
    query_row = down + ((iota((1, 256), 1) >> 3) & 7)
    key_away = (key_row < 0) | (key_row >= ROWS)
    query_away = (query_row < 0) | (query_row >= ROWS)
    pole = place.lat == jnp.where(a >= WIN // 2, 0, YHI * ZS - 1)
    apart = jnp.where(key_away, 1, 0) != jnp.where(query_away, 1, 0)
    bias = jnp.where(apart, jnp.where(pole, NEGATIVE, 0.0), 0.0)

    def forward(w, carry):
        rows = pl.ds(pl.multiple_of(w * 64, 64), 64)
        for g in range(4):
            queries = expand(packed[rows, lanes(0, g)])
            scores = dot_nt(packed[rows, lanes(1, g)], queries) * (FACTOR * LOG2E) + bias
            raised = jnp.exp2(scores - jnp.max(scores, axis=0, keepdims=True))
            prob = raised * (1.0 / jnp.sum(raised, axis=0, keepdims=True))
            rounded = prob.astype(B16)
            probs[w, g] = prob
            rounded_probs[w, g] = rounded
            output = dot_tn(rounded, packed[rows, lanes(2, g)])
            attended[rows, pl.ds(128 * g, 128)] = fold(output).astype(B16)
        return carry

    lax.fori_loop(0, WINDOWS, forward, 0, unroll=2)
    rounds[1].pick(attended[...], pick_window[...])
    rounds[1].start(attended[...])

    loads["w_proj"].wait()
    loads["w_merge"].wait()

    def merge_back(part, carry):
        rows = pl.ds(pl.multiple_of(D * part, D), D)
        back[part] = dot_nt(merged_grad[...], w_merge[rows])
        return carry

    lax.fori_loop(0, 4, merge_back, 0)
    share.give_features("hidden", 0, hidden, share.hidden)
    share.give_features("attended", 1, attended[...], share.attended)
    factors.pass_grads()

    own_attended = rounds[1].get(to_back[...]).astype(B16)
    merged_back = [back[part] for part in range(4)]
    own_out = (own_tokens + dot(own_attended, w_proj[...])).astype(B16)
    merged_in = own_out.astype(F32)
    quarters = [merged_in[MERGED * n : MERGED * (n + 1)] for n in range(4)]
    wide = 1.0 / (4 * D)

    def mean(values):
        return sum(jnp.sum(v, axis=-1, keepdims=True) for v in values) * wide

    center_at = mean(quarters)
    centers = [q - center_at for q in quarters]
    merged_inverse = lax.rsqrt(mean([c * c for c in centers]) + EPSILON)
    merged_normed = [c * merged_inverse for c in centers]
    back_mean = mean(merged_back)
    back_dot = mean([g * n for g, n in zip(merged_back, merged_normed)])
    for n in range(4):
        rows = pl.ds(MERGED * n, MERGED)
        merged_hidden[:, pl.ds(D * n, D)] = merged_normed[n].astype(B16)
        delta = merged_inverse * (merged_back[n] - back_mean - merged_normed[n] * back_dot)
        total_grad[rows] = (own_skip[MERGED * n : MERGED * (n + 1)] + delta).astype(B16)
    rounds[2].pick(total_grad[...], pick_merge[...])
    rounds[2].start(total_grad[...])
    factors.start_hidden(merged_hidden)

    skip_out[...] = dot(to_rows, own_out).astype(B16)
    merged_out[...] = dot(merged_hidden[...], w_merge[...]).astype(B16)
    factors.wait("passed")
    grads_t[...] = factors.grad[...].reshape(2 * XS * MERGED, D2).T

    window_total[...] = rounds[2].get(to_windows[...]).astype(B16)
    share.give("total", window_total, share.total)
    attended[...] = dot_nt(window_total[...], w_proj[...]).astype(B16)

    def backward(w, carry):
        rows = pl.ds(pl.multiple_of(w * 64, 64), 64)
        for g in range(4):
            queries = expand(packed[rows, lanes(0, g)])
            upstream = expand(attended[rows, pl.ds(128 * g, 128)])
            key_rows, value_rows = packed[rows, lanes(1, g)], packed[rows, lanes(2, g)]
            prob = probs[w, g]
            prob_grad = dot_nt(value_rows, upstream)
            total = jnp.sum(prob * prob_grad, axis=0, keepdims=True)
            score_grad = (prob * (prob_grad - total) * FACTOR).astype(B16)
            packed_grad[rows, lanes(0, g)] = fold(dot_tn(score_grad, key_rows)).astype(B16)
            packed_grad[rows, lanes(1, g)] = dot(score_grad, queries).astype(B16)
            packed_grad[rows, lanes(2, g)] = dot(rounded_probs[w, g], upstream).astype(B16)
        return carry

    def give_packed(part):
        rows = pl.ds(CELLS // 2 * part, CELLS // 2)
        share.give("packed", packed_grad.at[rows], share.packed.at[rows])

    def give_packed(part):
        rows = pl.ds(CELLS // 2 * part, CELLS // 2)
        share.give("packed", packed_grad.at[rows], share.packed.at[rows])

    factors.form(grads_t, merge_sum)
    merge_sum.start_second()
    lax.fori_loop(0, WINDOWS // 2, backward, 0, unroll=2)
    give_packed(0)
    share.wait("attended")
    share.wait("total")
    block = dot(share.attended[0], window_total[...]) + dot(share.attended[1], share.total[...])
    block = block.astype(B16)
    for yhi in range(YHI):
        for h in range(2):
            start = 256 * yhi + 128 * h
            proj_sum.parts[:, :, yhi, pl.ds(32 * h, 32)] = block[:, start : start + 128].reshape(
                XS, YLO, 32, 128
            )
    proj_sum.start_first()
    lax.fori_loop(WINDOWS // 2, WINDOWS, backward, 0, unroll=2)
    give_packed(1)

    share.wait("hidden")

    def form_own(n, carry):
        columns = pl.ds(pl.multiple_of(D * n, D), D)
        own_part[:, columns] = dot(share.hidden[0], packed_grad[:, columns])
        return carry

    lax.fori_loop(0, 3, form_own, 0)
    share.wait("packed")
    for h in range(2):

        def form_both(yhi, carry):
            columns = pl.ds(pl.multiple_of(768 * yhi + 384 * h, 128), 384)
            block = own_part[:, columns] + dot(share.hidden[1], share.packed[:, columns])
            block = block.astype(B16)
            for m in range(3):
                qkv_sums[h].parts[:, :, yhi, pl.ds(32 * m, 32)] = block[
                    :, 128 * m : 128 * (m + 1)
                ].reshape(XS, YLO, 32, 128)
            return carry

        lax.fori_loop(0, YHI, form_both, 0)
        qkv_sums[h].start_first()
    proj_sum.add_first()
    proj_sum.start_second()
    merge_last.column[...] = merge_sum.add_second().reshape(ZS, 64, 128)
    merge_last.start()

    hidden_grad = dot_nt(packed_grad[...], w_qkv[...])
    window_input = window_total[...].astype(F32) + inverse * (
        hidden_grad
        - jnp.mean(hidden_grad, axis=-1, keepdims=True)
        - normed[...] * jnp.mean(hidden_grad * normed[...], axis=-1, keepdims=True)
    )
    window_input = window_input.astype(B16)
    rounds[3].pick(window_input, pick_window[...])

    widen_fine = one_hot(384, 512, lambda n: (n // 96) * 128 + n % 96)
    widen_proj = one_hot(128, 512, lambda n: (n >> 5) * 128 + 96 + (n & 31))
    for path in qkv_sums:
        path.add_first()
        path.start_second()
    rounds[3].start(window_input)
    proj_total = proj_sum.add_second()
    proj_wide = [dot(proj_total[32 * h : 32 * (h + 1)], widen_proj) for h in range(2)]
    for h, path in enumerate(qkv_sums):
        total = path.add_second()
        wide_rows = jnp.concatenate([total[32 * m : 32 * (m + 1)] for m in range(3)], axis=1)
        block = (dot(wide_rows, widen_fine) + proj_wide[h]).astype(B16)
        for m in range(HALF):
            fine_last.column[HALF * h + m] = block[:, 128 * m : 128 * (m + 1)]
    fine_last.start()
    merge_last.add(sum_merge)
    input_grad[...] = rounds[3].get(to_output[...]).astype(B16)
    fine_last.add(sum_fine)


def finish_kernel(sum_merge, sum_fine, *refs):
    for src, dst in zip(refs[:3], refs[3:6]):
        dst[...] = src[...]
    dw_qkv, dw_proj, dw_merge = refs[6:]
    dw_qkv[...] = sum_fine[:, 0:96]
    dw_proj[...] = sum_fine[:, 96:128]
    dw_merge[...] = sum_merge[...]


def section(deep, *args):
    vmem, smem = pltpu.VMEM, pltpu.SMEM
    inside = pl.BlockSpec(memory_space=vmem)
    outside = pl.BlockSpec(memory_space=pl.ANY)
    shape = jax.ShapeDtypeStruct
    big = [shape((CELLS, D), B16), shape((MERGED, D2), B16), shape((CELLS, D), B16)]
    fringe = fringe_size(deep)
    return pl.pallas_call(
        functools.partial(section_kernel, deep),
        out_shape=big + [shape((64, 128), F32), shape((32, 128), F32)],
        in_specs=[pl.BlockSpec(memory_space=smem)] + [outside] * 6,
        out_specs=[inside] * 5,
        scratch_shapes=[
            vmem((CELLS, D), B16),
            vmem((CELLS, D), B16),
            vmem((D, 3 * D), B16),
            vmem((D, D), B16),
            vmem((4 * D, D2), B16),
            pltpu.SemaphoreType.DMA((6,)),
            vmem((CELLS, CELLS + fringe), B16),
            vmem((CELLS, CELLS + fringe), B16),
            vmem((CELLS, CELLS + fringe), B16),
            vmem((fringe, CELLS), B16),
            vmem((fringe, CELLS), B16),
            vmem((CELLS, D), F32),
            vmem((CELLS, 3 * D), B16),
            vmem((WINDOWS, 4, 64, 256), F32),
            vmem((WINDOWS, 4, 64, 256), B16),
            vmem((CELLS, D), B16),
            vmem((CELLS, D), B16),
            vmem((CELLS, 3 * D), B16),
            vmem((MERGED, 4 * D), B16),
            vmem((CELLS, D), B16),
            vmem((D2, 2 * XS * MERGED), B16),
            vmem((D // 2, 3 * D), F32),
            vmem((4, MERGED, D), F32),
        ]
        + around_scratch(deep) * 4
        + gather_scratch()
        + path_scratch(512, (False, 1), (YLO, YHI))
        + path_scratch(64, (True, XS), (YLO, YHI))
        + path_scratch(96, (True, XS), (YLO, YHI))
        + path_scratch(96, (True, YS), (XS,))
        + last_scratch(64)
        + last_scratch(32)
        + share_scratch(),
        compiler_params=pltpu.CompilerParams(
            collective_id=deep, has_side_effects=True, vmem_limit_bytes=56 * 2**20
        ),
    )(*args)


def on_device(tokens, w_qkv, w_proj, w_merge, skip_grad, merged_grad, window_shift):
    inside = pl.BlockSpec(memory_space=pltpu.VMEM)
    shape = jax.ShapeDtypeStruct
    big = [shape((CELLS, D), B16), shape((MERGED, D2), B16), shape((CELLS, D), B16)]
    args = (
        window_shift,
        tokens.reshape(CELLS, D),
        skip_grad.reshape(CELLS, D),
        merged_grad.reshape(MERGED, D2),
        w_qkv,
        w_proj,
        w_merge,
    )
    shift = window_shift[0]
    rows = jnp.minimum(shift, WIN - shift)
    skip_out, merged_out, input_grad, sum_merge, sum_fine = lax.switch(
        jnp.minimum(rows, 3) - 1, [functools.partial(section, deep) for deep in (1, 2, 4)], *args
    )
    skip_out, merged_out, input_grad, dw_qkv, dw_proj, dw_merge = pl.pallas_call(
        finish_kernel,
        out_shape=big + [shape((32, 96), F32), shape((32, 32), F32), shape((64, 128), F32)],
        in_specs=[inside] * 5,
        out_specs=[inside] * 6,
    )(sum_merge, sum_fine, skip_out, merged_out, input_grad)
    return (
        skip_out.reshape(ROWS, COLS, D),
        merged_out.reshape(ROWS // 2, COLS // 2, D2),
        input_grad.reshape(ROWS, COLS, D),
        dw_qkv,
        dw_proj,
        dw_merge.T,
    )


def solution(mesh):
    in_specs = (
        P("lat", "lon", None),
        P(),
        P(),
        P(),
        P("lat", "lon", None),
        P("lat", "lon", None),
        P(),
    )
    out_specs = (
        P("lat", "lon", None),
        P("lat", "lon", None),
        P("lat", "lon", None),
        P("lon", "lat"),
        P("lon", "lat"),
        P("lon", "lat"),
    )
    return jax.shard_map(
        on_device, mesh=mesh, in_specs=in_specs, out_specs=out_specs, check_vma=False
    )
```
